512 devices in a mesh: seq: 32 (over y, x, core), head: 16 (over z).
Axes of the slice: x: 4, y: 4, z: 16, core: 2. Of those that a mesh axis runs over, the one named last changes fastest.
Arguments:
- queries: bfloat16 [2, 32, 8, 32, 128], P(None, 'head'), may hold values from -128 to 128
- tree_keys: bfloat16 [2, 32, 32, 128], P(None, 'head'), may hold values from -8 to 8
- tree_values: bfloat16 [2, 32, 32, 128], P(None, 'head'), may hold values from -6 to 6
- cache_keys: bfloat16 [32, 32768, 128], P('head', 'seq'), may hold values from -6 to 6
- cache_values: bfloat16 [32, 32768, 128], P('head', 'seq'), may hold values from -6 to 6
- block_ids: int32 [32, 32], P('head'), may hold values from 0 to 255, as said below
- ancestors: int32 [4, 32, 32], replicated, may hold values from 0 to 1, as said below
- out_weight: bfloat16 [8192, 8192], P('seq', 'head'), may hold values from -0.0625 to 0.0625
Outputs:
- draft_mixed: bfloat16 [32, 4, 8192], P('seq', None, 'head')
- verify_mixed: bfloat16 [32, 4, 8192], P('seq', None, 'head')
The draws below stay inside these ranges and needn't reach their ends.
Inputs may be any that keep to these rules, and one draw needn't show every extreme that they name: `block_ids`: the 32 block numbers of one pair are distinct, and for every pair one run of 1024 positions (positions s * 1024 to (s + 1) * 1024 - 1 for some s) holds at least half of its 32 blocks, or all 8 blocks of the run where the run has fewer. ancestors[r, n, k] is 1 exactly when k is n or an ancestor of n in request r's tree; node 0 is the root and every other node's parent has a smaller number.
All inputs are finite; a program needn't handle non-finite values.
Results may differ from the reference program's by a relative error of at most 0.009.
Values may be sent and summed in bfloat16 or wider, within the bound.
No kernel may reach another device: no remote copies, remote signals or barrier semaphores. Data moves between devices by JAX's collectives and lax.ppermute only.
A program may use at most 64 MiB of HBM per device.

```python
import jax
import jax.numpy as jnp
from jax import lax

D = 8192
HQ = 64
KVH = 8
HD = 128
G = 8
NODES = 32
SEL = 32
BLOCK = 128
PAIRS = 32
REQUESTS = 4
CONTEXT = 32768
BLOCKS_DEV = 8
BLOCKS = 256
N_SEQ = 32


def tree_draw(base_key):
    own_keys = jnp.clip(jax.random.normal(jax.random.fold_in(base_key, 101), (2, PAIRS, NODES, HD), jnp.float32), -6.0, 6.0)
    jitter = jnp.clip(jax.random.normal(jax.random.fold_in(base_key, 102), (2, PAIRS, G, NODES, HD), jnp.float32), -6.0, 6.0)
    query_rows = 3.0 * jitter + 1.1 * own_keys[:, :, None]
    return (jnp.clip(query_rows, -128.0, 128.0), own_keys)


def draw_queries(key, part):
    return tree_draw(key)[0].astype(jnp.bfloat16)


def draw_tree_keys(key, part):
    return tree_draw(key)[1].astype(jnp.bfloat16)


def draw_block_ids(key, part):
    key_one = jax.random.fold_in(key, 201)
    key_two = jax.random.fold_in(key, 202)
    key_three = jax.random.fold_in(key, 203)
    hot_shard = jax.random.randint(key_one, (PAIRS, 1), 0, N_SEQ)
    ranked = jax.random.randint(key_two, (PAIRS, BLOCKS), 0, 1 << 19) * BLOCKS + jnp.arange(BLOCKS, dtype=jnp.int32)[None, :]
    local_rank = jax.vmap(lambda one_key: jax.random.permutation(one_key, BLOCKS_DEV))(jax.random.split(key_three, PAIRS)).astype(jnp.int32)
    block_numbers = jnp.arange(BLOCKS, dtype=jnp.int32)
    owner_shard = (block_numbers // BLOCKS_DEV)[None, :]
    rank_of_block = jnp.take(local_rank, block_numbers % BLOCKS_DEV, axis=1)
    preferred = jnp.logical_and(owner_shard == hot_shard, rank_of_block < min(SEL // 2, BLOCKS_DEV))
    ranked = jnp.where(preferred, ranked - (1 << 30), ranked)
    return jnp.argsort(ranked, axis=1, stable=True)[:, :SEL].astype(jnp.int32)


def draw_ancestors(key, part):

    def per_request(request_key):
        limits = jnp.maximum(jnp.arange(NODES, dtype=jnp.int32), 1)
        parents = jax.random.randint(request_key, (NODES,), 0, limits)
        identity_rows = jnp.eye(NODES, dtype=jnp.int32)

        def extend(position, lineage):
            return lineage.at[position].set(jnp.maximum(lineage[parents[position]], identity_rows[position]))
        return lax.fori_loop(1, NODES, extend, identity_rows)
    return jax.vmap(per_request)(jax.random.split(key, REQUESTS))


def level_of(own_key, shape, cuts, low, largest):
    def one(dim, blocks):
        steps = jax.random.uniform(jax.random.fold_in(jax.random.fold_in(own_key, 6), dim), (blocks,), jnp.float32, low / len(cuts), largest / len(cuts))
        return jnp.repeat(jnp.exp(steps), shape[dim] // blocks).reshape((-1,) + (1,) * (len(shape) - dim - 1))

    factor_of = one(*cuts[0])
    for cut in cuts[1:]:
        factor_of = factor_of * one(*cut)
    return factor_of


def normal_values(own_key, extent, width, reach, cuts=(), kind=jnp.bfloat16):
    values = jax.random.normal(own_key, extent, jnp.float32) * width
    if len(cuts) > 0:
        values = level_of(own_key, extent, cuts, -0.22, 0.18) * values
    return jnp.clip(values, min=-reach, max=reach).astype(kind)


def setup_inputs(seed: int = 0) -> dict:
    seeds = jax.random.split(jax.random.key(seed), 9)
    return {
        "queries": draw_queries(jax.random.fold_in(seeds[8], 71), 0),
        "tree_keys": draw_tree_keys(jax.random.fold_in(seeds[8], 71), 0),
        "tree_values": normal_values(seeds[2], (2, PAIRS, NODES, HD), 1.0, 6.0, ((1, 16),)),
        "cache_keys": normal_values(seeds[3], (PAIRS, CONTEXT, HD), 1.0, 6.0, ((0, 16), (1, 32))),
        "cache_values": normal_values(seeds[4], (PAIRS, CONTEXT, HD), 1.0, 6.0, ((0, 16), (1, 32))),
        "block_ids": draw_block_ids(jax.random.fold_in(seeds[8], 71), 0),
        "ancestors": draw_ancestors(jax.random.fold_in(seeds[8], 71), 0),
        "out_weight": normal_values(seeds[7], (HQ * HD, D), (HQ * HD) ** -0.5, 0.0625, ((0, 32), (1, 16))),
    }


def attend(query_rows, key_rows, value_rows, tree_key_rows, tree_value_rows, tree_mask):
    score_scale = HD ** -0.5
    cache_scores = jnp.einsum("gnh,lh->gnl", query_rows.astype(jnp.float32), key_rows.astype(jnp.float32)) * score_scale
    tree_scores = jnp.einsum("gnh,kh->gnk", query_rows.astype(jnp.float32), tree_key_rows.astype(jnp.float32)) * score_scale
    allowed = tree_mask[None] > 0
    tree_scores = jnp.where(allowed, tree_scores, -1e30)
    peak = jnp.maximum(jnp.max(cache_scores, axis=-1), jnp.max(tree_scores, axis=-1))[..., None]
    cache_weights = jnp.exp(cache_scores - peak)
    tree_weights = jnp.where(allowed, jnp.exp(tree_scores - peak), 0.0)
    totals = jnp.sum(cache_weights, axis=-1) + jnp.sum(tree_weights, axis=-1)
    summed = jnp.einsum("gnl,lh->gnh", cache_weights.astype(jnp.bfloat16).astype(jnp.float32), value_rows.astype(jnp.float32))
    summed = summed + jnp.einsum("gnk,kh->gnh", tree_weights.astype(jnp.bfloat16).astype(jnp.float32), tree_value_rows.astype(jnp.float32))
    result = summed / totals[..., None]
    return jnp.transpose(result, (1, 0, 2)).astype(jnp.bfloat16)


def reference(queries, tree_keys, tree_values, cache_keys, cache_values, block_ids, ancestors, out_weight):
    def per_pair(pair_index):
        key_rows = cache_keys[pair_index]
        value_rows = cache_values[pair_index]
        chosen_ids = block_ids[pair_index]
        tree_mask = ancestors[pair_index // KVH]
        picked_keys = key_rows.reshape(BLOCKS, BLOCK, HD)[chosen_ids].reshape(SEL * BLOCK, HD)
        picked_values = value_rows.reshape(BLOCKS, BLOCK, HD)[chosen_ids].reshape(SEL * BLOCK, HD)
        draft_rows = attend(queries[0, pair_index], picked_keys, picked_values, tree_keys[0, pair_index], tree_values[0, pair_index], tree_mask)
        verify_rows = attend(queries[1, pair_index], key_rows, value_rows, tree_keys[1, pair_index], tree_values[1, pair_index], tree_mask)
        return draft_rows, verify_rows

    drafts, verifies = lax.map(per_pair, jnp.arange(PAIRS, dtype=jnp.int32))

    def project_out(attended):
        flat_rows = attended.reshape(REQUESTS, KVH, NODES, G * HD)
        flat_rows = jnp.transpose(flat_rows, (2, 0, 1, 3)).reshape(NODES * REQUESTS, HQ * HD)
        mixed = jnp.dot(flat_rows, out_weight, preferred_element_type=jnp.float32)
        return mixed.astype(jnp.bfloat16).reshape(NODES, REQUESTS, D)

    return project_out(drafts), project_out(verifies)
```

```python
import jax
import jax.numpy as jnp
from jax import lax
from jax.experimental import pallas as pl
from jax.experimental.pallas import tpu as pltpu
from jax.sharding import PartitionSpec as P

KVH = 8
BLOCK = 128
SCALE = 128 ** (-0.5) * 1.4426950408889634
NEG = -(2.0**100)
F32 = jnp.float32
BF16 = jnp.bfloat16
Y_GROUPS = [[y * 8 + k for y in range(4)] for k in range(8)]
XC_GROUPS = [[y * 8 + k for k in range(8)] for y in range(4)]
NT = (((1,), (1,)), ((), ()))
VMEM = pl.BlockSpec(memory_space=pltpu.VMEM)
PARAMS = pltpu.CompilerParams(vmem_limit_bytes=32 * 1024 * 1024)


def four_lanes(lane, tiles):
    low = jnp.where(lane < 32, tiles[0], tiles[1])
    high = jnp.where(lane < 96, tiles[2], tiles[3])
    return jnp.where(lane < 64, low, high)


def attend_kernel(
    q_ref, k_ref, v_ref, ids_ref, tk_ref, tv_ref, anc_ref, send_ref, tree_ref, acc_ref, stat_ref
):
    seq = lax.axis_index("seq")
    head = lax.axis_index("head")
    lane = lax.broadcasted_iota(jnp.int32, (8, 128), 1)
    first_half = (lane % 32) < 16
    for p in range(2):
        keys = k_ref[p]
        values = jnp.concatenate([v_ref[p], jnp.ones((1024, 128), BF16)], axis=1)
        ids = ids_ref[p : p + 1, :]
        bias = []
        for b in range(8):
            hit = jnp.max(jnp.where(ids == seq * 8 + b, 1.0, 0.0), axis=1, keepdims=True)
            bias.append(jnp.broadcast_to(jnp.where(hit > 0.5, 0.0, NEG), (1, BLOCK)))
        bias = jnp.concatenate(bias, axis=1)
        peaks, sums = [], []
        for a in range(2):
            q = q_ref[a, p].reshape(256, 128)
            t = lax.dot_general(q, keys, NT, preferred_element_type=F32) * SCALE
            if a == 0:
                t = t + bias
            peak = jnp.max(t, axis=1, keepdims=True).astype(BF16).astype(F32)
            w = jnp.exp2(t - peak).astype(BF16)
            peaks.append(peak)
            sums.append(jnp.dot(w, values, preferred_element_type=F32))
        for y in range(4):
            for gp in range(4):
                dest = y * 8 + p * 4 + gp
                rows = [(gp * 2 + g2) * 32 + y * 8 for g2 in range(2)]
                for a in range(2):
                    both = jnp.concatenate([sums[a][r : r + 8, :128] for r in rows], axis=0)
                    send_ref[dest, a * 16 : (a + 1) * 16, :] = both.astype(BF16)
                m = four_lanes(lane, [peaks[a][r : r + 8] for a in range(2) for r in rows])
                tot = four_lanes(lane, [sums[a][r : r + 8, 128:] for a in range(2) for r in rows])
                high = tot.astype(BF16).astype(F32)
                tot = jnp.where(first_half, high, tot - high)
                send_ref[dest, 32:48, :] = jnp.concatenate([m, tot], axis=0).astype(BF16)
    y, x, core = seq // 8, (seq % 8) // 2, seq % 2
    own, gp = x // 2, (x % 2) * 2 + core
    allowed = anc_ref[head // 4] > 0
    allowed = jnp.concatenate([allowed, allowed], axis=0)
    for a in range(2):
        q = q_ref[a, own, pl.ds(gp * 2, 2)].reshape(64, 128)
        t = lax.dot_general(q, tk_ref[a, own], NT, preferred_element_type=F32) * SCALE
        t = jnp.where(allowed, t, NEG)
        peak = jnp.max(t, axis=1, keepdims=True)
        w = jnp.where(allowed, jnp.exp2(t - peak), 0.0)
        total = jnp.sum(w, axis=1, keepdims=True)
        summed = jnp.dot(w.astype(BF16), tv_ref[a, own], preferred_element_type=F32)
        acc_ref[a] = summed.reshape(2, 32, 128)
        stat_ref[0, a] = jnp.broadcast_to(peak, (64, 128)).reshape(2, 32, 128)
        stat_ref[1, a] = jnp.broadcast_to(total, (64, 128)).reshape(2, 32, 128)
    start = pl.multiple_of(y * 8, 8)
    for a in range(2):
        for g2 in range(2):
            tree_ref[a * 2 + g2] = acc_ref[a, g2, pl.ds(start, 8), :]
    for k in range(2):
        tile = four_lanes(
            lane, [stat_ref[k, a, g2, pl.ds(start, 8), :] for a in range(2) for g2 in range(2)]
        )
        tree_ref[4 + k] = tile if k == 0 else jnp.where(first_half, tile, 0.0)


def combine_kernel(got_ref, tree_ref, out_ref):
    def spread(tile, at):
        return jnp.broadcast_to(tile[:, at : at + 1], (8, 128))

    peak = tree_ref[4]
    for s in range(32):
        peak = jnp.maximum(peak, got_ref[s, 32:48, :].astype(F32)[:8])
    factor = jnp.exp2(tree_ref[4] - peak)
    total = factor * tree_ref[5]
    summed = [spread(factor, k * 32) * tree_ref[k] for k in range(4)]
    for s in range(32):
        stat = got_ref[s, 32:48, :].astype(F32)
        factor = jnp.exp2(stat[:8] - peak)
        total = total + factor * stat[8:]
        for a in range(2):
            part = got_ref[s, a * 16 : (a + 1) * 16, :].astype(F32)
            for g2 in range(2):
                k = a * 2 + g2
                summed[k] = summed[k] + spread(factor, k * 32) * part[g2 * 8 : (g2 + 1) * 8]
    done = [
        summed[k] / (spread(total, k * 32) + spread(total, k * 32 + 16)) for k in range(4)
    ]
    rows = jnp.concatenate([done[0], done[2], done[1], done[3]], axis=0).astype(BF16)
    for h in range(16):
        out_ref[h] = rows


def project_kernel(x_ref, w_ref, out_ref, turn_ref):
    total = jnp.zeros((64, 512), F32)
    for j in range(4):
        left = jnp.concatenate(
            [
                jnp.concatenate([x_ref[r * 4 + j, g2 * 16 : (g2 + 1) * 16, :] for r in range(4)], axis=0)
                for g2 in range(2)
            ],
            axis=1,
        )
        total = total + jnp.dot(left, w_ref[j], preferred_element_type=F32)
    for r in range(4):
        for a in range(2):
            at = (r * 2 + a) * 8
            turn_ref[:, a * 4 + r, :] = total[at : at + 8]
    out_ref[...] = turn_ref[...].astype(BF16)


def add_kernel(got_ref, draft_ref, verify_ref):
    total = got_ref[0].astype(F32)
    for s in range(1, 8):
        total = total + got_ref[s].astype(F32)
    draft_ref[0] = total[:4].astype(BF16)
    verify_ref[0] = total[4:].astype(BF16)


def swap(array, axis, groups=None):
    return lax.all_to_all(array, axis, 0, 0, tiled=True, axis_index_groups=groups)


def local(
    queries, tree_keys, tree_values, cache_keys, cache_values, block_ids, ancestors, out_weight
):
    weights = swap(jnp.broadcast_to(out_weight[None], (4, 256, 512)), "seq", Y_GROUPS)
    send, tree = pl.pallas_call(
        attend_kernel,
        out_shape=(
            jax.ShapeDtypeStruct((32, 48, 128), BF16),
            jax.ShapeDtypeStruct((6, 8, 128), F32),
        ),
        in_specs=[VMEM] * 7,
        out_specs=(VMEM, VMEM),
        scratch_shapes=[pltpu.VMEM((2, 2, 32, 128), F32), pltpu.VMEM((2, 2, 2, 32, 128), F32)],
        compiler_params=PARAMS,
    )(queries, cache_keys, cache_values, block_ids, tree_keys, tree_values, ancestors)
    got = swap(send, "seq")
    rows = pl.pallas_call(
        combine_kernel,
        out_shape=jax.ShapeDtypeStruct((16, 32, 128), BF16),
        in_specs=[VMEM] * 2,
        out_specs=VMEM,
        compiler_params=PARAMS,
    )(got, tree)
    gathered = swap(rows, "head")
    parts = pl.pallas_call(
        project_kernel,
        out_shape=jax.ShapeDtypeStruct((8, 8, 512), BF16),
        in_specs=[VMEM] * 2,
        out_specs=VMEM,
        scratch_shapes=[pltpu.VMEM((8, 8, 512), F32)],
        compiler_params=PARAMS,
    )(gathered, weights)
    parts = swap(parts, "seq", XC_GROUPS)
    return pl.pallas_call(
        add_kernel,
        out_shape=(jax.ShapeDtypeStruct((1, 4, 512), BF16), jax.ShapeDtypeStruct((1, 4, 512), BF16)),
        in_specs=[VMEM],
        out_specs=(VMEM, VMEM),
        compiler_params=PARAMS,
    )(parts)


def solution(mesh):
    in_specs = (
        P(None, "head", None, None, None),
        P(None, "head", None, None),
        P(None, "head", None, None),
        P("head", "seq", None),
        P("head", "seq", None),
        P("head", None),
        P(),
        P("seq", "head"),
    )
    out_specs = (P("seq", None, "head"), P("seq", None, "head"))
    return jax.shard_map(local, mesh=mesh, in_specs=in_specs, out_specs=out_specs, check_vma=False)
```

```python
import jax
import jax.numpy as jnp
from jax import lax
from jax.experimental import pallas as pl
from jax.experimental.pallas import tpu as pltpu
from jax.sharding import PartitionSpec as P

KVH = 8
BLOCK = 128
SCALE = 128 ** (-0.5) * 1.4426950408889634
NEG = -(2.0**100)
F32 = jnp.float32
BF16 = jnp.bfloat16
Y_GROUPS = [[y * 8 + k for y in range(4)] for k in range(8)]
Z_GROUPS = [[r * 4 + j for j in range(4) for r in range(4)]]
NT = (((1,), (1,)), ((), ()))
VMEM = pl.BlockSpec(memory_space=pltpu.VMEM)
HBM = pl.BlockSpec(memory_space=pltpu.HBM)
PARAMS = pltpu.CompilerParams(vmem_limit_bytes=32 * 1024 * 1024)


def four_lanes(lane, tiles):
    low = jnp.where(lane < 32, tiles[0], tiles[1])
    high = jnp.where(lane < 96, tiles[2], tiles[3])
    return jnp.where(lane < 64, low, high)


def attend_kernel(
    q_hbm, k_hbm, v_hbm, ids_hbm, tk_hbm, tv_hbm, anc_hbm,
    send_ref, tree_ref,
    q_ref, k_ref, v_ref, ids_ref, tk_ref, tv_ref, anc_ref, acc_ref, stat_ref, sems,
):
    moves = [
        (ids_hbm, ids_ref),
        (k_hbm.at[0], k_ref.at[0]),
        (q_hbm, q_ref),
        (v_hbm.at[0], v_ref.at[0]),
        (k_hbm.at[1], k_ref.at[1]),
        (v_hbm.at[1], v_ref.at[1]),
        (tk_hbm, tk_ref),
        (tv_hbm, tv_ref),
        (anc_hbm, anc_ref),
    ]
    moves = [pltpu.make_async_copy(a, b, sems.at[i]) for i, (a, b) in enumerate(moves)]
    for move in moves:
        move.start()
    seq = lax.axis_index("seq")
    head = lax.axis_index("head")
    lane = lax.broadcasted_iota(jnp.int32, (8, 128), 1)
    first_half = (lane % 32) < 16
    for p in range(2):
        for at in ((0, 1, 2, 3), (4, 5))[p]:
            moves[at].wait()
        keys = k_ref[p]
        values = jnp.concatenate([v_ref[p], jnp.ones((1024, 128), BF16)], axis=1)
        ids = ids_ref[p : p + 1, :]
        bias = []
        for b in range(8):
            hit = jnp.max(jnp.where(ids == seq * 8 + b, 1.0, 0.0), axis=1, keepdims=True)
            bias.append(jnp.broadcast_to(jnp.where(hit > 0.5, 0.0, NEG), (1, BLOCK)))
        bias = jnp.concatenate(bias, axis=1)
        peaks, sums = [], []
        for a in range(2):
            q = q_ref[a, p].reshape(256, 128)
            t = lax.dot_general(q, keys, NT, preferred_element_type=F32) * SCALE
            if a == 0:
                t = t + bias
            peak = jnp.max(t, axis=1, keepdims=True).astype(BF16).astype(F32)
            w = jnp.exp2(t - peak).astype(BF16)
            peaks.append(peak)
            sums.append(jnp.dot(w, values, preferred_element_type=F32))
        for y in range(4):
            for gp in range(4):
                dest = y * 8 + p * 4 + gp
                rows = [(gp * 2 + g2) * 32 + y * 8 for g2 in range(2)]
                for a in range(2):
                    both = jnp.concatenate([sums[a][r : r + 8, :128] for r in rows], axis=0)
                    send_ref[dest, a * 16 : (a + 1) * 16, :] = both.astype(BF16)
                m = four_lanes(lane, [peaks[a][r : r + 8] for a in range(2) for r in rows])
                tot = four_lanes(lane, [sums[a][r : r + 8, 128:] for a in range(2) for r in rows])
                high = tot.astype(BF16).astype(F32)
                tot = jnp.where(first_half, high, tot - high)
                send_ref[dest, 32:48, :] = jnp.concatenate([m, tot], axis=0).astype(BF16)
    for move in moves[6:]:
        move.wait()
    y, x, core = seq // 8, (seq % 8) // 2, seq % 2
    own, gp = x // 2, (x % 2) * 2 + core
    allowed = anc_ref[head // 4] > 0
    allowed = jnp.concatenate([allowed, allowed], axis=0)
    for a in range(2):
        q = q_ref[a, own, pl.ds(gp * 2, 2)].reshape(64, 128)
        t = lax.dot_general(q, tk_ref[a, own], NT, preferred_element_type=F32) * SCALE
        t = jnp.where(allowed, t, NEG)
        peak = jnp.max(t, axis=1, keepdims=True)
        w = jnp.where(allowed, jnp.exp2(t - peak), 0.0)
        total = jnp.sum(w, axis=1, keepdims=True)
        summed = jnp.dot(w.astype(BF16), tv_ref[a, own], preferred_element_type=F32)
        acc_ref[a] = summed.reshape(2, 32, 128)
        stat_ref[0, a] = jnp.broadcast_to(peak, (64, 128)).reshape(2, 32, 128)
        stat_ref[1, a] = jnp.broadcast_to(total, (64, 128)).reshape(2, 32, 128)
    start = pl.multiple_of(y * 8, 8)
    for a in range(2):
        for g2 in range(2):
            tree_ref[a * 2 + g2] = acc_ref[a, g2, pl.ds(start, 8), :]
    for k in range(2):
        tile = four_lanes(
            lane, [stat_ref[k, a, g2, pl.ds(start, 8), :] for a in range(2) for g2 in range(2)]
        )
        tree_ref[4 + k] = tile if k == 0 else jnp.where(first_half, tile, 0.0)


def combine_kernel(got_ref, tree_ref, out_ref):
    def spread(tile, at):
        return jnp.broadcast_to(tile[:, at : at + 1], (8, 128))

    peak = tree_ref[4]
    for s in range(32):
        peak = jnp.maximum(peak, got_ref[s, 32:48, :].astype(F32)[:8])
    factor = jnp.exp2(tree_ref[4] - peak)
    total = factor * tree_ref[5]
    summed = [spread(factor, k * 32) * tree_ref[k] for k in range(4)]
    for s in range(32):
        stat = got_ref[s, 32:48, :].astype(F32)
        factor = jnp.exp2(stat[:8] - peak)
        total = total + factor * stat[8:]
        for a in range(2):
            part = got_ref[s, a * 16 : (a + 1) * 16, :].astype(F32)
            for g2 in range(2):
                k = a * 2 + g2
                summed[k] = summed[k] + spread(factor, k * 32) * part[g2 * 8 : (g2 + 1) * 8]
    done = [
        summed[k] / (spread(total, k * 32) + spread(total, k * 32 + 16)) for k in range(4)
    ]
    rows = jnp.concatenate([done[0], done[2], done[1], done[3]], axis=0).astype(BF16)
    for h in range(16):
        out_ref[h] = rows


def project_kernel(x_ref, w_ref, out_ref, turn_ref):
    left = jnp.concatenate(
        [
            jnp.concatenate(
                [x_ref[q, r * 32 + g2 * 16 : r * 32 + g2 * 16 + 16, :] for q in range(4) for r in range(4)],
                axis=0,
            )
            for g2 in range(2)
        ],
        axis=1,
    )
    total = jnp.dot(left, w_ref[...], preferred_element_type=F32)
    for q in range(4):
        for r in range(4):
            for a in range(2):
                at = ((q * 4 + r) * 2 + a) * 8
                turn_ref[q * 8 : (q + 1) * 8, a * 4 + r, :] = total[at : at + 8]
    out_ref[...] = turn_ref[...].astype(BF16)


def add_kernel(got_ref, draft_ref, verify_ref):
    total = got_ref[0].astype(F32)
    for s in range(1, 32):
        total = total + got_ref[s].astype(F32)
    draft_ref[0] = total[:4].astype(BF16)
    verify_ref[0] = total[4:].astype(BF16)


def swap(array, axis, groups=None):
    return lax.all_to_all(array, axis, 0, 0, tiled=True, axis_index_groups=groups)


def local(
    queries, tree_keys, tree_values, cache_keys, cache_values, block_ids, ancestors, out_weight
):
    send, tree = pl.pallas_call(
        attend_kernel,
        out_shape=(
            jax.ShapeDtypeStruct((32, 48, 128), BF16),
            jax.ShapeDtypeStruct((6, 8, 128), F32),
        ),
        in_specs=[HBM] * 7,
        out_specs=(VMEM, VMEM),
        scratch_shapes=[
            pltpu.VMEM((2, 2, 8, 32, 128), BF16),
            pltpu.VMEM((2, 1024, 128), BF16),
            pltpu.VMEM((2, 1024, 128), BF16),
            pltpu.VMEM((2, 32), jnp.int32),
            pltpu.VMEM((2, 2, 32, 128), BF16),
            pltpu.VMEM((2, 2, 32, 128), BF16),
            pltpu.VMEM((4, 32, 32), jnp.int32),
            pltpu.VMEM((2, 2, 32, 128), F32),
            pltpu.VMEM((2, 2, 2, 32, 128), F32),
            pltpu.SemaphoreType.DMA((9,)),
        ],
        compiler_params=pltpu.CompilerParams(vmem_limit_bytes=55296 * 1024),
    )(queries, cache_keys, cache_values, block_ids, tree_keys, tree_values, ancestors)
    got = swap(send, "seq")
    rows = pl.pallas_call(
        combine_kernel,
        out_shape=jax.ShapeDtypeStruct((16, 32, 128), BF16),
        in_specs=[VMEM] * 2,
        out_specs=VMEM,
        compiler_params=PARAMS,
    )(got, tree)
    gathered = swap(rows, "head", Z_GROUPS)
    own = swap(gathered.reshape(4, 128, 128), "seq", Y_GROUPS)
    parts = pl.pallas_call(
        project_kernel,
        out_shape=jax.ShapeDtypeStruct((32, 8, 512), BF16),
        in_specs=[VMEM] * 2,
        out_specs=VMEM,
        scratch_shapes=[pltpu.VMEM((32, 8, 512), F32)],
        compiler_params=PARAMS,
    )(own, out_weight)
    parts = swap(parts, "seq")
    return pl.pallas_call(
        add_kernel,
        out_shape=(jax.ShapeDtypeStruct((1, 4, 512), BF16), jax.ShapeDtypeStruct((1, 4, 512), BF16)),
        in_specs=[VMEM],
        out_specs=(VMEM, VMEM),
        compiler_params=PARAMS,
    )(parts)


def solution(mesh):
    in_specs = (
        P(None, "head", None, None, None),
        P(None, "head", None, None),
        P(None, "head", None, None),
        P("head", "seq", None),
        P("head", "seq", None),
        P("head", None),
        P(),
        P("seq", "head"),
    )
    out_specs = (P("seq", None, "head"), P("seq", None, "head"))
    return jax.shard_map(local, mesh=mesh, in_specs=in_specs, out_specs=out_specs, check_vma=False)
```

```python
import jax
import jax.numpy as jnp
from jax import lax
from jax.experimental import pallas as pl
from jax.experimental.pallas import tpu as pltpu
from jax.sharding import PartitionSpec as P

KVH = 8
BLOCK = 128
SCALE = 128 ** (-0.5) * 1.4426950408889634
NEG = -(2.0**100)
F32 = jnp.float32
BF16 = jnp.bfloat16
Y_GROUPS = [[y * 8 + k for y in range(4)] for k in range(8)]
XC_GROUPS = [[y * 8 + k for k in range(8)] for y in range(4)]
NT = (((1,), (1,)), ((), ()))
VMEM = pl.BlockSpec(memory_space=pltpu.VMEM)
HBM = pl.BlockSpec(memory_space=pltpu.HBM)
PARAMS = pltpu.CompilerParams(vmem_limit_bytes=32 * 1024 * 1024)


def four_lanes(lane, tiles):
    low = jnp.where(lane < 32, tiles[0], tiles[1])
    high = jnp.where(lane < 96, tiles[2], tiles[3])
    return jnp.where(lane < 64, low, high)


def attend_kernel(
    q_hbm, k_hbm, v_hbm, ids_hbm, tk_hbm, tv_hbm, anc_hbm,
    send_ref, tree_ref,
    q_ref, k_ref, v_ref, ids_ref, tk_ref, tv_ref, anc_ref, acc_ref, stat_ref, sems,
):
    moves = [
        (ids_hbm, ids_ref),
        (k_hbm.at[0], k_ref.at[0]),
        (q_hbm, q_ref),
        (v_hbm.at[0], v_ref.at[0]),
        (k_hbm.at[1], k_ref.at[1]),
        (v_hbm.at[1], v_ref.at[1]),
        (tk_hbm, tk_ref),
        (tv_hbm, tv_ref),
        (anc_hbm, anc_ref),
    ]
    moves = [pltpu.make_async_copy(a, b, sems.at[i]) for i, (a, b) in enumerate(moves)]
    for move in moves:
        move.start()
    seq = lax.axis_index("seq")
    head = lax.axis_index("head")
    lane = lax.broadcasted_iota(jnp.int32, (8, 128), 1)
    first_half = (lane % 32) < 16
    for p in range(2):
        for at in ((0, 1, 2, 3), (4, 5))[p]:
            moves[at].wait()
        keys = k_ref[p]
        values = jnp.concatenate([v_ref[p], jnp.ones((1024, 128), BF16)], axis=1)
        ids = ids_ref[p : p + 1, :]
        bias = []
        for b in range(8):
            hit = jnp.max(jnp.where(ids == seq * 8 + b, 1.0, 0.0), axis=1, keepdims=True)
            bias.append(jnp.broadcast_to(jnp.where(hit > 0.5, 0.0, NEG), (1, BLOCK)))
        bias = jnp.concatenate(bias, axis=1)
        peaks, sums = [], []
        for a in range(2):
            q = q_ref[a, p].reshape(256, 128)
            t = lax.dot_general(q, keys, NT, preferred_element_type=F32) * SCALE
            if a == 0:
                t = t + bias
            peak = jnp.max(t, axis=1, keepdims=True).astype(BF16).astype(F32)
            w = jnp.exp2(t - peak).astype(BF16)
            peaks.append(peak)
            sums.append(jnp.dot(w, values, preferred_element_type=F32))
        for y in range(4):
            for gp in range(4):
                dest = y * 8 + p * 4 + gp
                rows = [(gp * 2 + g2) * 32 + y * 8 for g2 in range(2)]
                for a in range(2):
                    both = jnp.concatenate([sums[a][r : r + 8, :128] for r in rows], axis=0)
                    send_ref[dest, a * 16 : (a + 1) * 16, :] = both.astype(BF16)
                m = four_lanes(lane, [peaks[a][r : r + 8] for a in range(2) for r in rows])
                tot = four_lanes(lane, [sums[a][r : r + 8, 128:] for a in range(2) for r in rows])
                high = tot.astype(BF16).astype(F32)
                tot = jnp.where(first_half, high, tot - high)
                send_ref[dest, 32:48, :] = jnp.concatenate([m, tot], axis=0).astype(BF16)
    for move in moves[6:]:
        move.wait()
    y, x, core = seq // 8, (seq % 8) // 2, seq % 2
    own, gp = x // 2, (x % 2) * 2 + core
    allowed = anc_ref[head // 4] > 0
    allowed = jnp.concatenate([allowed, allowed], axis=0)
    for a in range(2):
        q = q_ref[a, own, pl.ds(gp * 2, 2)].reshape(64, 128)
        t = lax.dot_general(q, tk_ref[a, own], NT, preferred_element_type=F32) * SCALE
        t = jnp.where(allowed, t, NEG)
        peak = jnp.max(t, axis=1, keepdims=True)
        w = jnp.where(allowed, jnp.exp2(t - peak), 0.0)
        total = jnp.sum(w, axis=1, keepdims=True)
        summed = jnp.dot(w.astype(BF16), tv_ref[a, own], preferred_element_type=F32)
        acc_ref[a] = summed.reshape(2, 32, 128)
        stat_ref[0, a] = jnp.broadcast_to(peak, (64, 128)).reshape(2, 32, 128)
        stat_ref[1, a] = jnp.broadcast_to(total, (64, 128)).reshape(2, 32, 128)
    start = pl.multiple_of(y * 8, 8)
    for a in range(2):
        for g2 in range(2):
            tree_ref[a * 2 + g2] = acc_ref[a, g2, pl.ds(start, 8), :]
    for k in range(2):
        tile = four_lanes(
            lane, [stat_ref[k, a, g2, pl.ds(start, 8), :] for a in range(2) for g2 in range(2)]
        )
        tree_ref[4 + k] = tile if k == 0 else jnp.where(first_half, tile, 0.0)


def combine_kernel(got_ref, tree_ref, out_ref):
    def spread(tile, at):
        return jnp.broadcast_to(tile[:, at : at + 1], (8, 128))

    peak = tree_ref[4]
    for s in range(32):
        peak = jnp.maximum(peak, got_ref[s, 32:48, :].astype(F32)[:8])
    factor = jnp.exp2(tree_ref[4] - peak)
    total = factor * tree_ref[5]
    summed = [spread(factor, k * 32) * tree_ref[k] for k in range(4)]
    for s in range(32):
        stat = got_ref[s, 32:48, :].astype(F32)
        factor = jnp.exp2(stat[:8] - peak)
        total = total + factor * stat[8:]
        for a in range(2):
            part = got_ref[s, a * 16 : (a + 1) * 16, :].astype(F32)
            for g2 in range(2):
                k = a * 2 + g2
                summed[k] = summed[k] + spread(factor, k * 32) * part[g2 * 8 : (g2 + 1) * 8]
    done = [
        summed[k] / (spread(total, k * 32) + spread(total, k * 32 + 16)) for k in range(4)
    ]
    rows = jnp.concatenate([done[0], done[2], done[1], done[3]], axis=0).astype(BF16)
    for h in range(16):
        out_ref[h] = rows


def project_kernel(x_ref, w_ref, out_ref, turn_ref):
    total = jnp.zeros((64, 512), F32)
    for j in range(4):
        left = jnp.concatenate(
            [
                jnp.concatenate([x_ref[r * 4 + j, g2 * 16 : (g2 + 1) * 16, :] for r in range(4)], axis=0)
                for g2 in range(2)
            ],
            axis=1,
        )
        total = total + jnp.dot(left, w_ref[j], preferred_element_type=F32)
    for r in range(4):
        for a in range(2):
            at = (r * 2 + a) * 8
            turn_ref[:, a * 4 + r, :] = total[at : at + 8]
    out_ref[...] = turn_ref[...].astype(BF16)


def add_kernel(got_ref, draft_ref, verify_ref):
    total = got_ref[0].astype(F32)
    for s in range(1, 8):
        total = total + got_ref[s].astype(F32)
    draft_ref[0] = total[:4].astype(BF16)
    verify_ref[0] = total[4:].astype(BF16)


def swap(array, axis, groups=None):
    return lax.all_to_all(array, axis, 0, 0, tiled=True, axis_index_groups=groups)


def local(
    queries, tree_keys, tree_values, cache_keys, cache_values, block_ids, ancestors, out_weight
):
    send, tree = pl.pallas_call(
        attend_kernel,
        out_shape=(
            jax.ShapeDtypeStruct((32, 48, 128), BF16),
            jax.ShapeDtypeStruct((6, 8, 128), F32),
        ),
        in_specs=[HBM] * 7,
        out_specs=(VMEM, VMEM),
        scratch_shapes=[
            pltpu.VMEM((2, 2, 8, 32, 128), BF16),
            pltpu.VMEM((2, 1024, 128), BF16),
            pltpu.VMEM((2, 1024, 128), BF16),
            pltpu.VMEM((2, 32), jnp.int32),
            pltpu.VMEM((2, 2, 32, 128), BF16),
            pltpu.VMEM((2, 2, 32, 128), BF16),
            pltpu.VMEM((4, 32, 32), jnp.int32),
            pltpu.VMEM((2, 2, 32, 128), F32),
            pltpu.VMEM((2, 2, 2, 32, 128), F32),
            pltpu.SemaphoreType.DMA((9,)),
        ],
        compiler_params=pltpu.CompilerParams(vmem_limit_bytes=55296 * 1024),
    )(queries, cache_keys, cache_values, block_ids, tree_keys, tree_values, ancestors)
    got = swap(send, "seq")
    rows = pl.pallas_call(
        combine_kernel,
        out_shape=jax.ShapeDtypeStruct((16, 32, 128), BF16),
        in_specs=[VMEM] * 2,
        out_specs=VMEM,
        compiler_params=PARAMS,
    )(got, tree)
    gathered = swap(rows, "head")
    weights = lax.all_gather(out_weight, "seq", axis_index_groups=Y_GROUPS)
    parts = pl.pallas_call(
        project_kernel,
        out_shape=jax.ShapeDtypeStruct((8, 8, 512), BF16),
        in_specs=[VMEM] * 2,
        out_specs=VMEM,
        scratch_shapes=[pltpu.VMEM((8, 8, 512), F32)],
        compiler_params=PARAMS,
    )(gathered, weights)
    parts = swap(parts, "seq", XC_GROUPS)
    return pl.pallas_call(
        add_kernel,
        out_shape=(jax.ShapeDtypeStruct((1, 4, 512), BF16), jax.ShapeDtypeStruct((1, 4, 512), BF16)),
        in_specs=[VMEM],
        out_specs=(VMEM, VMEM),
        compiler_params=PARAMS,
    )(parts)


def solution(mesh):
    in_specs = (
        P(None, "head", None, None, None),
        P(None, "head", None, None),
        P(None, "head", None, None),
        P("head", "seq", None),
        P("head", "seq", None),
        P("head", None),
        P(),
        P("seq", "head"),
    )
    out_specs = (P("seq", None, "head"), P("seq", None, "head"))
    return jax.shard_map(local, mesh=mesh, in_specs=in_specs, out_specs=out_specs, check_vma=False)
```

```python
import jax
import jax.numpy as jnp
from jax import lax
from jax.experimental import pallas as pl
from jax.experimental.pallas import tpu as pltpu
from jax.sharding import PartitionSpec as P

KVH = 8
BLOCK = 128
SCALE = 128 ** (-0.5) * 1.4426950408889634
NEG = -(2.0**100)
F32 = jnp.float32
BF16 = jnp.bfloat16
XC_GROUPS = [[y * 8 + k for k in range(8)] for y in range(4)]
NT = (((1,), (1,)), ((), ()))
VMEM = pl.BlockSpec(memory_space=pltpu.VMEM)
ANY = pl.BlockSpec(memory_space=pl.ANY)
HBM = pl.BlockSpec(memory_space=pltpu.HBM)
PARAMS = pltpu.CompilerParams(vmem_limit_bytes=32 * 1024 * 1024)


def four_lanes(lane, tiles):
    low = jnp.where(lane < 32, tiles[0], tiles[1])
    high = jnp.where(lane < 96, tiles[2], tiles[3])
    return jnp.where(lane < 64, low, high)


def attend_kernel(
    q_hbm, k_hbm, v_hbm, ids_hbm, tk_hbm, tv_hbm, anc_hbm,
    send_ref, tree_ref,
    q_ref, k_ref, v_ref, ids_ref, tk_ref, tv_ref, anc_ref, acc_ref, stat_ref, sems,
):
    moves = [
        (ids_hbm, ids_ref),
        (k_hbm.at[0], k_ref.at[0]),
        (q_hbm, q_ref),
        (v_hbm.at[0], v_ref.at[0]),
        (k_hbm.at[1], k_ref.at[1]),
        (v_hbm.at[1], v_ref.at[1]),
        (tk_hbm, tk_ref),
        (tv_hbm, tv_ref),
        (anc_hbm, anc_ref),
    ]
    moves = [pltpu.make_async_copy(a, b, sems.at[i]) for i, (a, b) in enumerate(moves)]
    for move in moves:
        move.start()
    seq = lax.axis_index("seq")
    head = lax.axis_index("head")
    lane = lax.broadcasted_iota(jnp.int32, (8, 128), 1)
    first_half = (lane % 32) < 16
    for p in range(2):
        for at in ((0, 1, 2, 3), (4, 5))[p]:
            moves[at].wait()
        keys = k_ref[p]
        values = jnp.concatenate([v_ref[p], jnp.ones((1024, 128), BF16)], axis=1)
        ids = ids_ref[p : p + 1, :]
        bias = []
        for b in range(8):
            hit = jnp.max(jnp.where(ids == seq * 8 + b, 1.0, 0.0), axis=1, keepdims=True)
            bias.append(jnp.broadcast_to(jnp.where(hit > 0.5, 0.0, NEG), (1, BLOCK)))
        bias = jnp.concatenate(bias, axis=1)
        peaks, sums = [], []
        for a in range(2):
            q = q_ref[a, p].reshape(256, 128)
            t = lax.dot_general(q, keys, NT, preferred_element_type=F32) * SCALE
            if a == 0:
                t = t + bias
            peak = jnp.max(t, axis=1, keepdims=True).astype(BF16).astype(F32)
            w = jnp.exp2(t - peak).astype(BF16)
            peaks.append(peak)
            sums.append(jnp.dot(w, values, preferred_element_type=F32))
        for y in range(4):
            for gp in range(4):
                dest = y * 8 + p * 4 + gp
                rows = [(gp * 2 + g2) * 32 + y * 8 for g2 in range(2)]
                for a in range(2):
                    both = jnp.concatenate([sums[a][r : r + 8, :128] for r in rows], axis=0)
                    send_ref[dest, a * 16 : (a + 1) * 16, :] = both.astype(BF16)
                m = four_lanes(lane, [peaks[a][r : r + 8] for a in range(2) for r in rows])
                tot = four_lanes(lane, [sums[a][r : r + 8, 128:] for a in range(2) for r in rows])
                high = tot.astype(BF16).astype(F32)
                tot = jnp.where(first_half, high, tot - high)
                send_ref[dest, 32:48, :] = jnp.concatenate([m, tot], axis=0).astype(BF16)
    for move in moves[6:]:
        move.wait()
    y, x, core = seq // 8, (seq % 8) // 2, seq % 2
    own, gp = x // 2, (x % 2) * 2 + core
    allowed = anc_ref[head // 4] > 0
    allowed = jnp.concatenate([allowed, allowed], axis=0)
    for a in range(2):
        q = q_ref[a, own, pl.ds(gp * 2, 2)].reshape(64, 128)
        t = lax.dot_general(q, tk_ref[a, own], NT, preferred_element_type=F32) * SCALE
        t = jnp.where(allowed, t, NEG)
        peak = jnp.max(t, axis=1, keepdims=True)
        w = jnp.where(allowed, jnp.exp2(t - peak), 0.0)
        total = jnp.sum(w, axis=1, keepdims=True)
        summed = jnp.dot(w.astype(BF16), tv_ref[a, own], preferred_element_type=F32)
        acc_ref[a] = summed.reshape(2, 32, 128)
        stat_ref[0, a] = jnp.broadcast_to(peak, (64, 128)).reshape(2, 32, 128)
        stat_ref[1, a] = jnp.broadcast_to(total, (64, 128)).reshape(2, 32, 128)
    start = pl.multiple_of(y * 8, 8)
    for a in range(2):
        for g2 in range(2):
            tree_ref[a * 2 + g2] = acc_ref[a, g2, pl.ds(start, 8), :]
    for k in range(2):
        tile = four_lanes(
            lane, [stat_ref[k, a, g2, pl.ds(start, 8), :] for a in range(2) for g2 in range(2)]
        )
        tree_ref[4 + k] = tile if k == 0 else jnp.where(first_half, tile, 0.0)


def combine_kernel(got_ref, tree_ref, before_ref, after_ref, out_ref):
    def spread(tile, at):
        return jnp.broadcast_to(tile[:, at : at + 1], (8, 128))

    peak = tree_ref[4]
    for s in range(32):
        peak = jnp.maximum(peak, got_ref[s, 32:48, :].astype(F32)[:8])
    factor = jnp.exp2(tree_ref[4] - peak)
    total = factor * tree_ref[5]
    summed = [spread(factor, k * 32) * tree_ref[k] for k in range(4)]
    for s in range(32):
        stat = got_ref[s, 32:48, :].astype(F32)
        factor = jnp.exp2(stat[:8] - peak)
        total = total + factor * stat[8:]
        for a in range(2):
            part = got_ref[s, a * 16 : (a + 1) * 16, :].astype(F32)
            for g2 in range(2):
                k = a * 2 + g2
                summed[k] = summed[k] + spread(factor, k * 32) * part[g2 * 8 : (g2 + 1) * 8]
    done = [
        summed[k] / (spread(total, k * 32) + spread(total, k * 32 + 16)) for k in range(4)
    ]
    rows = jnp.concatenate([done[0], done[2], done[1], done[3]], axis=0).astype(BF16)
    for h in range(16):
        out_ref[h] = rows


def project_kernel(x_ref, *refs):
    w_refs, out_ref, turn_ref = refs[:4], refs[4], refs[5]
    y = lax.axis_index("seq") // 8
    total = jnp.zeros((64, 512), F32)
    for k in range(4):
        j = (y + 4 - k) % 4
        left = jnp.concatenate(
            [
                jnp.concatenate(
                    [x_ref[r * 4 + j, g2 * 16 : (g2 + 1) * 16, :] for r in range(4)], axis=0
                )
                for g2 in range(2)
            ],
            axis=1,
        )
        total = total + jnp.dot(left, w_refs[k][...], preferred_element_type=F32)
    for r in range(4):
        for a in range(2):
            at = (r * 2 + a) * 8
            turn_ref[:, a * 4 + r, :] = total[at : at + 8]
    out_ref[...] = turn_ref[...].astype(BF16)


def add_kernel(got_ref, draft_ref, verify_ref):
    total = got_ref[0].astype(F32)
    for s in range(1, 8):
        total = total + got_ref[s].astype(F32)
    draft_ref[0] = total[:4].astype(BF16)
    verify_ref[0] = total[4:].astype(BF16)


def swap(array, axis, groups=None):
    return lax.all_to_all(array, axis, 0, 0, tiled=True, axis_index_groups=groups)


def shift(array, k):
    return lax.ppermute(array, "seq", [(s, (s + 8 * k) % 32) for s in range(32)])


def local(
    queries, tree_keys, tree_values, cache_keys, cache_values, block_ids, ancestors, out_weight
):
    send, tree = pl.pallas_call(
        attend_kernel,
        out_shape=(
            jax.ShapeDtypeStruct((32, 48, 128), BF16),
            jax.ShapeDtypeStruct((6, 8, 128), F32),
        ),
        in_specs=[HBM] * 7,
        out_specs=(VMEM, VMEM),
        scratch_shapes=[
            pltpu.VMEM((2, 2, 8, 32, 128), BF16),
            pltpu.VMEM((2, 1024, 128), BF16),
            pltpu.VMEM((2, 1024, 128), BF16),
            pltpu.VMEM((2, 32), jnp.int32),
            pltpu.VMEM((2, 2, 32, 128), BF16),
            pltpu.VMEM((2, 2, 32, 128), BF16),
            pltpu.VMEM((4, 32, 32), jnp.int32),
            pltpu.VMEM((2, 2, 32, 128), F32),
            pltpu.VMEM((2, 2, 2, 32, 128), F32),
            pltpu.SemaphoreType.DMA((9,)),
        ],
        compiler_params=pltpu.CompilerParams(vmem_limit_bytes=55296 * 1024),
    )(queries, cache_keys, cache_values, block_ids, tree_keys, tree_values, ancestors)
    got = swap(send, "seq")
    one, three = shift(out_weight, 1), shift(out_weight, 3)
    rows = pl.pallas_call(
        combine_kernel,
        out_shape=jax.ShapeDtypeStruct((16, 32, 128), BF16),
        in_specs=[VMEM, VMEM, ANY, ANY],
        out_specs=VMEM,
        compiler_params=PARAMS,
    )(got, tree, one, three)
    gathered = swap(rows, "head")
    two = shift(out_weight, 2)
    parts = pl.pallas_call(
        project_kernel,
        out_shape=jax.ShapeDtypeStruct((8, 8, 512), BF16),
        in_specs=[VMEM] * 5,
        out_specs=VMEM,
        scratch_shapes=[pltpu.VMEM((8, 8, 512), F32)],
        compiler_params=PARAMS,
    )(gathered, out_weight, one, two, three)
    parts = swap(parts, "seq", XC_GROUPS)
    return pl.pallas_call(
        add_kernel,
        out_shape=(jax.ShapeDtypeStruct((1, 4, 512), BF16), jax.ShapeDtypeStruct((1, 4, 512), BF16)),
        in_specs=[VMEM],
        out_specs=(VMEM, VMEM),
        compiler_params=PARAMS,
    )(parts)


def solution(mesh):
    in_specs = (
        P(None, "head", None, None, None),
        P(None, "head", None, None),
        P(None, "head", None, None),
        P("head", "seq", None),
        P("head", "seq", None),
        P("head", None),
        P(),
        P("seq", "head"),
    )
    out_specs = (P("seq", None, "head"), P("seq", None, "head"))
    return jax.shard_map(local, mesh=mesh, in_specs=in_specs, out_specs=out_specs, check_vma=False)
```

```python
import jax
import jax.numpy as jnp
from jax import lax
from jax.experimental import pallas as pl
from jax.experimental.pallas import tpu as pltpu
from jax.sharding import PartitionSpec as P

KVH = 8
BLOCK = 128
SCALE = 128 ** (-0.5) * 1.4426950408889634
NEG = -(2.0**100)
F32 = jnp.float32
BF16 = jnp.bfloat16
XC_GROUPS = [[y * 8 + k for k in range(8)] for y in range(4)]
NT = (((1,), (1,)), ((), ()))
VMEM = pl.BlockSpec(memory_space=pltpu.VMEM)
ANY = pl.BlockSpec(memory_space=pl.ANY)
HBM = pl.BlockSpec(memory_space=pltpu.HBM)
PARAMS = pltpu.CompilerParams(vmem_limit_bytes=32 * 1024 * 1024)


def four_lanes(lane, tiles):
    low = jnp.where(lane < 32, tiles[0], tiles[1])
    high = jnp.where(lane < 96, tiles[2], tiles[3])
    return jnp.where(lane < 64, low, high)


def attend_kernel(
    q_hbm, k_hbm, v_hbm, ids_hbm, tk_hbm, tv_hbm, anc_hbm,
    send_ref, tree_ref,
    q_ref, k_ref, v_ref, ids_ref, tk_ref, tv_ref, anc_ref, acc_ref, stat_ref, sems,
):
    moves = [
        (ids_hbm, ids_ref),
        (k_hbm.at[0], k_ref.at[0]),
        (q_hbm, q_ref),
        (v_hbm.at[0], v_ref.at[0]),
        (k_hbm.at[1], k_ref.at[1]),
        (v_hbm.at[1], v_ref.at[1]),
        (tk_hbm, tk_ref),
        (tv_hbm, tv_ref),
        (anc_hbm, anc_ref),
    ]
    moves = [pltpu.make_async_copy(a, b, sems.at[i]) for i, (a, b) in enumerate(moves)]
    for move in moves:
        move.start()
    seq = lax.axis_index("seq")
    head = lax.axis_index("head")
    lane = lax.broadcasted_iota(jnp.int32, (8, 128), 1)
    first_half = (lane % 32) < 16
    for p in range(2):
        for at in ((0, 1, 2, 3), (4, 5))[p]:
            moves[at].wait()
        keys = k_ref[p]
        values = jnp.concatenate([v_ref[p], jnp.ones((1024, 128), BF16)], axis=1)
        ids = ids_ref[p : p + 1, :]
        bias = []
        for b in range(8):
            hit = jnp.max(jnp.where(ids == seq * 8 + b, 1.0, 0.0), axis=1, keepdims=True)
            bias.append(jnp.broadcast_to(jnp.where(hit > 0.5, 0.0, NEG), (1, BLOCK)))
        bias = jnp.concatenate(bias, axis=1)
        peaks, sums = [], []
        for a in range(2):
            q = q_ref[a, p].reshape(256, 128)
            t = lax.dot_general(q, keys, NT, preferred_element_type=F32) * SCALE
            if a == 0:
                t = t + bias
            peak = jnp.max(t, axis=1, keepdims=True).astype(BF16).astype(F32)
            w = jnp.exp2(t - peak).astype(BF16)
            peaks.append(peak)
            sums.append(jnp.dot(w, values, preferred_element_type=F32))
        for y in range(4):
            for gp in range(4):
                dest = y * 8 + p * 4 + gp
                rows = [(gp * 2 + g2) * 32 + y * 8 for g2 in range(2)]
                for a in range(2):
                    both = jnp.concatenate([sums[a][r : r + 8, :128] for r in rows], axis=0)
                    send_ref[dest, a * 16 : (a + 1) * 16, :] = both.astype(BF16)
                m = four_lanes(lane, [peaks[a][r : r + 8] for a in range(2) for r in rows])
                tot = four_lanes(lane, [sums[a][r : r + 8, 128:] for a in range(2) for r in rows])
                high = tot.astype(BF16).astype(F32)
                tot = jnp.where(first_half, high, tot - high)
                send_ref[dest, 32:48, :] = jnp.concatenate([m, tot], axis=0).astype(BF16)
    for move in moves[6:]:
        move.wait()
    y, x, core = seq // 8, (seq % 8) // 2, seq % 2
    own, gp = x // 2, (x % 2) * 2 + core
    allowed = anc_ref[head // 4] > 0
    allowed = jnp.concatenate([allowed, allowed], axis=0)
    for a in range(2):
        q = q_ref[a, own, pl.ds(gp * 2, 2)].reshape(64, 128)
        t = lax.dot_general(q, tk_ref[a, own], NT, preferred_element_type=F32) * SCALE
        t = jnp.where(allowed, t, NEG)
        peak = jnp.max(t, axis=1, keepdims=True)
        w = jnp.where(allowed, jnp.exp2(t - peak), 0.0)
        total = jnp.sum(w, axis=1, keepdims=True)
        summed = jnp.dot(w.astype(BF16), tv_ref[a, own], preferred_element_type=F32)
        acc_ref[a] = summed.reshape(2, 32, 128)
        stat_ref[0, a] = jnp.broadcast_to(peak, (64, 128)).reshape(2, 32, 128)
        stat_ref[1, a] = jnp.broadcast_to(total, (64, 128)).reshape(2, 32, 128)
    start = pl.multiple_of(y * 8, 8)
    for a in range(2):
        for g2 in range(2):
            tree_ref[a * 2 + g2] = acc_ref[a, g2, pl.ds(start, 8), :]
    for k in range(2):
        tile = four_lanes(
            lane, [stat_ref[k, a, g2, pl.ds(start, 8), :] for a in range(2) for g2 in range(2)]
        )
        tree_ref[4 + k] = tile if k == 0 else jnp.where(first_half, tile, 0.0)


def combine_kernel(got_ref, tree_ref, before_ref, out_ref):
    def spread(tile, at):
        return jnp.broadcast_to(tile[:, at : at + 1], (8, 128))

    peak = tree_ref[4]
    for s in range(32):
        peak = jnp.maximum(peak, got_ref[s, 32:48, :].astype(F32)[:8])
    factor = jnp.exp2(tree_ref[4] - peak)
    total = factor * tree_ref[5]
    summed = [spread(factor, k * 32) * tree_ref[k] for k in range(4)]
    for s in range(32):
        stat = got_ref[s, 32:48, :].astype(F32)
        factor = jnp.exp2(stat[:8] - peak)
        total = total + factor * stat[8:]
        for a in range(2):
            part = got_ref[s, a * 16 : (a + 1) * 16, :].astype(F32)
            for g2 in range(2):
                k = a * 2 + g2
                summed[k] = summed[k] + spread(factor, k * 32) * part[g2 * 8 : (g2 + 1) * 8]
    done = [
        summed[k] / (spread(total, k * 32) + spread(total, k * 32 + 16)) for k in range(4)
    ]
    rows = jnp.concatenate([done[0], done[2], done[1], done[3]], axis=0).astype(BF16)
    for h in range(16):
        out_ref[h] = rows


def project_kernel(x_ref, *refs):
    w_refs, out_ref, turn_ref = refs[:4], refs[4], refs[5]
    y = lax.axis_index("seq") // 8
    total = jnp.zeros((64, 512), F32)
    for k in range(4):
        j = (y + 4 - k) % 4
        left = jnp.concatenate(
            [
                jnp.concatenate(
                    [x_ref[r * 4 + j, g2 * 16 : (g2 + 1) * 16, :] for r in range(4)], axis=0
                )
                for g2 in range(2)
            ],
            axis=1,
        )
        total = total + jnp.dot(left, w_refs[k][...], preferred_element_type=F32)
    for r in range(4):
        for a in range(2):
            at = (r * 2 + a) * 8
            turn_ref[:, a * 4 + r, :] = total[at : at + 8]
    out_ref[...] = turn_ref[...].astype(BF16)


def add_kernel(got_ref, draft_ref, verify_ref):
    total = got_ref[0].astype(F32)
    for s in range(1, 8):
        total = total + got_ref[s].astype(F32)
    draft_ref[0] = total[:4].astype(BF16)
    verify_ref[0] = total[4:].astype(BF16)


def swap(array, axis, groups=None):
    return lax.all_to_all(array, axis, 0, 0, tiled=True, axis_index_groups=groups)


def shift(array, k):
    return lax.ppermute(array, "seq", [(s, (s + 8 * k) % 32) for s in range(32)])


def local(
    queries, tree_keys, tree_values, cache_keys, cache_values, block_ids, ancestors, out_weight
):
    send, tree = pl.pallas_call(
        attend_kernel,
        out_shape=(
            jax.ShapeDtypeStruct((32, 48, 128), BF16),
            jax.ShapeDtypeStruct((6, 8, 128), F32),
        ),
        in_specs=[HBM] * 7,
        out_specs=(VMEM, VMEM),
        scratch_shapes=[
            pltpu.VMEM((2, 2, 8, 32, 128), BF16),
            pltpu.VMEM((2, 1024, 128), BF16),
            pltpu.VMEM((2, 1024, 128), BF16),
            pltpu.VMEM((2, 32), jnp.int32),
            pltpu.VMEM((2, 2, 32, 128), BF16),
            pltpu.VMEM((2, 2, 32, 128), BF16),
            pltpu.VMEM((4, 32, 32), jnp.int32),
            pltpu.VMEM((2, 2, 32, 128), F32),
            pltpu.VMEM((2, 2, 2, 32, 128), F32),
            pltpu.SemaphoreType.DMA((9,)),
        ],
        compiler_params=pltpu.CompilerParams(vmem_limit_bytes=55296 * 1024),
    )(queries, cache_keys, cache_values, block_ids, tree_keys, tree_values, ancestors)
    got = swap(send, "seq")
    one, three = shift(out_weight, 1), shift(out_weight, 3)
    rows = pl.pallas_call(
        combine_kernel,
        out_shape=jax.ShapeDtypeStruct((16, 32, 128), BF16),
        in_specs=[VMEM, VMEM, ANY],
        out_specs=VMEM,
        compiler_params=PARAMS,
    )(got, tree, one)
    gathered = swap(rows, "head")
    two = shift(out_weight, 2)
    parts = pl.pallas_call(
        project_kernel,
        out_shape=jax.ShapeDtypeStruct((8, 8, 512), BF16),
        in_specs=[VMEM] * 5,
        out_specs=VMEM,
        scratch_shapes=[pltpu.VMEM((8, 8, 512), F32)],
        compiler_params=PARAMS,
    )(gathered, out_weight, one, two, three)
    parts = swap(parts, "seq", XC_GROUPS)
    return pl.pallas_call(
        add_kernel,
        out_shape=(jax.ShapeDtypeStruct((1, 4, 512), BF16), jax.ShapeDtypeStruct((1, 4, 512), BF16)),
        in_specs=[VMEM],
        out_specs=(VMEM, VMEM),
        compiler_params=PARAMS,
    )(parts)


def solution(mesh):
    in_specs = (
        P(None, "head", None, None, None),
        P(None, "head", None, None),
        P(None, "head", None, None),
        P("head", "seq", None),
        P("head", "seq", None),
        P("head", None),
        P(),
        P("seq", "head"),
    )
    out_specs = (P("seq", None, "head"), P("seq", None, "head"))
    return jax.shard_map(local, mesh=mesh, in_specs=in_specs, out_specs=out_specs, check_vma=False)
```

```python
import jax
import jax.numpy as jnp
from jax import lax
from jax.experimental import pallas as pl
from jax.experimental.pallas import tpu as pltpu
from jax.sharding import PartitionSpec as P

KVH = 8
BLOCK = 128
SCALE = 128 ** (-0.5) * 1.4426950408889634
NEG = -(2.0**100)
F32 = jnp.float32
BF16 = jnp.bfloat16
XC_GROUPS = [[y * 8 + k for k in range(8)] for y in range(4)]
NT = (((1,), (1,)), ((), ()))
VMEM = pl.BlockSpec(memory_space=pltpu.VMEM)
ANY = pl.BlockSpec(memory_space=pl.ANY)
HBM = pl.BlockSpec(memory_space=pltpu.HBM)
PARAMS = pltpu.CompilerParams(vmem_limit_bytes=32 * 1024 * 1024)


def four_lanes(lane, tiles):
    low = jnp.where(lane < 32, tiles[0], tiles[1])
    high = jnp.where(lane < 96, tiles[2], tiles[3])
    return jnp.where(lane < 64, low, high)


def attend_kernel(
    q_hbm, k_hbm, v_hbm, ids_hbm, tk_hbm, tv_hbm, anc_hbm,
    send_ref, tree_ref,
    q_ref, k_ref, v_ref, ids_ref, tk_ref, tv_ref, anc_ref, acc_ref, stat_ref, sems,
):
    moves = [
        (ids_hbm, ids_ref),
        (k_hbm.at[0], k_ref.at[0]),
        (q_hbm, q_ref),
        (v_hbm.at[0], v_ref.at[0]),
        (k_hbm.at[1], k_ref.at[1]),
        (v_hbm.at[1], v_ref.at[1]),
        (tk_hbm, tk_ref),
        (tv_hbm, tv_ref),
        (anc_hbm, anc_ref),
    ]
    moves = [pltpu.make_async_copy(a, b, sems.at[i]) for i, (a, b) in enumerate(moves)]
    for move in moves:
        move.start()
    seq = lax.axis_index("seq")
    head = lax.axis_index("head")
    lane = lax.broadcasted_iota(jnp.int32, (8, 128), 1)
    first_half = (lane % 32) < 16
    for p in range(2):
        for at in ((0, 1, 2, 3), (4, 5))[p]:
            moves[at].wait()
        keys = k_ref[p]
        values = jnp.concatenate([v_ref[p], jnp.ones((1024, 128), BF16)], axis=1)
        ids = ids_ref[p : p + 1, :]
        bias = []
        for b in range(8):
            hit = jnp.max(jnp.where(ids == seq * 8 + b, 1.0, 0.0), axis=1, keepdims=True)
            bias.append(jnp.broadcast_to(jnp.where(hit > 0.5, 0.0, NEG), (1, BLOCK)))
        bias = jnp.concatenate(bias, axis=1)
        peaks, sums = [], []
        for a in range(2):
            q = q_ref[a, p].reshape(256, 128)
            t = lax.dot_general(q, keys, NT, preferred_element_type=F32) * SCALE
            if a == 0:
                t = t + bias
            peak = jnp.max(t, axis=1, keepdims=True).astype(BF16).astype(F32)
            w = jnp.exp2(t - peak).astype(BF16)
            peaks.append(peak)
            sums.append(jnp.dot(w, values, preferred_element_type=F32))
        for y in range(4):
            for gp in range(4):
                dest = y * 8 + p * 4 + gp
                rows = [(gp * 2 + g2) * 32 + y * 8 for g2 in range(2)]
                for a in range(2):
                    both = jnp.concatenate([sums[a][r : r + 8, :128] for r in rows], axis=0)
                    send_ref[dest, a * 16 : (a + 1) * 16, :] = both.astype(BF16)
                m = four_lanes(lane, [peaks[a][r : r + 8] for a in range(2) for r in rows])
                tot = four_lanes(lane, [sums[a][r : r + 8, 128:] for a in range(2) for r in rows])
                high = tot.astype(BF16).astype(F32)
                tot = jnp.where(first_half, high, tot - high)
                send_ref[dest, 32:48, :] = jnp.concatenate([m, tot], axis=0).astype(BF16)
    for move in moves[6:]:
        move.wait()
    y, x, core = seq // 8, (seq % 8) // 2, seq % 2
    own, gp = x // 2, (x % 2) * 2 + core
    allowed = anc_ref[head // 4] > 0
    allowed = jnp.concatenate([allowed, allowed], axis=0)
    for a in range(2):
        q = q_ref[a, own, pl.ds(gp * 2, 2)].reshape(64, 128)
        t = lax.dot_general(q, tk_ref[a, own], NT, preferred_element_type=F32) * SCALE
        t = jnp.where(allowed, t, NEG)
        peak = jnp.max(t, axis=1, keepdims=True)
        w = jnp.where(allowed, jnp.exp2(t - peak), 0.0)
        total = jnp.sum(w, axis=1, keepdims=True)
        summed = jnp.dot(w.astype(BF16), tv_ref[a, own], preferred_element_type=F32)
        acc_ref[a] = summed.reshape(2, 32, 128)
        stat_ref[0, a] = jnp.broadcast_to(peak, (64, 128)).reshape(2, 32, 128)
        stat_ref[1, a] = jnp.broadcast_to(total, (64, 128)).reshape(2, 32, 128)
    start = pl.multiple_of(y * 8, 8)
    for a in range(2):
        for g2 in range(2):
            tree_ref[a * 2 + g2] = acc_ref[a, g2, pl.ds(start, 8), :]
    for k in range(2):
        tile = four_lanes(
            lane, [stat_ref[k, a, g2, pl.ds(start, 8), :] for a in range(2) for g2 in range(2)]
        )
        tree_ref[4 + k] = tile if k == 0 else jnp.where(first_half, tile, 0.0)


def combine_kernel(got_ref, tree_ref, out_ref):
    def spread(tile, at):
        return jnp.broadcast_to(tile[:, at : at + 1], (8, 128))

    peak = tree_ref[4]
    for s in range(32):
        peak = jnp.maximum(peak, got_ref[s, 32:48, :].astype(F32)[:8])
    factor = jnp.exp2(tree_ref[4] - peak)
    total = factor * tree_ref[5]
    summed = [spread(factor, k * 32) * tree_ref[k] for k in range(4)]
    for s in range(32):
        stat = got_ref[s, 32:48, :].astype(F32)
        factor = jnp.exp2(stat[:8] - peak)
        total = total + factor * stat[8:]
        for a in range(2):
            part = got_ref[s, a * 16 : (a + 1) * 16, :].astype(F32)
            for g2 in range(2):
                k = a * 2 + g2
                summed[k] = summed[k] + spread(factor, k * 32) * part[g2 * 8 : (g2 + 1) * 8]
    done = [
        summed[k] / (spread(total, k * 32) + spread(total, k * 32 + 16)) for k in range(4)
    ]
    rows = jnp.concatenate([done[0], done[2], done[1], done[3]], axis=0).astype(BF16)
    for h in range(16):
        out_ref[h] = rows


def project_kernel(x_ref, *refs):
    w_refs, out_ref, turn_ref = refs[:4], refs[4], refs[5]
    y = lax.axis_index("seq") // 8
    total = jnp.zeros((64, 512), F32)
    for k in range(4):
        j = (y + 4 - k) % 4
        left = jnp.concatenate(
            [
                jnp.concatenate(
                    [x_ref[r * 4 + j, g2 * 16 : (g2 + 1) * 16, :] for r in range(4)], axis=0
                )
                for g2 in range(2)
            ],
            axis=1,
        )
        total = total + jnp.dot(left, w_refs[k][...], preferred_element_type=F32)
    for r in range(4):
        for a in range(2):
            at = (r * 2 + a) * 8
            turn_ref[:, a * 4 + r, :] = total[at : at + 8]
    out_ref[...] = turn_ref[...].astype(BF16)


def add_kernel(got_ref, draft_ref, verify_ref):
    total = got_ref[0].astype(F32)
    for s in range(1, 8):
        total = total + got_ref[s].astype(F32)
    draft_ref[0] = total[:4].astype(BF16)
    verify_ref[0] = total[4:].astype(BF16)


def swap(array, axis, groups=None):
    return lax.all_to_all(array, axis, 0, 0, tiled=True, axis_index_groups=groups)


def shift(array, k):
    return lax.ppermute(array, "seq", [(s, (s + 8 * k) % 32) for s in range(32)])


def local(
    queries, tree_keys, tree_values, cache_keys, cache_values, block_ids, ancestors, out_weight
):
    send, tree = pl.pallas_call(
        attend_kernel,
        out_shape=(
            jax.ShapeDtypeStruct((32, 48, 128), BF16),
            jax.ShapeDtypeStruct((6, 8, 128), F32),
        ),
        in_specs=[HBM] * 7,
        out_specs=(VMEM, VMEM),
        scratch_shapes=[
            pltpu.VMEM((2, 2, 8, 32, 128), BF16),
            pltpu.VMEM((2, 1024, 128), BF16),
            pltpu.VMEM((2, 1024, 128), BF16),
            pltpu.VMEM((2, 32), jnp.int32),
            pltpu.VMEM((2, 2, 32, 128), BF16),
            pltpu.VMEM((2, 2, 32, 128), BF16),
            pltpu.VMEM((4, 32, 32), jnp.int32),
            pltpu.VMEM((2, 2, 32, 128), F32),
            pltpu.VMEM((2, 2, 2, 32, 128), F32),
            pltpu.SemaphoreType.DMA((9,)),
        ],
        compiler_params=pltpu.CompilerParams(vmem_limit_bytes=55296 * 1024),
    )(queries, cache_keys, cache_values, block_ids, tree_keys, tree_values, ancestors)
    got = swap(send, "seq")
    one, three = shift(out_weight, 1), shift(out_weight, 3)
    rows = pl.pallas_call(
        combine_kernel,
        out_shape=jax.ShapeDtypeStruct((16, 32, 128), BF16),
        in_specs=[VMEM, VMEM],
        out_specs=VMEM,
        compiler_params=PARAMS,
    )(got, tree)
    gathered = swap(rows, "head")
    two = shift(one, 1)
    parts = pl.pallas_call(
        project_kernel,
        out_shape=jax.ShapeDtypeStruct((8, 8, 512), BF16),
        in_specs=[VMEM] * 5,
        out_specs=VMEM,
        scratch_shapes=[pltpu.VMEM((8, 8, 512), F32)],
        compiler_params=PARAMS,
    )(gathered, out_weight, one, two, three)
    parts = swap(parts, "seq", XC_GROUPS)
    return pl.pallas_call(
        add_kernel,
        out_shape=(jax.ShapeDtypeStruct((1, 4, 512), BF16), jax.ShapeDtypeStruct((1, 4, 512), BF16)),
        in_specs=[VMEM],
        out_specs=(VMEM, VMEM),
        compiler_params=PARAMS,
    )(parts)


def solution(mesh):
    in_specs = (
        P(None, "head", None, None, None),
        P(None, "head", None, None),
        P(None, "head", None, None),
        P("head", "seq", None),
        P("head", "seq", None),
        P("head", None),
        P(),
        P("seq", "head"),
    )
    out_specs = (P("seq", None, "head"), P("seq", None, "head"))
    return jax.shard_map(local, mesh=mesh, in_specs=in_specs, out_specs=out_specs, check_vma=False)
```

```python
import jax
import jax.numpy as jnp
from jax import lax
from jax.experimental import pallas as pl
from jax.experimental.pallas import tpu as pltpu
from jax.sharding import PartitionSpec as P

KVH = 8
BLOCK = 128
SCALE = 128 ** (-0.5) * 1.4426950408889634
NEG = -(2.0**100)
F32 = jnp.float32
BF16 = jnp.bfloat16
XC_GROUPS = [[y * 8 + k for k in range(8)] for y in range(4)]
NT = (((1,), (1,)), ((), ()))
VMEM = pl.BlockSpec(memory_space=pltpu.VMEM)
ANY = pl.BlockSpec(memory_space=pl.ANY)
HBM = pl.BlockSpec(memory_space=pltpu.HBM)
PARAMS = pltpu.CompilerParams(vmem_limit_bytes=32 * 1024 * 1024)


def four_lanes(lane, tiles):
    low = jnp.where(lane < 32, tiles[0], tiles[1])
    high = jnp.where(lane < 96, tiles[2], tiles[3])
    return jnp.where(lane < 64, low, high)


def attend_kernel(
    q_hbm, k_hbm, v_hbm, ids_hbm, tk_hbm, tv_hbm, anc_hbm,
    send_ref, tree_ref,
    q_ref, k_ref, v_ref, ids_ref, tk_ref, tv_ref, anc_ref, acc_ref, stat_ref, sems,
):
    moves = [
        (ids_hbm, ids_ref),
        (k_hbm.at[0], k_ref.at[0]),
        (q_hbm, q_ref),
        (v_hbm.at[0], v_ref.at[0]),
        (k_hbm.at[1], k_ref.at[1]),
        (v_hbm.at[1], v_ref.at[1]),
        (tk_hbm, tk_ref),
        (tv_hbm, tv_ref),
        (anc_hbm, anc_ref),
    ]
    moves = [pltpu.make_async_copy(a, b, sems.at[i]) for i, (a, b) in enumerate(moves)]
    for move in moves:
        move.start()
    seq = lax.axis_index("seq")
    head = lax.axis_index("head")
    lane = lax.broadcasted_iota(jnp.int32, (8, 128), 1)
    first_half = (lane % 32) < 16
    for p in range(2):
        for at in ((0, 1, 2, 3), (4, 5))[p]:
            moves[at].wait()
        keys = k_ref[p]
        values = jnp.concatenate([v_ref[p], jnp.ones((1024, 128), BF16)], axis=1)
        ids = ids_ref[p : p + 1, :]
        bias = []
        for b in range(8):
            hit = jnp.max(jnp.where(ids == seq * 8 + b, 1.0, 0.0), axis=1, keepdims=True)
            bias.append(jnp.broadcast_to(jnp.where(hit > 0.5, 0.0, NEG), (1, BLOCK)))
        bias = jnp.concatenate(bias, axis=1)
        peaks, sums = [], []
        for a in range(2):
            q = q_ref[a, p].reshape(256, 128)
            t = lax.dot_general(q, keys, NT, preferred_element_type=F32) * SCALE
            if a == 0:
                t = t + bias
            peak = jnp.max(t, axis=1, keepdims=True).astype(BF16).astype(F32)
            w = jnp.exp2(t - peak).astype(BF16)
            peaks.append(peak)
            sums.append(jnp.dot(w, values, preferred_element_type=F32))
        for y in range(4):
            for gp in range(4):
                dest = y * 8 + p * 4 + gp
                rows = [(gp * 2 + g2) * 32 + y * 8 for g2 in range(2)]
                for a in range(2):
                    both = jnp.concatenate([sums[a][r : r + 8, :128] for r in rows], axis=0)
                    send_ref[dest, a * 16 : (a + 1) * 16, :] = both.astype(BF16)
                m = four_lanes(lane, [peaks[a][r : r + 8] for a in range(2) for r in rows])
                tot = four_lanes(lane, [sums[a][r : r + 8, 128:] for a in range(2) for r in rows])
                high = tot.astype(BF16).astype(F32)
                tot = jnp.where(first_half, high, tot - high)
                send_ref[dest, 32:48, :] = jnp.concatenate([m, tot], axis=0).astype(BF16)
    for move in moves[6:]:
        move.wait()
    y, x, core = seq // 8, (seq % 8) // 2, seq % 2
    own, gp = x // 2, (x % 2) * 2 + core
    allowed = anc_ref[head // 4] > 0
    allowed = jnp.concatenate([allowed, allowed], axis=0)
    for a in range(2):
        q = q_ref[a, own, pl.ds(gp * 2, 2)].reshape(64, 128)
        t = lax.dot_general(q, tk_ref[a, own], NT, preferred_element_type=F32) * SCALE
        t = jnp.where(allowed, t, NEG)
        peak = jnp.max(t, axis=1, keepdims=True)
        w = jnp.where(allowed, jnp.exp2(t - peak), 0.0)
        total = jnp.sum(w, axis=1, keepdims=True)
        summed = jnp.dot(w.astype(BF16), tv_ref[a, own], preferred_element_type=F32)
        acc_ref[a] = summed.reshape(2, 32, 128)
        stat_ref[0, a] = jnp.broadcast_to(peak, (64, 128)).reshape(2, 32, 128)
        stat_ref[1, a] = jnp.broadcast_to(total, (64, 128)).reshape(2, 32, 128)
    start = pl.multiple_of(y * 8, 8)
    for a in range(2):
        for g2 in range(2):
            tree_ref[a * 2 + g2] = acc_ref[a, g2, pl.ds(start, 8), :]
    for k in range(2):
        tile = four_lanes(
            lane, [stat_ref[k, a, g2, pl.ds(start, 8), :] for a in range(2) for g2 in range(2)]
        )
        tree_ref[4 + k] = tile if k == 0 else jnp.where(first_half, tile, 0.0)


def combine_kernel(got_ref, tree_ref, out_ref):
    def spread(tile, at):
        return jnp.broadcast_to(tile[:, at : at + 1], (8, 128))

    peak = tree_ref[4]
    for s in range(32):
        peak = jnp.maximum(peak, got_ref[s, 32:48, :].astype(F32)[:8])
    factor = jnp.exp2(tree_ref[4] - peak)
    total = factor * tree_ref[5]
    summed = [spread(factor, k * 32) * tree_ref[k] for k in range(4)]
    for s in range(32):
        stat = got_ref[s, 32:48, :].astype(F32)
        factor = jnp.exp2(stat[:8] - peak)
        total = total + factor * stat[8:]
        for a in range(2):
            part = got_ref[s, a * 16 : (a + 1) * 16, :].astype(F32)
            for g2 in range(2):
                k = a * 2 + g2
                summed[k] = summed[k] + spread(factor, k * 32) * part[g2 * 8 : (g2 + 1) * 8]
    done = [
        summed[k] / (spread(total, k * 32) + spread(total, k * 32 + 16)) for k in range(4)
    ]
    rows = jnp.concatenate([done[0], done[2], done[1], done[3]], axis=0).astype(BF16)
    for h in range(16):
        out_ref[h] = rows


def onward_kernel(one_ref, three_ref, out_ref):
    del three_ref
    out_ref[...] = one_ref[...]


def project_kernel(x_ref, *refs):
    w_refs, out_ref, turn_ref = refs[:4], refs[4], refs[5]
    y = lax.axis_index("seq") // 8
    total = jnp.zeros((64, 512), F32)
    for k in range(4):
        j = (y + 4 - k) % 4
        left = jnp.concatenate(
            [
                jnp.concatenate(
                    [x_ref[r * 4 + j, g2 * 16 : (g2 + 1) * 16, :] for r in range(4)], axis=0
                )
                for g2 in range(2)
            ],
            axis=1,
        )
        total = total + jnp.dot(left, w_refs[k][...], preferred_element_type=F32)
    for r in range(4):
        for a in range(2):
            at = (r * 2 + a) * 8
            turn_ref[:, a * 4 + r, :] = total[at : at + 8]
    out_ref[...] = turn_ref[...].astype(BF16)


def add_kernel(got_ref, draft_ref, verify_ref):
    total = got_ref[0].astype(F32)
    for s in range(1, 8):
        total = total + got_ref[s].astype(F32)
    draft_ref[0] = total[:4].astype(BF16)
    verify_ref[0] = total[4:].astype(BF16)


def swap(array, axis, groups=None):
    return lax.all_to_all(array, axis, 0, 0, tiled=True, axis_index_groups=groups)


def shift(array, k):
    return lax.ppermute(array, "seq", [(s, (s + 8 * k) % 32) for s in range(32)])


def local(
    queries, tree_keys, tree_values, cache_keys, cache_values, block_ids, ancestors, out_weight
):
    send, tree = pl.pallas_call(
        attend_kernel,
        out_shape=(
            jax.ShapeDtypeStruct((32, 48, 128), BF16),
            jax.ShapeDtypeStruct((6, 8, 128), F32),
        ),
        in_specs=[HBM] * 7,
        out_specs=(VMEM, VMEM),
        scratch_shapes=[
            pltpu.VMEM((2, 2, 8, 32, 128), BF16),
            pltpu.VMEM((2, 1024, 128), BF16),
            pltpu.VMEM((2, 1024, 128), BF16),
            pltpu.VMEM((2, 32), jnp.int32),
            pltpu.VMEM((2, 2, 32, 128), BF16),
            pltpu.VMEM((2, 2, 32, 128), BF16),
            pltpu.VMEM((4, 32, 32), jnp.int32),
            pltpu.VMEM((2, 2, 32, 128), F32),
            pltpu.VMEM((2, 2, 2, 32, 128), F32),
            pltpu.SemaphoreType.DMA((9,)),
        ],
        compiler_params=pltpu.CompilerParams(vmem_limit_bytes=55296 * 1024),
    )(queries, cache_keys, cache_values, block_ids, tree_keys, tree_values, ancestors)
    got = swap(send, "seq")
    one, three = shift(out_weight, 1), shift(out_weight, 3)
    rows = pl.pallas_call(
        combine_kernel,
        out_shape=jax.ShapeDtypeStruct((16, 32, 128), BF16),
        in_specs=[VMEM, VMEM],
        out_specs=VMEM,
        compiler_params=PARAMS,
    )(got, tree)
    gathered = swap(rows, "head")
    onward = pl.pallas_call(
        onward_kernel,
        out_shape=jax.ShapeDtypeStruct((256, 512), BF16),
        in_specs=[VMEM, ANY],
        out_specs=VMEM,
        cost_estimate=pl.CostEstimate(flops=10**10, bytes_accessed=0, transcendentals=0),
        compiler_params=PARAMS,
    )(one, three)
    two = shift(onward, 1)
    parts = pl.pallas_call(
        project_kernel,
        out_shape=jax.ShapeDtypeStruct((8, 8, 512), BF16),
        in_specs=[VMEM] * 5,
        out_specs=VMEM,
        scratch_shapes=[pltpu.VMEM((8, 8, 512), F32)],
        compiler_params=PARAMS,
    )(gathered, out_weight, one, two, three)
    parts = swap(parts, "seq", XC_GROUPS)
    return pl.pallas_call(
        add_kernel,
        out_shape=(jax.ShapeDtypeStruct((1, 4, 512), BF16), jax.ShapeDtypeStruct((1, 4, 512), BF16)),
        in_specs=[VMEM],
        out_specs=(VMEM, VMEM),
        compiler_params=PARAMS,
    )(parts)


def solution(mesh):
    in_specs = (
        P(None, "head", None, None, None),
        P(None, "head", None, None),
        P(None, "head", None, None),
        P("head", "seq", None),
        P("head", "seq", None),
        P("head", None),
        P(),
        P("seq", "head"),
    )
    out_specs = (P("seq", None, "head"), P("seq", None, "head"))
    return jax.shard_map(local, mesh=mesh, in_specs=in_specs, out_specs=out_specs, check_vma=False)
```

```python
import jax
import jax.numpy as jnp
from jax import lax
from jax.experimental import pallas as pl
from jax.experimental.pallas import tpu as pltpu
from jax.sharding import PartitionSpec as P

KVH = 8
BLOCK = 128
SCALE = 128 ** (-0.5) * 1.4426950408889634
NEG = -(2.0**100)
F32 = jnp.float32
BF16 = jnp.bfloat16
XC_GROUPS = [[y * 8 + k for k in range(8)] for y in range(4)]
NT = (((1,), (1,)), ((), ()))
VMEM = pl.BlockSpec(memory_space=pltpu.VMEM)
ANY = pl.BlockSpec(memory_space=pl.ANY)
HBM = pl.BlockSpec(memory_space=pltpu.HBM)
PARAMS = pltpu.CompilerParams(vmem_limit_bytes=32 * 1024 * 1024)


def four_lanes(lane, tiles):
    low = jnp.where(lane < 32, tiles[0], tiles[1])
    high = jnp.where(lane < 96, tiles[2], tiles[3])
    return jnp.where(lane < 64, low, high)


def attend_kernel(
    q_hbm, k_hbm, v_hbm, ids_hbm, tk_hbm, tv_hbm, anc_hbm,
    send_hbm, tree_hbm,
    q_ref, k_ref, v_ref, ids_ref, tk_ref, tv_ref, anc_ref,
    send_ref, tree_ref, acc_ref, stat_ref, sems, out_sems,
):
    moves = [
        (k_hbm.at[0], k_ref.at[0]),
        (q_hbm, q_ref),
        (ids_hbm, ids_ref),
        (v_hbm.at[0], v_ref.at[0]),
        (tk_hbm, tk_ref),
        (tv_hbm, tv_ref),
        (anc_hbm, anc_ref),
        (k_hbm.at[1], k_ref.at[1]),
        (v_hbm.at[1], v_ref.at[1]),
    ]
    moves = [pltpu.make_async_copy(a, b, sems.at[i]) for i, (a, b) in enumerate(moves)]
    for move in moves:
        move.start()
    seq = lax.axis_index("seq")
    head = lax.axis_index("head")
    lane = lax.broadcasted_iota(jnp.int32, (8, 128), 1)
    part = (lane % 32) // 8
    leaving = []

    def leave(source, target):
        copy = pltpu.make_async_copy(source, target, out_sems.at[len(leaving)])
        copy.start()
        leaving.append(copy)

    def tree_part():
        y, x, core = seq // 8, (seq % 8) // 2, seq % 2
        own, gp = x // 2, (x % 2) * 2 + core
        allowed = anc_ref[head // 4] > 0
        allowed = jnp.concatenate([allowed, allowed], axis=0)
        for a in range(2):
            q = q_ref[a, own, pl.ds(gp * 2, 2)].reshape(64, 128)
            t = lax.dot_general(q, tk_ref[a, own], NT, preferred_element_type=F32) * SCALE
            t = jnp.where(allowed, t, NEG)
            peak = jnp.max(t, axis=1, keepdims=True)
            w = jnp.where(allowed, jnp.exp2(t - peak), 0.0)
            total = jnp.sum(w, axis=1, keepdims=True)
            summed = jnp.dot(w.astype(BF16), tv_ref[a, own], preferred_element_type=F32)
            acc_ref[a] = summed.reshape(2, 32, 128)
            stat_ref[0, a] = jnp.broadcast_to(peak, (64, 128)).reshape(2, 32, 128)
            stat_ref[1, a] = jnp.broadcast_to(total, (64, 128)).reshape(2, 32, 128)
        start = pl.multiple_of(y * 8, 8)
        for a in range(2):
            for g2 in range(2):
                tree_ref[a * 2 + g2] = acc_ref[a, g2, pl.ds(start, 8), :]
        peak, total = (
            four_lanes(
                lane, [stat_ref[k, a, g2, pl.ds(start, 8), :] for a in range(2) for g2 in range(2)]
            )
            for k in range(2)
        )
        tree_ref[4] = peak
        tree_ref[5] = jnp.where(part == 2, total, 0.0)

    for move in moves[:3]:
        move.wait()
    for p in range(2):
        if p == 1:
            for move in moves[4:]:
                move.wait()
        keys = k_ref[p]
        ids = ids_ref[p : p + 1, :]
        bias = []
        for b in range(8):
            hit = jnp.max(jnp.where(ids == seq * 8 + b, 1.0, 0.0), axis=1, keepdims=True)
            bias.append(jnp.broadcast_to(jnp.where(hit > 0.5, 0.0, NEG), (1, BLOCK)))
        bias = jnp.concatenate(bias, axis=1)
        peaks, weights = [], []
        for a in range(2):
            q = q_ref[a, p].reshape(256, 128)
            t = lax.dot_general(q, keys, NT, preferred_element_type=F32) * SCALE
            if a == 0:
                t = t + bias
            peak = jnp.max(t, axis=1, keepdims=True).astype(BF16).astype(F32)
            weights.append(jnp.exp2(t - peak).astype(BF16))
            peaks.append(peak)
        if p == 0:
            moves[3].wait()
        values = jnp.concatenate([v_ref[p], jnp.ones((1024, 128), BF16)], axis=1)
        sums = [jnp.dot(w, values, preferred_element_type=F32) for w in weights]
        if p == 1:
            tree_part()
        for y in range(4):
            for gp in range(4):
                dest = y * 8 + p * 4 + gp
                rows = [(gp * 2 + g2) * 32 + y * 8 for g2 in range(2)]
                for a in range(2):
                    both = jnp.concatenate([sums[a][r : r + 8, :128] for r in rows], axis=0)
                    send_ref[dest, a * 16 : (a + 1) * 16, :] = both.astype(BF16)
                m = four_lanes(lane, [peaks[a][r : r + 8] for a in range(2) for r in rows])
                tot = four_lanes(lane, [sums[a][r : r + 8, 128:] for a in range(2) for r in rows])
                high = tot.astype(BF16).astype(F32)
                stat = jnp.where(part < 2, m, jnp.where(part == 2, high, tot - high))
                send_ref[dest, 32:40, :] = stat.astype(BF16)
            chunk = pl.ds(y * 8 + p * 4, 4)
            leave(send_ref.at[chunk], send_hbm.at[chunk])
    leave(tree_ref, tree_hbm)
    for copy in leaving:
        copy.wait()


def combine_kernel(got_ref, tree_ref, out_ref):
    def spread(tile, at):
        return jnp.broadcast_to(tile[:, at : at + 1], (8, 128))

    peak = tree_ref[4]
    for s in range(32):
        peak = jnp.maximum(peak, got_ref[s, 32:40, :].astype(F32))
    factor = jnp.exp2(tree_ref[4] - peak)
    total = pltpu.roll(factor, 16, 1) * tree_ref[5]
    summed = [spread(factor, k * 32) * tree_ref[k] for k in range(4)]
    for s in range(32):
        stat = got_ref[s, 32:40, :].astype(F32)
        factor = jnp.exp2(stat - peak)
        total = total + pltpu.roll(factor, 16, 1) * stat
        for a in range(2):
            part = got_ref[s, a * 16 : (a + 1) * 16, :].astype(F32)
            for g2 in range(2):
                k = a * 2 + g2
                summed[k] = summed[k] + spread(factor, k * 32) * part[g2 * 8 : (g2 + 1) * 8]
    done = [
        summed[k] / (spread(total, k * 32 + 16) + spread(total, k * 32 + 24)) for k in range(4)
    ]
    rows = jnp.concatenate([done[0], done[2], done[1], done[3]], axis=0).astype(BF16)
    for h in range(16):
        out_ref[h] = rows


def onward_kernel(one_ref, three_ref, out_ref):
    del three_ref
    out_ref[...] = one_ref[...]


def project_kernel(x_ref, *refs):
    w_refs, out_ref, turn_ref = refs[:4], refs[4], refs[5]
    y = lax.axis_index("seq") // 8
    total = jnp.zeros((64, 512), F32)
    for k in range(4):
        j = (y + 4 - k) % 4
        left = jnp.concatenate(
            [
                jnp.concatenate(
                    [x_ref[r * 4 + j, g2 * 16 : (g2 + 1) * 16, :] for r in range(4)], axis=0
                )
                for g2 in range(2)
            ],
            axis=1,
        )
        total = total + jnp.dot(left, w_refs[k][...], preferred_element_type=F32)
    for r in range(4):
        for a in range(2):
            at = (r * 2 + a) * 8
            turn_ref[:, a * 4 + r, :] = total[at : at + 8]
    out_ref[...] = turn_ref[...].astype(BF16)


def add_kernel(got_ref, draft_ref, verify_ref):
    total = got_ref[0].astype(F32)
    for s in range(1, 8):
        total = total + got_ref[s].astype(F32)
    draft_ref[0] = total[:4].astype(BF16)
    verify_ref[0] = total[4:].astype(BF16)


def swap(array, axis, groups=None):
    return lax.all_to_all(array, axis, 0, 0, tiled=True, axis_index_groups=groups)


def attend(
    queries, cache_keys, cache_values, block_ids, tree_keys, tree_values, ancestors
):
    return pl.pallas_call(
        attend_kernel,
        out_shape=(
            jax.ShapeDtypeStruct((32, 40, 128), BF16),
            jax.ShapeDtypeStruct((6, 8, 128), F32),
        ),
        in_specs=[HBM] * 7,
        out_specs=(HBM, HBM),
        scratch_shapes=[
            pltpu.VMEM((2, 2, 8, 32, 128), BF16),
            pltpu.VMEM((2, 1024, 128), BF16),
            pltpu.VMEM((2, 1024, 128), BF16),
            pltpu.VMEM((2, 32), jnp.int32),
            pltpu.VMEM((2, 2, 32, 128), BF16),
            pltpu.VMEM((2, 2, 32, 128), BF16),
            pltpu.VMEM((4, 32, 32), jnp.int32),
            pltpu.VMEM((32, 40, 128), BF16),
            pltpu.VMEM((6, 8, 128), F32),
            pltpu.VMEM((2, 2, 32, 128), F32),
            pltpu.VMEM((2, 2, 2, 32, 128), F32),
            pltpu.SemaphoreType.DMA((9,)),
            pltpu.SemaphoreType.DMA((9,)),
        ],
        compiler_params=pltpu.CompilerParams(vmem_limit_bytes=55296 * 1024),
    )(queries, cache_keys, cache_values, block_ids, tree_keys, tree_values, ancestors)


def shift(array, k):
    return lax.ppermute(array, "seq", [(s, (s + 8 * k) % 32) for s in range(32)])


def local(
    queries, tree_keys, tree_values, cache_keys, cache_values, block_ids, ancestors, out_weight
):
    send, tree = attend(
        queries, cache_keys, cache_values, block_ids, tree_keys, tree_values, ancestors
    )
    got = swap(send, "seq")
    one, three = shift(out_weight, 1), shift(out_weight, 3)
    rows = pl.pallas_call(
        combine_kernel,
        out_shape=jax.ShapeDtypeStruct((16, 32, 128), BF16),
        in_specs=[VMEM, VMEM],
        out_specs=VMEM,
        compiler_params=PARAMS,
    )(got, tree)
    gathered = swap(rows, "head")
    onward = pl.pallas_call(
        onward_kernel,
        out_shape=jax.ShapeDtypeStruct((256, 512), BF16),
        in_specs=[VMEM, ANY],
        out_specs=VMEM,
        cost_estimate=pl.CostEstimate(flops=10**10, bytes_accessed=0, transcendentals=0),
        compiler_params=PARAMS,
    )(one, three)
    two = shift(onward, 1)
    parts = pl.pallas_call(
        project_kernel,
        out_shape=jax.ShapeDtypeStruct((8, 8, 512), BF16),
        in_specs=[VMEM] * 5,
        out_specs=VMEM,
        scratch_shapes=[pltpu.VMEM((8, 8, 512), F32)],
        compiler_params=PARAMS,
    )(gathered, out_weight, one, two, three)
    parts = swap(parts, "seq", XC_GROUPS)
    return pl.pallas_call(
        add_kernel,
        out_shape=(jax.ShapeDtypeStruct((1, 4, 512), BF16), jax.ShapeDtypeStruct((1, 4, 512), BF16)),
        in_specs=[VMEM],
        out_specs=(VMEM, VMEM),
        compiler_params=PARAMS,
    )(parts)


def solution(mesh):
    in_specs = (
        P(None, "head", None, None, None),
        P(None, "head", None, None),
        P(None, "head", None, None),
        P("head", "seq", None),
        P("head", "seq", None),
        P("head", None),
        P(),
        P("seq", "head"),
    )
    out_specs = (P("seq", None, "head"), P("seq", None, "head"))
    return jax.shard_map(local, mesh=mesh, in_specs=in_specs, out_specs=out_specs, check_vma=False)
```

```python
import jax
import jax.numpy as jnp
from jax import lax
from jax.experimental import pallas as pl
from jax.experimental.pallas import tpu as pltpu
from jax.sharding import PartitionSpec as P

KVH = 8
BLOCK = 128
SCALE = 128 ** (-0.5) * 1.4426950408889634
NEG = -(2.0**100)
F32 = jnp.float32
BF16 = jnp.bfloat16
XC_GROUPS = [[y * 8 + k for k in range(8)] for y in range(4)]
NT = (((1,), (1,)), ((), ()))
VMEM = pl.BlockSpec(memory_space=pltpu.VMEM)
ANY = pl.BlockSpec(memory_space=pl.ANY)
HBM = pl.BlockSpec(memory_space=pltpu.HBM)
PARAMS = pltpu.CompilerParams(vmem_limit_bytes=32 * 1024 * 1024)


def four_lanes(lane, tiles):
    low = jnp.where(lane < 32, tiles[0], tiles[1])
    high = jnp.where(lane < 96, tiles[2], tiles[3])
    return jnp.where(lane < 64, low, high)


def attend_kernel(
    q_hbm, k_hbm, v_hbm, ids_hbm, tk_hbm, tv_hbm, anc_hbm,
    send_hbm, tree_hbm,
    q_ref, k_ref, v_ref, ids_ref, tk_ref, tv_ref, anc_ref,
    send_ref, tree_ref, acc_ref, stat_ref, sems, out_sems,
):
    moves = [
        (k_hbm.at[0], k_ref.at[0]),
        (q_hbm, q_ref),
        (ids_hbm, ids_ref),
        (v_hbm.at[0], v_ref.at[0]),
        (tk_hbm, tk_ref),
        (tv_hbm, tv_ref),
        (anc_hbm, anc_ref),
        (k_hbm.at[1], k_ref.at[1]),
        (v_hbm.at[1], v_ref.at[1]),
    ]
    moves = [pltpu.make_async_copy(a, b, sems.at[i]) for i, (a, b) in enumerate(moves)]
    for move in moves:
        move.start()
    seq = lax.axis_index("seq")
    head = lax.axis_index("head")
    lane = lax.broadcasted_iota(jnp.int32, (8, 128), 1)
    part = (lane % 32) // 8
    leaving = []

    def leave(source, target):
        copy = pltpu.make_async_copy(source, target, out_sems.at[len(leaving)])
        copy.start()
        leaving.append(copy)

    def tree_part():
        y, x, core = seq // 8, (seq % 8) // 2, seq % 2
        own, gp = x // 2, (x % 2) * 2 + core
        allowed = anc_ref[head // 4] > 0
        allowed = jnp.concatenate([allowed, allowed], axis=0)
        for a in range(2):
            q = q_ref[a, own, pl.ds(gp * 2, 2)].reshape(64, 128)
            t = lax.dot_general(q, tk_ref[a, own], NT, preferred_element_type=F32) * SCALE
            t = jnp.where(allowed, t, NEG)
            peak = jnp.max(t, axis=1, keepdims=True)
            w = jnp.where(allowed, jnp.exp2(t - peak), 0.0)
            total = jnp.sum(w, axis=1, keepdims=True)
            summed = jnp.dot(w.astype(BF16), tv_ref[a, own], preferred_element_type=F32)
            acc_ref[a] = summed.reshape(2, 32, 128)
            stat_ref[0, a] = jnp.broadcast_to(peak, (64, 128)).reshape(2, 32, 128)
            stat_ref[1, a] = jnp.broadcast_to(total, (64, 128)).reshape(2, 32, 128)
        start = pl.multiple_of(y * 8, 8)
        for a in range(2):
            for g2 in range(2):
                tree_ref[a * 2 + g2] = acc_ref[a, g2, pl.ds(start, 8), :]
        peak, total = (
            four_lanes(
                lane, [stat_ref[k, a, g2, pl.ds(start, 8), :] for a in range(2) for g2 in range(2)]
            )
            for k in range(2)
        )
        tree_ref[4] = peak
        tree_ref[5] = jnp.where(part == 2, total, 0.0)

    for move in moves[:4]:
        move.wait()
    for p in range(2):
        if p == 1:
            for move in moves[4:]:
                move.wait()
        keys = k_ref[p]
        ids = ids_ref[p : p + 1, :]
        bias = []
        for b in range(8):
            hit = jnp.max(jnp.where(ids == seq * 8 + b, 1.0, 0.0), axis=1, keepdims=True)
            bias.append(jnp.broadcast_to(jnp.where(hit > 0.5, 0.0, NEG), (1, BLOCK)))
        bias = jnp.concatenate(bias, axis=1)
        peaks, weights = [], []
        for a in range(2):
            q = q_ref[a, p].reshape(256, 128)
            t = lax.dot_general(q, keys, NT, preferred_element_type=F32) * SCALE
            if a == 0:
                t = t + bias
            peak = jnp.max(t, axis=1, keepdims=True).astype(BF16).astype(F32)
            weights.append(jnp.exp2(t - peak).astype(BF16))
            peaks.append(peak)
        values = jnp.concatenate([v_ref[p], jnp.ones((1024, 128), BF16)], axis=1)
        sums = [jnp.dot(w, values, preferred_element_type=F32) for w in weights]
        if p == 1:
            tree_part()
        for y in range(4):
            for gp in range(4):
                dest = y * 8 + p * 4 + gp
                rows = [(gp * 2 + g2) * 32 + y * 8 for g2 in range(2)]
                for a in range(2):
                    both = jnp.concatenate([sums[a][r : r + 8, :128] for r in rows], axis=0)
                    send_ref[dest, a * 16 : (a + 1) * 16, :] = both.astype(BF16)
                m = four_lanes(lane, [peaks[a][r : r + 8] for a in range(2) for r in rows])
                tot = four_lanes(lane, [sums[a][r : r + 8, 128:] for a in range(2) for r in rows])
                high = tot.astype(BF16).astype(F32)
                stat = jnp.where(part < 2, m, jnp.where(part == 2, high, tot - high))
                send_ref[dest, 32:40, :] = stat.astype(BF16)
            chunk = pl.ds(y * 8 + p * 4, 4)
            leave(send_ref.at[chunk], send_hbm.at[chunk])
    leave(tree_ref, tree_hbm)
    for copy in leaving:
        copy.wait()


def combine_kernel(got_ref, tree_ref, out_ref):
    def spread(tile, at):
        return jnp.broadcast_to(tile[:, at : at + 1], (8, 128))

    peak = tree_ref[4]
    for s in range(32):
        peak = jnp.maximum(peak, got_ref[s, 32:40, :].astype(F32))
    factor = jnp.exp2(tree_ref[4] - peak)
    total = pltpu.roll(factor, 16, 1) * tree_ref[5]
    summed = [spread(factor, k * 32) * tree_ref[k] for k in range(4)]
    for s in range(32):
        stat = got_ref[s, 32:40, :].astype(F32)
        factor = jnp.exp2(stat - peak)
        total = total + pltpu.roll(factor, 16, 1) * stat
        for a in range(2):
            part = got_ref[s, a * 16 : (a + 1) * 16, :].astype(F32)
            for g2 in range(2):
                k = a * 2 + g2
                summed[k] = summed[k] + spread(factor, k * 32) * part[g2 * 8 : (g2 + 1) * 8]
    done = [
        summed[k] / (spread(total, k * 32 + 16) + spread(total, k * 32 + 24)) for k in range(4)
    ]
    rows = jnp.concatenate([done[0], done[2], done[1], done[3]], axis=0).astype(BF16)
    for h in range(16):
        out_ref[h] = rows


def onward_kernel(one_ref, three_ref, low_ref, high_ref):
    low_ref[...] = one_ref[:128]
    high_ref[...] = three_ref[128:]


def project_kernel(x_ref, own_ref, one_ref, three_ref, low_ref, high_ref, out_ref, turn_ref):
    y = lax.axis_index("seq") // 8
    total = jnp.zeros((64, 512), F32)
    for k in range(4):
        j = (y + 4 - k) % 4
        left = [
            jnp.concatenate(
                [x_ref[r * 4 + j, g2 * 16 : (g2 + 1) * 16, :] for r in range(4)], axis=0
            )
            for g2 in range(2)
        ]
        right = (own_ref, one_ref, None, three_ref)[k]
        if right is None:
            right = jnp.concatenate([low_ref[...], high_ref[...]], axis=0)
        else:
            right = right[...]
        left = jnp.concatenate(left, axis=1)
        total = total + jnp.dot(left, right, preferred_element_type=F32)
    for r in range(4):
        for a in range(2):
            at = (r * 2 + a) * 8
            turn_ref[:, a * 4 + r, :] = total[at : at + 8]
    out_ref[...] = turn_ref[...].astype(BF16)


def add_kernel(got_ref, draft_ref, verify_ref):
    total = got_ref[0].astype(F32)
    for s in range(1, 8):
        total = total + got_ref[s].astype(F32)
    draft_ref[0] = total[:4].astype(BF16)
    verify_ref[0] = total[4:].astype(BF16)


def swap(array, axis, groups=None):
    return lax.all_to_all(array, axis, 0, 0, tiled=True, axis_index_groups=groups)


def attend(
    queries, cache_keys, cache_values, block_ids, tree_keys, tree_values, ancestors
):
    return pl.pallas_call(
        attend_kernel,
        out_shape=(
            jax.ShapeDtypeStruct((32, 40, 128), BF16),
            jax.ShapeDtypeStruct((6, 8, 128), F32),
        ),
        in_specs=[HBM] * 7,
        out_specs=(HBM, HBM),
        scratch_shapes=[
            pltpu.VMEM((2, 2, 8, 32, 128), BF16),
            pltpu.VMEM((2, 1024, 128), BF16),
            pltpu.VMEM((2, 1024, 128), BF16),
            pltpu.VMEM((2, 32), jnp.int32),
            pltpu.VMEM((2, 2, 32, 128), BF16),
            pltpu.VMEM((2, 2, 32, 128), BF16),
            pltpu.VMEM((4, 32, 32), jnp.int32),
            pltpu.VMEM((32, 40, 128), BF16),
            pltpu.VMEM((6, 8, 128), F32),
            pltpu.VMEM((2, 2, 32, 128), F32),
            pltpu.VMEM((2, 2, 2, 32, 128), F32),
            pltpu.SemaphoreType.DMA((9,)),
            pltpu.SemaphoreType.DMA((9,)),
        ],
        compiler_params=pltpu.CompilerParams(vmem_limit_bytes=55296 * 1024),
    )(queries, cache_keys, cache_values, block_ids, tree_keys, tree_values, ancestors)


def shift(array, k):
    return lax.ppermute(array, "seq", [(s, (s + 8 * k) % 32) for s in range(32)])


def local(
    queries, tree_keys, tree_values, cache_keys, cache_values, block_ids, ancestors, out_weight
):
    send, tree = attend(
        queries, cache_keys, cache_values, block_ids, tree_keys, tree_values, ancestors
    )
    got = swap(send, "seq")
    one, three = shift(out_weight, 1), shift(out_weight, 3)
    rows = pl.pallas_call(
        combine_kernel,
        out_shape=jax.ShapeDtypeStruct((16, 32, 128), BF16),
        in_specs=[VMEM, VMEM],
        out_specs=VMEM,
        compiler_params=PARAMS,
    )(got, tree)
    gathered = swap(rows, "head")
    low, high = pl.pallas_call(
        onward_kernel,
        out_shape=(jax.ShapeDtypeStruct((128, 512), BF16),) * 2,
        in_specs=[VMEM] * 2,
        out_specs=(VMEM, VMEM),
        cost_estimate=pl.CostEstimate(flops=10**10, bytes_accessed=0, transcendentals=0),
        compiler_params=PARAMS,
    )(one, three)
    low, high = shift(low, 1), shift(high, 3)
    parts = pl.pallas_call(
        project_kernel,
        out_shape=jax.ShapeDtypeStruct((8, 8, 512), BF16),
        in_specs=[VMEM] * 6,
        out_specs=VMEM,
        scratch_shapes=[pltpu.VMEM((8, 8, 512), F32)],
        compiler_params=PARAMS,
    )(gathered, out_weight, one, three, low, high)
    parts = swap(parts, "seq", XC_GROUPS)
    return pl.pallas_call(
        add_kernel,
        out_shape=(jax.ShapeDtypeStruct((1, 4, 512), BF16), jax.ShapeDtypeStruct((1, 4, 512), BF16)),
        in_specs=[VMEM],
        out_specs=(VMEM, VMEM),
        compiler_params=PARAMS,
    )(parts)


def solution(mesh):
    in_specs = (
        P(None, "head", None, None, None),
        P(None, "head", None, None),
        P(None, "head", None, None),
        P("head", "seq", None),
        P("head", "seq", None),
        P("head", None),
        P(),
        P("seq", "head"),
    )
    out_specs = (P("seq", None, "head"), P("seq", None, "head"))
    return jax.shard_map(local, mesh=mesh, in_specs=in_specs, out_specs=out_specs, check_vma=False)
```

```python
import jax
import jax.numpy as jnp
from jax import lax
from jax.experimental import pallas as pl
from jax.experimental.pallas import tpu as pltpu
from jax.sharding import PartitionSpec as P

KVH = 8
BLOCK = 128
SCALE = 128 ** (-0.5) * 1.4426950408889634
NEG = -(2.0**100)
F32 = jnp.float32
BF16 = jnp.bfloat16
Z_GROUPS = [[k // 2 + (k % 2) * 8 for k in range(16)]]
XC_GROUPS = [[y * 8 + k for k in range(8)] for y in range(4)]
NT = (((1,), (1,)), ((), ()))
VMEM = pl.BlockSpec(memory_space=pltpu.VMEM)
ANY = pl.BlockSpec(memory_space=pl.ANY)
HBM = pl.BlockSpec(memory_space=pltpu.HBM)
PARAMS = pltpu.CompilerParams(vmem_limit_bytes=32 * 1024 * 1024)


def four_lanes(lane, tiles):
    low = jnp.where(lane < 32, tiles[0], tiles[1])
    high = jnp.where(lane < 96, tiles[2], tiles[3])
    return jnp.where(lane < 64, low, high)


def attend_kernel(
    q_hbm, k_hbm, v_hbm, ids_hbm, tk_hbm, tv_hbm, anc_hbm,
    send_hbm, tree_hbm,
    q_ref, k_ref, v_ref, ids_ref, tk_ref, tv_ref, anc_ref,
    send_ref, tree_ref, acc_ref, stat_ref, sems, out_sems,
):
    moves = [
        (k_hbm.at[0], k_ref.at[0]),
        (q_hbm, q_ref),
        (ids_hbm, ids_ref),
        (v_hbm.at[0], v_ref.at[0]),
        (tk_hbm, tk_ref),
        (tv_hbm, tv_ref),
        (anc_hbm, anc_ref),
        (k_hbm.at[1], k_ref.at[1]),
        (v_hbm.at[1], v_ref.at[1]),
    ]
    moves = [pltpu.make_async_copy(a, b, sems.at[i]) for i, (a, b) in enumerate(moves)]
    for move in moves:
        move.start()
    seq = lax.axis_index("seq")
    head = lax.axis_index("head")
    lane = lax.broadcasted_iota(jnp.int32, (8, 128), 1)
    part = (lane % 32) // 8
    leaving = []

    def leave(source, target):
        copy = pltpu.make_async_copy(source, target, out_sems.at[len(leaving)])
        copy.start()
        leaving.append(copy)

    def tree_part():
        y, x, core = seq // 8, (seq % 8) // 2, seq % 2
        own, gp = x // 2, (x % 2) * 2 + core
        allowed = anc_ref[head // 4] > 0
        allowed = jnp.concatenate([allowed, allowed], axis=0)
        for a in range(2):
            q = q_ref[a, own, pl.ds(gp * 2, 2)].reshape(64, 128)
            t = lax.dot_general(q, tk_ref[a, own], NT, preferred_element_type=F32) * SCALE
            t = jnp.where(allowed, t, NEG)
            peak = jnp.max(t, axis=1, keepdims=True)
            w = jnp.where(allowed, jnp.exp2(t - peak), 0.0)
            total = jnp.sum(w, axis=1, keepdims=True)
            summed = jnp.dot(w.astype(BF16), tv_ref[a, own], preferred_element_type=F32)
            acc_ref[a] = summed.reshape(2, 32, 128)
            stat_ref[0, a] = jnp.broadcast_to(peak, (64, 128)).reshape(2, 32, 128)
            stat_ref[1, a] = jnp.broadcast_to(total, (64, 128)).reshape(2, 32, 128)
        start = pl.multiple_of(y * 8, 8)
        for a in range(2):
            for g2 in range(2):
                tree_ref[a * 2 + g2] = acc_ref[a, g2, pl.ds(start, 8), :]
        peak, total = (
            four_lanes(
                lane, [stat_ref[k, a, g2, pl.ds(start, 8), :] for a in range(2) for g2 in range(2)]
            )
            for k in range(2)
        )
        tree_ref[4] = peak
        tree_ref[5] = jnp.where(part == 2, total, 0.0)


    def scores(p):
        q = q_ref[:, p].reshape(512, 128)
        return lax.dot_general(q, k_ref[p], NT, preferred_element_type=F32)

    def softmax(raw, p):
        ids = ids_ref[p : p + 1, :]
        bias = []
        for b in range(8):
            hit = jnp.max(jnp.where(ids == seq * 8 + b, 1.0, 0.0), axis=1, keepdims=True)
            bias.append(jnp.broadcast_to(jnp.where(hit > 0.5, 0.0, NEG), (1, BLOCK)))
        bias = jnp.concatenate(bias, axis=1)
        peaks, weights = [], []
        for at in range(0, 512, 64):
            t = raw[at : at + 64] * SCALE
            if at < 256:
                t = t + bias
            peak = jnp.max(t, axis=1, keepdims=True).astype(BF16).astype(F32)
            peaks.append(peak)
            weights.append(jnp.exp2(t - peak).astype(BF16))
        return jnp.concatenate(peaks, axis=0), jnp.concatenate(weights, axis=0)

    def summed(w, p):
        values = jnp.concatenate([v_ref[p], jnp.ones((1024, 128), BF16)], axis=1)
        return jnp.dot(w, values, preferred_element_type=F32)

    for move in moves:
        move.wait()
    raw = [scores(0), scores(1)]
    for p in range(2):
        peaks, w = softmax(raw[p], p)
        sums = summed(w, p)
        peaks, sums = [peaks[:256], peaks[256:]], [sums[:256], sums[256:]]
        if p == 1:
            tree_part()
        for y in range(4):
            for gp in range(4):
                dest = y * 8 + p * 4 + gp
                rows = [(gp * 2 + g2) * 32 + y * 8 for g2 in range(2)]
                for a in range(2):
                    both = jnp.concatenate([sums[a][r : r + 8, :128] for r in rows], axis=0)
                    send_ref[dest, a * 16 : (a + 1) * 16, :] = both.astype(BF16)
                m = four_lanes(lane, [peaks[a][r : r + 8] for a in range(2) for r in rows])
                tot = four_lanes(lane, [sums[a][r : r + 8, 128:] for a in range(2) for r in rows])
                high = tot.astype(BF16).astype(F32)
                stat = jnp.where(part < 2, m, jnp.where(part == 2, high, tot - high))
                send_ref[dest, 32:40, :] = stat.astype(BF16)
            chunk = pl.ds(y * 8 + p * 4, 4)
            leave(send_ref.at[chunk], send_hbm.at[chunk])
    leave(tree_ref, tree_hbm)
    for copy in leaving:
        copy.wait()


def combine_kernel(got_ref, tree_ref, out_ref):
    def spread(tile, at):
        return jnp.broadcast_to(tile[:, at : at + 1], (8, 128))

    peak = tree_ref[4]
    for s in range(32):
        peak = jnp.maximum(peak, got_ref[s, 32:40, :].astype(F32))
    factor = jnp.exp2(tree_ref[4] - peak)
    total = pltpu.roll(factor, 16, 1) * tree_ref[5]
    summed = [spread(factor, k * 32) * tree_ref[k] for k in range(4)]
    for s in range(32):
        stat = got_ref[s, 32:40, :].astype(F32)
        factor = jnp.exp2(stat - peak)
        total = total + pltpu.roll(factor, 16, 1) * stat
        for a in range(2):
            part = got_ref[s, a * 16 : (a + 1) * 16, :].astype(F32)
            for g2 in range(2):
                k = a * 2 + g2
                summed[k] = summed[k] + spread(factor, k * 32) * part[g2 * 8 : (g2 + 1) * 8]
    done = [
        summed[k] / (spread(total, k * 32 + 16) + spread(total, k * 32 + 24)) for k in range(4)
    ]
    rows = jnp.concatenate([done[0], done[2], done[1], done[3]], axis=0).astype(BF16)
    for h in range(16):
        out_ref[h] = rows


def onward_kernel(one_ref, three_ref, low_ref, high_ref):
    low_ref[...] = one_ref[:128]
    high_ref[...] = three_ref[128:]


def project_kernel(x_ref, own_ref, one_ref, three_ref, low_ref, high_ref, out_ref, turn_ref):
    y = lax.axis_index("seq") // 8
    total = jnp.zeros((64, 512), F32)

    def place(r, j):
        return ((r % 2) * 4 + j) * 2 + r // 2

    for k in range(4):
        j = (y + 4 - k) % 4
        left = [
            jnp.concatenate(
                [x_ref[place(r, j), g2 * 16 : (g2 + 1) * 16, :] for r in range(4)], axis=0
            )
            for g2 in range(2)
        ]
        right = (own_ref, one_ref, None, three_ref)[k]
        if right is None:
            right = jnp.concatenate([low_ref[...], high_ref[...]], axis=0)
        else:
            right = right[...]
        left = jnp.concatenate(left, axis=1)
        total = total + jnp.dot(left, right, preferred_element_type=F32)
    for r in range(4):
        for a in range(2):
            at = (r * 2 + a) * 8
            turn_ref[:, a * 4 + r, :] = total[at : at + 8]
    out_ref[...] = turn_ref[...].astype(BF16)


def add_kernel(got_ref, draft_ref, verify_ref):
    total = got_ref[0].astype(F32)
    for s in range(1, 8):
        total = total + got_ref[s].astype(F32)
    draft_ref[0] = total[:4].astype(BF16)
    verify_ref[0] = total[4:].astype(BF16)


def swap(array, axis, groups=None):
    return lax.all_to_all(array, axis, 0, 0, tiled=True, axis_index_groups=groups)


def attend(
    queries, cache_keys, cache_values, block_ids, tree_keys, tree_values, ancestors
):
    return pl.pallas_call(
        attend_kernel,
        out_shape=(
            jax.ShapeDtypeStruct((32, 40, 128), BF16),
            jax.ShapeDtypeStruct((6, 8, 128), F32),
        ),
        in_specs=[HBM] * 7,
        out_specs=(HBM, HBM),
        scratch_shapes=[
            pltpu.VMEM((2, 2, 8, 32, 128), BF16),
            pltpu.VMEM((2, 1024, 128), BF16),
            pltpu.VMEM((2, 1024, 128), BF16),
            pltpu.VMEM((2, 32), jnp.int32),
            pltpu.VMEM((2, 2, 32, 128), BF16),
            pltpu.VMEM((2, 2, 32, 128), BF16),
            pltpu.VMEM((4, 32, 32), jnp.int32),
            pltpu.VMEM((32, 40, 128), BF16),
            pltpu.VMEM((6, 8, 128), F32),
            pltpu.VMEM((2, 2, 32, 128), F32),
            pltpu.VMEM((2, 2, 2, 32, 128), F32),
            pltpu.SemaphoreType.DMA((9,)),
            pltpu.SemaphoreType.DMA((9,)),
        ],
        compiler_params=pltpu.CompilerParams(vmem_limit_bytes=55296 * 1024),
    )(queries, cache_keys, cache_values, block_ids, tree_keys, tree_values, ancestors)


def shift(array, k):
    return lax.ppermute(array, "seq", [(s, (s + 8 * k) % 32) for s in range(32)])


def local(
    queries, tree_keys, tree_values, cache_keys, cache_values, block_ids, ancestors, out_weight
):
    send, tree = attend(
        queries, cache_keys, cache_values, block_ids, tree_keys, tree_values, ancestors
    )
    got = swap(send, "seq")
    one, three = shift(out_weight, 1), shift(out_weight, 3)
    rows = pl.pallas_call(
        combine_kernel,
        out_shape=jax.ShapeDtypeStruct((16, 32, 128), BF16),
        in_specs=[VMEM, VMEM],
        out_specs=VMEM,
        compiler_params=PARAMS,
    )(got, tree)
    gathered = swap(rows, "head", Z_GROUPS)
    low, high = pl.pallas_call(
        onward_kernel,
        out_shape=(jax.ShapeDtypeStruct((128, 512), BF16),) * 2,
        in_specs=[VMEM] * 2,
        out_specs=(VMEM, VMEM),
        cost_estimate=pl.CostEstimate(flops=10**10, bytes_accessed=0, transcendentals=0),
        compiler_params=PARAMS,
    )(one, three)
    low, high = shift(low, 1), shift(high, 3)
    parts = pl.pallas_call(
        project_kernel,
        out_shape=jax.ShapeDtypeStruct((8, 8, 512), BF16),
        in_specs=[VMEM] * 6,
        out_specs=VMEM,
        scratch_shapes=[pltpu.VMEM((8, 8, 512), F32)],
        compiler_params=PARAMS,
    )(gathered, out_weight, one, three, low, high)
    parts = swap(parts, "seq", XC_GROUPS)
    return pl.pallas_call(
        add_kernel,
        out_shape=(jax.ShapeDtypeStruct((1, 4, 512), BF16), jax.ShapeDtypeStruct((1, 4, 512), BF16)),
        in_specs=[VMEM],
        out_specs=(VMEM, VMEM),
        compiler_params=PARAMS,
    )(parts)


def solution(mesh):
    in_specs = (
        P(None, "head", None, None, None),
        P(None, "head", None, None),
        P(None, "head", None, None),
        P("head", "seq", None),
        P("head", "seq", None),
        P("head", None),
        P(),
        P("seq", "head"),
    )
    out_specs = (P("seq", None, "head"), P("seq", None, "head"))
    return jax.shard_map(local, mesh=mesh, in_specs=in_specs, out_specs=out_specs, check_vma=False)
```

```python
import jax
import jax.numpy as jnp
from jax import lax
from jax.experimental import pallas as pl
from jax.experimental.pallas import tpu as pltpu
from jax.sharding import PartitionSpec as P

KVH = 8
BLOCK = 128
SCALE = 128 ** (-0.5) * 1.4426950408889634
NEG = -(2.0**100)
F32 = jnp.float32
BF16 = jnp.bfloat16
Z_GROUPS = [[0, 1, 15, 2, 14, 3, 13, 4, 12, 5, 11, 6, 10, 7, 9, 8]]
XC_GROUPS = [[y * 8 + k for k in range(8)] for y in range(4)]
NT = (((1,), (1,)), ((), ()))
VMEM = pl.BlockSpec(memory_space=pltpu.VMEM)
ANY = pl.BlockSpec(memory_space=pl.ANY)
HBM = pl.BlockSpec(memory_space=pltpu.HBM)
PARAMS = pltpu.CompilerParams(vmem_limit_bytes=32 * 1024 * 1024)


def four_lanes(lane, tiles):
    low = jnp.where(lane < 32, tiles[0], tiles[1])
    high = jnp.where(lane < 96, tiles[2], tiles[3])
    return jnp.where(lane < 64, low, high)


def attend_kernel(
    q_hbm, k_hbm, v_hbm, ids_hbm, tk_hbm, tv_hbm, anc_hbm,
    send_hbm, tree_hbm,
    q_ref, k_ref, v_ref, ids_ref, tk_ref, tv_ref, anc_ref,
    send_ref, tree_ref, acc_ref, stat_ref, sems, out_sems,
):
    moves = [
        (k_hbm.at[0], k_ref.at[0]),
        (q_hbm, q_ref),
        (ids_hbm, ids_ref),
        (v_hbm.at[0], v_ref.at[0]),
        (tk_hbm, tk_ref),
        (tv_hbm, tv_ref),
        (anc_hbm, anc_ref),
        (k_hbm.at[1], k_ref.at[1]),
        (v_hbm.at[1], v_ref.at[1]),
    ]
    moves = [pltpu.make_async_copy(a, b, sems.at[i]) for i, (a, b) in enumerate(moves)]
    for move in moves:
        move.start()
    seq = lax.axis_index("seq")
    head = lax.axis_index("head")
    lane = lax.broadcasted_iota(jnp.int32, (8, 128), 1)
    part = (lane % 32) // 8
    leaving = []

    def leave(source, target):
        copy = pltpu.make_async_copy(source, target, out_sems.at[len(leaving)])
        copy.start()
        leaving.append(copy)

    def tree_part():
        y, x, core = seq // 8, (seq % 8) // 2, seq % 2
        own, gp = x // 2, (x % 2) * 2 + core
        allowed = anc_ref[head // 4] > 0
        allowed = jnp.concatenate([allowed, allowed], axis=0)
        for a in range(2):
            q = q_ref[a, own, pl.ds(gp * 2, 2)].reshape(64, 128)
            t = lax.dot_general(q, tk_ref[a, own], NT, preferred_element_type=F32) * SCALE
            t = jnp.where(allowed, t, NEG)
            peak = jnp.max(t, axis=1, keepdims=True)
            w = jnp.where(allowed, jnp.exp2(t - peak), 0.0)
            total = jnp.sum(w, axis=1, keepdims=True)
            summed = jnp.dot(w.astype(BF16), tv_ref[a, own], preferred_element_type=F32)
            acc_ref[a] = summed.reshape(2, 32, 128)
            stat_ref[0, a] = jnp.broadcast_to(peak, (64, 128)).reshape(2, 32, 128)
            stat_ref[1, a] = jnp.broadcast_to(total, (64, 128)).reshape(2, 32, 128)
        start = pl.multiple_of(y * 8, 8)
        for a in range(2):
            for g2 in range(2):
                tree_ref[a * 2 + g2] = acc_ref[a, g2, pl.ds(start, 8), :]
        peak, total = (
            four_lanes(
                lane, [stat_ref[k, a, g2, pl.ds(start, 8), :] for a in range(2) for g2 in range(2)]
            )
            for k in range(2)
        )
        tree_ref[4] = peak
        tree_ref[5] = jnp.where(part == 2, total, 0.0)


    def scores(p):
        q = q_ref[:, p].reshape(512, 128)
        return lax.dot_general(q, k_ref[p], NT, preferred_element_type=F32)

    def softmax(raw, p):
        ids = ids_ref[p : p + 1, :]
        bias = []
        for b in range(8):
            hit = jnp.max(jnp.where(ids == seq * 8 + b, 1.0, 0.0), axis=1, keepdims=True)
            bias.append(jnp.broadcast_to(jnp.where(hit > 0.5, 0.0, NEG), (1, BLOCK)))
        bias = jnp.concatenate(bias, axis=1)
        peaks, weights = [], []
        for at in range(0, 512, 64):
            t = raw[at : at + 64] * SCALE
            if at < 256:
                t = t + bias
            peak = jnp.max(t, axis=1, keepdims=True).astype(BF16).astype(F32)
            peaks.append(peak)
            weights.append(jnp.exp2(t - peak).astype(BF16))
        return jnp.concatenate(peaks, axis=0), jnp.concatenate(weights, axis=0)

    def summed(w, p):
        values = jnp.concatenate([v_ref[p], jnp.ones((1024, 128), BF16)], axis=1)
        return jnp.dot(w, values, preferred_element_type=F32)

    for move in moves:
        move.wait()
    raw = [scores(0), scores(1)]
    for p in range(2):
        peaks, w = softmax(raw[p], p)
        sums = summed(w, p)
        peaks, sums = [peaks[:256], peaks[256:]], [sums[:256], sums[256:]]
        if p == 1:
            tree_part()
        for y in range(4):
            for gp in range(4):
                dest = y * 8 + p * 4 + gp
                rows = [(gp * 2 + g2) * 32 + y * 8 for g2 in range(2)]
                for a in range(2):
                    both = jnp.concatenate([sums[a][r : r + 8, :128] for r in rows], axis=0)
                    send_ref[dest, a * 16 : (a + 1) * 16, :] = both.astype(BF16)
                m = four_lanes(lane, [peaks[a][r : r + 8] for a in range(2) for r in rows])
                tot = four_lanes(lane, [sums[a][r : r + 8, 128:] for a in range(2) for r in rows])
                high = tot.astype(BF16).astype(F32)
                stat = jnp.where(part < 2, m, jnp.where(part == 2, high, tot - high))
                send_ref[dest, 32:40, :] = stat.astype(BF16)
            chunk = pl.ds(y * 8 + p * 4, 4)
            leave(send_ref.at[chunk], send_hbm.at[chunk])
    leave(tree_ref, tree_hbm)
    for copy in leaving:
        copy.wait()


def combine_kernel(got_ref, tree_ref, out_ref):
    def spread(tile, at):
        return jnp.broadcast_to(tile[:, at : at + 1], (8, 128))

    peak = tree_ref[4]
    for s in range(32):
        peak = jnp.maximum(peak, got_ref[s, 32:40, :].astype(F32))
    factor = jnp.exp2(tree_ref[4] - peak)
    total = pltpu.roll(factor, 16, 1) * tree_ref[5]
    summed = [spread(factor, k * 32) * tree_ref[k] for k in range(4)]
    for s in range(32):
        stat = got_ref[s, 32:40, :].astype(F32)
        factor = jnp.exp2(stat - peak)
        total = total + pltpu.roll(factor, 16, 1) * stat
        for a in range(2):
            part = got_ref[s, a * 16 : (a + 1) * 16, :].astype(F32)
            for g2 in range(2):
                k = a * 2 + g2
                summed[k] = summed[k] + spread(factor, k * 32) * part[g2 * 8 : (g2 + 1) * 8]
    done = [
        summed[k] / (spread(total, k * 32 + 16) + spread(total, k * 32 + 24)) for k in range(4)
    ]
    rows = jnp.concatenate([done[0], done[2], done[1], done[3]], axis=0).astype(BF16)
    for h in range(16):
        out_ref[h] = rows


def onward_kernel(one_ref, three_ref, low_ref, high_ref):
    low_ref[...] = one_ref[:128]
    high_ref[...] = three_ref[128:]


def project_kernel(x_ref, own_ref, one_ref, three_ref, low_ref, high_ref, out_ref, turn_ref):
    y = lax.axis_index("seq") // 8
    total = jnp.zeros((64, 512), F32)

    def place(r, j):
        h = r * 4 + j
        return jnp.where(h > 8, 32 - 2 * h, jnp.maximum(2 * h - 1, 0))

    for k in range(4):
        j = (y + 4 - k) % 4
        left = [
            jnp.concatenate(
                [x_ref[place(r, j), g2 * 16 : (g2 + 1) * 16, :] for r in range(4)], axis=0
            )
            for g2 in range(2)
        ]
        right = (own_ref, one_ref, None, three_ref)[k]
        if right is None:
            right = jnp.concatenate([low_ref[...], high_ref[...]], axis=0)
        else:
            right = right[...]
        left = jnp.concatenate(left, axis=1)
        total = total + jnp.dot(left, right, preferred_element_type=F32)
    for r in range(4):
        for a in range(2):
            at = (r * 2 + a) * 8
            turn_ref[:, a * 4 + r, :] = total[at : at + 8]
    out_ref[...] = turn_ref[...].astype(BF16)


def add_kernel(got_ref, draft_ref, verify_ref):
    total = got_ref[0].astype(F32)
    for s in range(1, 8):
        total = total + got_ref[s].astype(F32)
    draft_ref[0] = total[:4].astype(BF16)
    verify_ref[0] = total[4:].astype(BF16)


def swap(array, axis, groups=None):
    return lax.all_to_all(array, axis, 0, 0, tiled=True, axis_index_groups=groups)


def attend(
    queries, cache_keys, cache_values, block_ids, tree_keys, tree_values, ancestors
):
    return pl.pallas_call(
        attend_kernel,
        out_shape=(
            jax.ShapeDtypeStruct((32, 40, 128), BF16),
            jax.ShapeDtypeStruct((6, 8, 128), F32),
        ),
        in_specs=[HBM] * 7,
        out_specs=(HBM, HBM),
        scratch_shapes=[
            pltpu.VMEM((2, 2, 8, 32, 128), BF16),
            pltpu.VMEM((2, 1024, 128), BF16),
            pltpu.VMEM((2, 1024, 128), BF16),
            pltpu.VMEM((2, 32), jnp.int32),
            pltpu.VMEM((2, 2, 32, 128), BF16),
            pltpu.VMEM((2, 2, 32, 128), BF16),
            pltpu.VMEM((4, 32, 32), jnp.int32),
            pltpu.VMEM((32, 40, 128), BF16),
            pltpu.VMEM((6, 8, 128), F32),
            pltpu.VMEM((2, 2, 32, 128), F32),
            pltpu.VMEM((2, 2, 2, 32, 128), F32),
            pltpu.SemaphoreType.DMA((9,)),
            pltpu.SemaphoreType.DMA((9,)),
        ],
        compiler_params=pltpu.CompilerParams(vmem_limit_bytes=55296 * 1024),
    )(queries, cache_keys, cache_values, block_ids, tree_keys, tree_values, ancestors)


def shift(array, k):
    return lax.ppermute(array, "seq", [(s, (s + 8 * k) % 32) for s in range(32)])


def local(
    queries, tree_keys, tree_values, cache_keys, cache_values, block_ids, ancestors, out_weight
):
    send, tree = attend(
        queries, cache_keys, cache_values, block_ids, tree_keys, tree_values, ancestors
    )
    got = swap(send, "seq")
    one, three = shift(out_weight, 1), shift(out_weight, 3)
    rows = pl.pallas_call(
        combine_kernel,
        out_shape=jax.ShapeDtypeStruct((16, 32, 128), BF16),
        in_specs=[VMEM, VMEM],
        out_specs=VMEM,
        compiler_params=PARAMS,
    )(got, tree)
    gathered = swap(rows, "head", Z_GROUPS)
    low, high = pl.pallas_call(
        onward_kernel,
        out_shape=(jax.ShapeDtypeStruct((128, 512), BF16),) * 2,
        in_specs=[VMEM] * 2,
        out_specs=(VMEM, VMEM),
        cost_estimate=pl.CostEstimate(flops=10**10, bytes_accessed=0, transcendentals=0),
        compiler_params=PARAMS,
    )(one, three)
    low, high = shift(low, 1), shift(high, 3)
    parts = pl.pallas_call(
        project_kernel,
        out_shape=jax.ShapeDtypeStruct((8, 8, 512), BF16),
        in_specs=[VMEM] * 6,
        out_specs=VMEM,
        scratch_shapes=[pltpu.VMEM((8, 8, 512), F32)],
        compiler_params=PARAMS,
    )(gathered, out_weight, one, three, low, high)
    parts = swap(parts, "seq", XC_GROUPS)
    return pl.pallas_call(
        add_kernel,
        out_shape=(jax.ShapeDtypeStruct((1, 4, 512), BF16), jax.ShapeDtypeStruct((1, 4, 512), BF16)),
        in_specs=[VMEM],
        out_specs=(VMEM, VMEM),
        compiler_params=PARAMS,
    )(parts)


def solution(mesh):
    in_specs = (
        P(None, "head", None, None, None),
        P(None, "head", None, None),
        P(None, "head", None, None),
        P("head", "seq", None),
        P("head", "seq", None),
        P("head", None),
        P(),
        P("seq", "head"),
    )
    out_specs = (P("seq", None, "head"), P("seq", None, "head"))
    return jax.shard_map(local, mesh=mesh, in_specs=in_specs, out_specs=out_specs, check_vma=False)
```

```python
import jax
import jax.numpy as jnp
from jax import lax
from jax.experimental import pallas as pl
from jax.experimental.pallas import tpu as pltpu
from jax.sharding import PartitionSpec as P

KVH = 8
BLOCK = 128
SCALE = 128 ** (-0.5) * 1.4426950408889634
NEG = -(2.0**100)
F32 = jnp.float32
BF16 = jnp.bfloat16
Z_GROUPS = [[s * 16 + (7 + s % 2 * 2) * k % 16 for k in range(16)] for s in range(32)]
XC_GROUPS = [[y * 8 + k for k in range(8)] for y in range(4)]
NT = (((1,), (1,)), ((), ()))
VMEM = pl.BlockSpec(memory_space=pltpu.VMEM)
ANY = pl.BlockSpec(memory_space=pl.ANY)
HBM = pl.BlockSpec(memory_space=pltpu.HBM)
PARAMS = pltpu.CompilerParams(vmem_limit_bytes=32 * 1024 * 1024)


def four_lanes(lane, tiles):
    low = jnp.where(lane < 32, tiles[0], tiles[1])
    high = jnp.where(lane < 96, tiles[2], tiles[3])
    return jnp.where(lane < 64, low, high)


def attend_kernel(
    q_hbm, k_hbm, v_hbm, ids_hbm, tk_hbm, tv_hbm, anc_hbm,
    send_hbm, tree_hbm,
    q_ref, k_ref, v_ref, ids_ref, tk_ref, tv_ref, anc_ref,
    send_ref, tree_ref, acc_ref, stat_ref, sems, out_sems,
):
    moves = [
        (k_hbm.at[0], k_ref.at[0]),
        (q_hbm, q_ref),
        (ids_hbm, ids_ref),
        (v_hbm.at[0], v_ref.at[0]),
        (tk_hbm, tk_ref),
        (tv_hbm, tv_ref),
        (anc_hbm, anc_ref),
        (k_hbm.at[1], k_ref.at[1]),
        (v_hbm.at[1], v_ref.at[1]),
    ]
    moves = [pltpu.make_async_copy(a, b, sems.at[i]) for i, (a, b) in enumerate(moves)]
    for move in moves:
        move.start()
    seq = lax.axis_index("seq")
    head = lax.axis_index("head")
    lane = lax.broadcasted_iota(jnp.int32, (8, 128), 1)
    part = (lane % 32) // 8
    leaving = []

    def leave(source, target):
        copy = pltpu.make_async_copy(source, target, out_sems.at[len(leaving)])
        copy.start()
        leaving.append(copy)

    def tree_part():
        y, x, core = seq // 8, (seq % 8) // 2, seq % 2
        own, gp = x // 2, (x % 2) * 2 + core
        allowed = anc_ref[head // 4] > 0
        allowed = jnp.concatenate([allowed, allowed], axis=0)
        for a in range(2):
            q = q_ref[a, own, pl.ds(gp * 2, 2)].reshape(64, 128)
            t = lax.dot_general(q, tk_ref[a, own], NT, preferred_element_type=F32) * SCALE
            t = jnp.where(allowed, t, NEG)
            peak = jnp.max(t, axis=1, keepdims=True)
            w = jnp.where(allowed, jnp.exp2(t - peak), 0.0)
            total = jnp.sum(w, axis=1, keepdims=True)
            summed = jnp.dot(w.astype(BF16), tv_ref[a, own], preferred_element_type=F32)
            acc_ref[a] = summed.reshape(2, 32, 128)
            stat_ref[0, a] = jnp.broadcast_to(peak, (64, 128)).reshape(2, 32, 128)
            stat_ref[1, a] = jnp.broadcast_to(total, (64, 128)).reshape(2, 32, 128)
        start = pl.multiple_of(y * 8, 8)
        for a in range(2):
            for g2 in range(2):
                tree_ref[a * 2 + g2] = acc_ref[a, g2, pl.ds(start, 8), :]
        peak, total = (
            four_lanes(
                lane, [stat_ref[k, a, g2, pl.ds(start, 8), :] for a in range(2) for g2 in range(2)]
            )
            for k in range(2)
        )
        tree_ref[4] = peak
        tree_ref[5] = jnp.where(part == 2, total, 0.0)


    def scores(p):
        q = q_ref[:, p].reshape(512, 128)
        return lax.dot_general(q, k_ref[p], NT, preferred_element_type=F32)

    def softmax(raw, p):
        ids = ids_ref[p : p + 1, :]
        bias = []
        for b in range(8):
            hit = jnp.max(jnp.where(ids == seq * 8 + b, 1.0, 0.0), axis=1, keepdims=True)
            bias.append(jnp.broadcast_to(jnp.where(hit > 0.5, 0.0, NEG), (1, BLOCK)))
        bias = jnp.concatenate(bias, axis=1)
        peaks, weights = [], []
        for at in range(0, 512, 64):
            t = raw[at : at + 64] * SCALE
            if at < 256:
                t = t + bias
            peak = jnp.max(t, axis=1, keepdims=True).astype(BF16).astype(F32)
            peaks.append(peak)
            weights.append(jnp.exp2(t - peak).astype(BF16))
        return jnp.concatenate(peaks, axis=0), jnp.concatenate(weights, axis=0)

    def summed(w, p):
        values = jnp.concatenate([v_ref[p], jnp.ones((1024, 128), BF16)], axis=1)
        return jnp.dot(w, values, preferred_element_type=F32)

    for move in moves:
        move.wait()
    raw = [scores(0), scores(1)]
    for p in range(2):
        peaks, w = softmax(raw[p], p)
        sums = summed(w, p)
        peaks, sums = [peaks[:256], peaks[256:]], [sums[:256], sums[256:]]
        if p == 1:
            tree_part()
        for y in range(4):
            for gp in range(4):
                dest = y * 8 + p * 4 + gp
                rows = [(gp * 2 + g2) * 32 + y * 8 for g2 in range(2)]
                for a in range(2):
                    both = jnp.concatenate([sums[a][r : r + 8, :128] for r in rows], axis=0)
                    send_ref[dest, a * 16 : (a + 1) * 16, :] = both.astype(BF16)
                m = four_lanes(lane, [peaks[a][r : r + 8] for a in range(2) for r in rows])
                tot = four_lanes(lane, [sums[a][r : r + 8, 128:] for a in range(2) for r in rows])
                high = tot.astype(BF16).astype(F32)
                stat = jnp.where(part < 2, m, jnp.where(part == 2, high, tot - high))
                send_ref[dest, 32:40, :] = stat.astype(BF16)
            chunk = pl.ds(y * 8 + p * 4, 4)
            leave(send_ref.at[chunk], send_hbm.at[chunk])
    leave(tree_ref, tree_hbm)
    for copy in leaving:
        copy.wait()


def combine_kernel(got_ref, tree_ref, out_ref):
    def spread(tile, at):
        return jnp.broadcast_to(tile[:, at : at + 1], (8, 128))

    peak = tree_ref[4]
    for s in range(32):
        peak = jnp.maximum(peak, got_ref[s, 32:40, :].astype(F32))
    factor = jnp.exp2(tree_ref[4] - peak)
    total = pltpu.roll(factor, 16, 1) * tree_ref[5]
    summed = [spread(factor, k * 32) * tree_ref[k] for k in range(4)]
    for s in range(32):
        stat = got_ref[s, 32:40, :].astype(F32)
        factor = jnp.exp2(stat - peak)
        total = total + pltpu.roll(factor, 16, 1) * stat
        for a in range(2):
            part = got_ref[s, a * 16 : (a + 1) * 16, :].astype(F32)
            for g2 in range(2):
                k = a * 2 + g2
                summed[k] = summed[k] + spread(factor, k * 32) * part[g2 * 8 : (g2 + 1) * 8]
    done = [
        summed[k] / (spread(total, k * 32 + 16) + spread(total, k * 32 + 24)) for k in range(4)
    ]
    rows = jnp.concatenate([done[0], done[2], done[1], done[3]], axis=0).astype(BF16)
    for h in range(16):
        out_ref[h] = rows


def onward_kernel(one_ref, three_ref, low_ref, high_ref):
    low_ref[...] = one_ref[:128]
    high_ref[...] = three_ref[128:]


def project_kernel(x_ref, own_ref, one_ref, three_ref, low_ref, high_ref, out_ref, turn_ref):
    seq = lax.axis_index("seq")
    y = seq // 8
    total = jnp.zeros((64, 512), F32)

    def place(r, j):
        return (7 + seq % 2 * 2) * (r * 4 + j) % 16

    for k in range(4):
        j = (y + 4 - k) % 4
        left = [
            jnp.concatenate(
                [x_ref[place(r, j), g2 * 16 : (g2 + 1) * 16, :] for r in range(4)], axis=0
            )
            for g2 in range(2)
        ]
        right = (own_ref, one_ref, None, three_ref)[k]
        if right is None:
            right = jnp.concatenate([low_ref[...], high_ref[...]], axis=0)
        else:
            right = right[...]
        left = jnp.concatenate(left, axis=1)
        total = total + jnp.dot(left, right, preferred_element_type=F32)
    for r in range(4):
        for a in range(2):
            at = (r * 2 + a) * 8
            turn_ref[:, a * 4 + r, :] = total[at : at + 8]
    out_ref[...] = turn_ref[...].astype(BF16)


def add_kernel(got_ref, draft_ref, verify_ref):
    total = got_ref[0].astype(F32)
    for s in range(1, 8):
        total = total + got_ref[s].astype(F32)
    draft_ref[0] = total[:4].astype(BF16)
    verify_ref[0] = total[4:].astype(BF16)


def swap(array, axis, groups=None):
    return lax.all_to_all(array, axis, 0, 0, tiled=True, axis_index_groups=groups)


def attend(
    queries, cache_keys, cache_values, block_ids, tree_keys, tree_values, ancestors
):
    return pl.pallas_call(
        attend_kernel,
        out_shape=(
            jax.ShapeDtypeStruct((32, 40, 128), BF16),
            jax.ShapeDtypeStruct((6, 8, 128), F32),
        ),
        in_specs=[HBM] * 7,
        out_specs=(HBM, HBM),
        scratch_shapes=[
            pltpu.VMEM((2, 2, 8, 32, 128), BF16),
            pltpu.VMEM((2, 1024, 128), BF16),
            pltpu.VMEM((2, 1024, 128), BF16),
            pltpu.VMEM((2, 32), jnp.int32),
            pltpu.VMEM((2, 2, 32, 128), BF16),
            pltpu.VMEM((2, 2, 32, 128), BF16),
            pltpu.VMEM((4, 32, 32), jnp.int32),
            pltpu.VMEM((32, 40, 128), BF16),
            pltpu.VMEM((6, 8, 128), F32),
            pltpu.VMEM((2, 2, 32, 128), F32),
            pltpu.VMEM((2, 2, 2, 32, 128), F32),
            pltpu.SemaphoreType.DMA((9,)),
            pltpu.SemaphoreType.DMA((9,)),
        ],
        compiler_params=pltpu.CompilerParams(vmem_limit_bytes=55296 * 1024),
    )(queries, cache_keys, cache_values, block_ids, tree_keys, tree_values, ancestors)


def shift(array, k):
    return lax.ppermute(array, "seq", [(s, (s + 8 * k) % 32) for s in range(32)])


def local(
    queries, tree_keys, tree_values, cache_keys, cache_values, block_ids, ancestors, out_weight
):
    send, tree = attend(
        queries, cache_keys, cache_values, block_ids, tree_keys, tree_values, ancestors
    )
    got = swap(send, "seq")
    one, three = shift(out_weight, 1), shift(out_weight, 3)
    rows = pl.pallas_call(
        combine_kernel,
        out_shape=jax.ShapeDtypeStruct((16, 32, 128), BF16),
        in_specs=[VMEM, VMEM],
        out_specs=VMEM,
        compiler_params=PARAMS,
    )(got, tree)
    gathered = swap(rows, ("seq", "head"), Z_GROUPS)
    low, high = pl.pallas_call(
        onward_kernel,
        out_shape=(jax.ShapeDtypeStruct((128, 512), BF16),) * 2,
        in_specs=[VMEM] * 2,
        out_specs=(VMEM, VMEM),
        cost_estimate=pl.CostEstimate(flops=10**10, bytes_accessed=0, transcendentals=0),
        compiler_params=PARAMS,
    )(one, three)
    low, high = shift(low, 1), shift(high, 3)
    parts = pl.pallas_call(
        project_kernel,
        out_shape=jax.ShapeDtypeStruct((8, 8, 512), BF16),
        in_specs=[VMEM] * 6,
        out_specs=VMEM,
        scratch_shapes=[pltpu.VMEM((8, 8, 512), F32)],
        compiler_params=PARAMS,
    )(gathered, out_weight, one, three, low, high)
    parts = swap(parts, "seq", XC_GROUPS)
    return pl.pallas_call(
        add_kernel,
        out_shape=(jax.ShapeDtypeStruct((1, 4, 512), BF16), jax.ShapeDtypeStruct((1, 4, 512), BF16)),
        in_specs=[VMEM],
        out_specs=(VMEM, VMEM),
        compiler_params=PARAMS,
    )(parts)


def solution(mesh):
    in_specs = (
        P(None, "head", None, None, None),
        P(None, "head", None, None),
        P(None, "head", None, None),
        P("head", "seq", None),
        P("head", "seq", None),
        P("head", None),
        P(),
        P("seq", "head"),
    )
    out_specs = (P("seq", None, "head"), P("seq", None, "head"))
    return jax.shard_map(local, mesh=mesh, in_specs=in_specs, out_specs=out_specs, check_vma=False)
```

```python
import jax
import jax.numpy as jnp
from jax import lax
from jax.experimental import pallas as pl
from jax.experimental.pallas import tpu as pltpu
from jax.sharding import PartitionSpec as P

KVH = 8
BLOCK = 128
SCALE = 128 ** (-0.5) * 1.4426950408889634
NEG = -(2.0**100)
F32 = jnp.float32
BF16 = jnp.bfloat16
Z_GROUPS = [[s * 16 + (1 + s % 2 * 14) * k % 16 for k in range(16)] for s in range(32)]
XC_GROUPS = [[y * 8 + k for k in range(8)] for y in range(4)]
NT = (((1,), (1,)), ((), ()))
VMEM = pl.BlockSpec(memory_space=pltpu.VMEM)
ANY = pl.BlockSpec(memory_space=pl.ANY)
HBM = pl.BlockSpec(memory_space=pltpu.HBM)
PARAMS = pltpu.CompilerParams(vmem_limit_bytes=32 * 1024 * 1024)


def four_lanes(lane, tiles):
    low = jnp.where(lane < 32, tiles[0], tiles[1])
    high = jnp.where(lane < 96, tiles[2], tiles[3])
    return jnp.where(lane < 64, low, high)


def attend_kernel(
    q_hbm, k_hbm, v_hbm, ids_hbm, tk_hbm, tv_hbm, anc_hbm,
    send_hbm, tree_hbm,
    q_ref, k_ref, v_ref, ids_ref, tk_ref, tv_ref, anc_ref,
    send_ref, tree_ref, acc_ref, stat_ref, sems, out_sems,
):
    moves = [
        (k_hbm.at[0], k_ref.at[0]),
        (q_hbm, q_ref),
        (ids_hbm, ids_ref),
        (v_hbm.at[0], v_ref.at[0]),
        (tk_hbm, tk_ref),
        (tv_hbm, tv_ref),
        (anc_hbm, anc_ref),
        (k_hbm.at[1], k_ref.at[1]),
        (v_hbm.at[1], v_ref.at[1]),
    ]
    moves = [pltpu.make_async_copy(a, b, sems.at[i]) for i, (a, b) in enumerate(moves)]
    for move in moves:
        move.start()
    seq = lax.axis_index("seq")
    head = lax.axis_index("head")
    lane = lax.broadcasted_iota(jnp.int32, (8, 128), 1)
    part = (lane % 32) // 8
    leaving = []

    def leave(source, target):
        copy = pltpu.make_async_copy(source, target, out_sems.at[len(leaving)])
        copy.start()
        leaving.append(copy)

    def tree_part():
        y, x, core = seq // 8, (seq % 8) // 2, seq % 2
        own, gp = x // 2, (x % 2) * 2 + core
        allowed = anc_ref[head // 4] > 0
        allowed = jnp.concatenate([allowed, allowed], axis=0)
        for a in range(2):
            q = q_ref[a, own, pl.ds(gp * 2, 2)].reshape(64, 128)
            t = lax.dot_general(q, tk_ref[a, own], NT, preferred_element_type=F32) * SCALE
            t = jnp.where(allowed, t, NEG)
            peak = jnp.max(t, axis=1, keepdims=True)
            w = jnp.where(allowed, jnp.exp2(t - peak), 0.0)
            total = jnp.sum(w, axis=1, keepdims=True)
            summed = jnp.dot(w.astype(BF16), tv_ref[a, own], preferred_element_type=F32)
            acc_ref[a] = summed.reshape(2, 32, 128)
            stat_ref[0, a] = jnp.broadcast_to(peak, (64, 128)).reshape(2, 32, 128)
            stat_ref[1, a] = jnp.broadcast_to(total, (64, 128)).reshape(2, 32, 128)
        start = pl.multiple_of(y * 8, 8)
        for a in range(2):
            for g2 in range(2):
                tree_ref[a * 2 + g2] = acc_ref[a, g2, pl.ds(start, 8), :]
        peak, total = (
            four_lanes(
                lane, [stat_ref[k, a, g2, pl.ds(start, 8), :] for a in range(2) for g2 in range(2)]
            )
            for k in range(2)
        )
        tree_ref[4] = peak
        tree_ref[5] = jnp.where(part == 2, total, 0.0)


    def scores(p):
        q = q_ref[:, p].reshape(512, 128)
        return lax.dot_general(q, k_ref[p], NT, preferred_element_type=F32)

    def softmax(raw, p):
        ids = ids_ref[p : p + 1, :]
        bias = []
        for b in range(8):
            hit = jnp.max(jnp.where(ids == seq * 8 + b, 1.0, 0.0), axis=1, keepdims=True)
            bias.append(jnp.broadcast_to(jnp.where(hit > 0.5, 0.0, NEG), (1, BLOCK)))
        bias = jnp.concatenate(bias, axis=1)
        peaks, weights = [], []
        for at in range(0, 512, 64):
            t = raw[at : at + 64] * SCALE
            if at < 256:
                t = t + bias
            peak = jnp.max(t, axis=1, keepdims=True).astype(BF16).astype(F32)
            peaks.append(peak)
            weights.append(jnp.exp2(t - peak).astype(BF16))
        return jnp.concatenate(peaks, axis=0), jnp.concatenate(weights, axis=0)

    def summed(w, p):
        values = jnp.concatenate([v_ref[p], jnp.ones((1024, 128), BF16)], axis=1)
        return jnp.dot(w, values, preferred_element_type=F32)

    for move in moves:
        move.wait()
    raw = [scores(0), scores(1)]
    for p in range(2):
        peaks, w = softmax(raw[p], p)
        sums = summed(w, p)
        peaks, sums = [peaks[:256], peaks[256:]], [sums[:256], sums[256:]]
        if p == 1:
            tree_part()
        for y in range(4):
            for gp in range(4):
                dest = y * 8 + p * 4 + gp
                rows = [(gp * 2 + g2) * 32 + y * 8 for g2 in range(2)]
                for a in range(2):
                    both = jnp.concatenate([sums[a][r : r + 8, :128] for r in rows], axis=0)
                    send_ref[dest, a * 16 : (a + 1) * 16, :] = both.astype(BF16)
                m = four_lanes(lane, [peaks[a][r : r + 8] for a in range(2) for r in rows])
                tot = four_lanes(lane, [sums[a][r : r + 8, 128:] for a in range(2) for r in rows])
                high = tot.astype(BF16).astype(F32)
                stat = jnp.where(part < 2, m, jnp.where(part == 2, high, tot - high))
                send_ref[dest, 32:40, :] = stat.astype(BF16)
            chunk = pl.ds(y * 8 + p * 4, 4)
            leave(send_ref.at[chunk], send_hbm.at[chunk])
    leave(tree_ref, tree_hbm)
    for copy in leaving:
        copy.wait()


def combine_kernel(got_ref, tree_ref, out_ref):
    def spread(tile, at):
        return jnp.broadcast_to(tile[:, at : at + 1], (8, 128))

    peak = tree_ref[4]
    for s in range(32):
        peak = jnp.maximum(peak, got_ref[s, 32:40, :].astype(F32))
    factor = jnp.exp2(tree_ref[4] - peak)
    total = pltpu.roll(factor, 16, 1) * tree_ref[5]
    summed = [spread(factor, k * 32) * tree_ref[k] for k in range(4)]
    for s in range(32):
        stat = got_ref[s, 32:40, :].astype(F32)
        factor = jnp.exp2(stat - peak)
        total = total + pltpu.roll(factor, 16, 1) * stat
        for a in range(2):
            part = got_ref[s, a * 16 : (a + 1) * 16, :].astype(F32)
            for g2 in range(2):
                k = a * 2 + g2
                summed[k] = summed[k] + spread(factor, k * 32) * part[g2 * 8 : (g2 + 1) * 8]
    done = [
        summed[k] / (spread(total, k * 32 + 16) + spread(total, k * 32 + 24)) for k in range(4)
    ]
    rows = jnp.concatenate([done[0], done[2], done[1], done[3]], axis=0).astype(BF16)
    for h in range(16):
        out_ref[h] = rows


def onward_kernel(one_ref, three_ref, low_ref, high_ref):
    low_ref[...] = one_ref[:128]
    high_ref[...] = three_ref[128:]


def project_kernel(x_ref, own_ref, one_ref, three_ref, low_ref, high_ref, out_ref, turn_ref):
    seq = lax.axis_index("seq")
    y = seq // 8
    total = jnp.zeros((64, 512), F32)

    def place(r, j):
        return (1 + seq % 2 * 14) * (r * 4 + j) % 16

    for k in range(4):
        j = (y + 4 - k) % 4
        left = [
            jnp.concatenate(
                [x_ref[place(r, j), g2 * 16 : (g2 + 1) * 16, :] for r in range(4)], axis=0
            )
            for g2 in range(2)
        ]
        right = (own_ref, one_ref, None, three_ref)[k]
        if right is None:
            right = jnp.concatenate([low_ref[...], high_ref[...]], axis=0)
        else:
            right = right[...]
        left = jnp.concatenate(left, axis=1)
        total = total + jnp.dot(left, right, preferred_element_type=F32)
    for r in range(4):
        for a in range(2):
            at = (r * 2 + a) * 8
            turn_ref[:, a * 4 + r, :] = total[at : at + 8]
    out_ref[...] = turn_ref[...].astype(BF16)


def add_kernel(got_ref, draft_ref, verify_ref):
    total = got_ref[0].astype(F32)
    for s in range(1, 8):
        total = total + got_ref[s].astype(F32)
    draft_ref[0] = total[:4].astype(BF16)
    verify_ref[0] = total[4:].astype(BF16)


def swap(array, axis, groups=None):
    return lax.all_to_all(array, axis, 0, 0, tiled=True, axis_index_groups=groups)


def attend(
    queries, cache_keys, cache_values, block_ids, tree_keys, tree_values, ancestors
):
    return pl.pallas_call(
        attend_kernel,
        out_shape=(
            jax.ShapeDtypeStruct((32, 40, 128), BF16),
            jax.ShapeDtypeStruct((6, 8, 128), F32),
        ),
        in_specs=[HBM] * 7,
        out_specs=(HBM, HBM),
        scratch_shapes=[
            pltpu.VMEM((2, 2, 8, 32, 128), BF16),
            pltpu.VMEM((2, 1024, 128), BF16),
            pltpu.VMEM((2, 1024, 128), BF16),
            pltpu.VMEM((2, 32), jnp.int32),
            pltpu.VMEM((2, 2, 32, 128), BF16),
            pltpu.VMEM((2, 2, 32, 128), BF16),
            pltpu.VMEM((4, 32, 32), jnp.int32),
            pltpu.VMEM((32, 40, 128), BF16),
            pltpu.VMEM((6, 8, 128), F32),
            pltpu.VMEM((2, 2, 32, 128), F32),
            pltpu.VMEM((2, 2, 2, 32, 128), F32),
            pltpu.SemaphoreType.DMA((9,)),
            pltpu.SemaphoreType.DMA((9,)),
        ],
        compiler_params=pltpu.CompilerParams(vmem_limit_bytes=55296 * 1024),
    )(queries, cache_keys, cache_values, block_ids, tree_keys, tree_values, ancestors)


def shift(array, k):
    return lax.ppermute(array, "seq", [(s, (s + 8 * k) % 32) for s in range(32)])


def local(
    queries, tree_keys, tree_values, cache_keys, cache_values, block_ids, ancestors, out_weight
):
    send, tree = attend(
        queries, cache_keys, cache_values, block_ids, tree_keys, tree_values, ancestors
    )
    got = swap(send, "seq")
    one, three = shift(out_weight, 1), shift(out_weight, 3)
    rows = pl.pallas_call(
        combine_kernel,
        out_shape=jax.ShapeDtypeStruct((16, 32, 128), BF16),
        in_specs=[VMEM, VMEM],
        out_specs=VMEM,
        compiler_params=PARAMS,
    )(got, tree)
    gathered = swap(rows, ("seq", "head"), Z_GROUPS)
    low, high = pl.pallas_call(
        onward_kernel,
        out_shape=(jax.ShapeDtypeStruct((128, 512), BF16),) * 2,
        in_specs=[VMEM] * 2,
        out_specs=(VMEM, VMEM),
        cost_estimate=pl.CostEstimate(flops=10**10, bytes_accessed=0, transcendentals=0),
        compiler_params=PARAMS,
    )(one, three)
    low, high = shift(low, 1), shift(high, 3)
    parts = pl.pallas_call(
        project_kernel,
        out_shape=jax.ShapeDtypeStruct((8, 8, 512), BF16),
        in_specs=[VMEM] * 6,
        out_specs=VMEM,
        scratch_shapes=[pltpu.VMEM((8, 8, 512), F32)],
        compiler_params=PARAMS,
    )(gathered, out_weight, one, three, low, high)
    parts = swap(parts, "seq", XC_GROUPS)
    return pl.pallas_call(
        add_kernel,
        out_shape=(jax.ShapeDtypeStruct((1, 4, 512), BF16), jax.ShapeDtypeStruct((1, 4, 512), BF16)),
        in_specs=[VMEM],
        out_specs=(VMEM, VMEM),
        compiler_params=PARAMS,
    )(parts)


def solution(mesh):
    in_specs = (
        P(None, "head", None, None, None),
        P(None, "head", None, None),
        P(None, "head", None, None),
        P("head", "seq", None),
        P("head", "seq", None),
        P("head", None),
        P(),
        P("seq", "head"),
    )
    out_specs = (P("seq", None, "head"), P("seq", None, "head"))
    return jax.shard_map(local, mesh=mesh, in_specs=in_specs, out_specs=out_specs, check_vma=False)
```

```python
import jax
import jax.numpy as jnp
from jax import lax
from jax.experimental import pallas as pl
from jax.experimental.pallas import tpu as pltpu
from jax.sharding import PartitionSpec as P

KVH = 8
BLOCK = 128
SCALE = 128 ** (-0.5) * 1.4426950408889634
NEG = -(2.0**100)
F32 = jnp.float32
BF16 = jnp.bfloat16
Z_GROUPS = [[s * 16 + (1 + s % 2 * 14) * k % 16 for k in range(16)] for s in range(32)]
XC_GROUPS = [[y * 8 + k for k in range(8)] for y in range(4)]
NT = (((1,), (1,)), ((), ()))
VMEM = pl.BlockSpec(memory_space=pltpu.VMEM)
ANY = pl.BlockSpec(memory_space=pl.ANY)
HBM = pl.BlockSpec(memory_space=pltpu.HBM)
PARAMS = pltpu.CompilerParams(vmem_limit_bytes=32 * 1024 * 1024)


def four_lanes(lane, tiles):
    low = jnp.where(lane < 32, tiles[0], tiles[1])
    high = jnp.where(lane < 96, tiles[2], tiles[3])
    return jnp.where(lane < 64, low, high)


def attend_kernel(
    q_hbm, k_hbm, v_hbm, ids_hbm, tk_hbm, tv_hbm, anc_hbm,
    send_hbm, tree_hbm,
    q_ref, k_ref, v_ref, ids_ref, tk_ref, tv_ref, anc_ref,
    send_ref, tree_ref, acc_ref, stat_ref, sems, out_sems,
):
    moves = [
        (k_hbm.at[0], k_ref.at[0]),
        (q_hbm, q_ref),
        (ids_hbm, ids_ref),
        (v_hbm.at[0], v_ref.at[0]),
        (tk_hbm, tk_ref),
        (tv_hbm, tv_ref),
        (anc_hbm, anc_ref),
        (k_hbm.at[1], k_ref.at[1]),
        (v_hbm.at[1], v_ref.at[1]),
    ]
    moves = [pltpu.make_async_copy(a, b, sems.at[i]) for i, (a, b) in enumerate(moves)]
    for move in moves:
        move.start()
    seq = lax.axis_index("seq")
    head = lax.axis_index("head")
    lane = lax.broadcasted_iota(jnp.int32, (8, 128), 1)
    first_half = (lane % 32) < 16
    leaving = []

    def leave(source, target):
        copy = pltpu.make_async_copy(source, target, out_sems.at[len(leaving)])
        copy.start()
        leaving.append(copy)

    def tree_part():
        y, x, core = seq // 8, (seq % 8) // 2, seq % 2
        own, gp = x // 2, (x % 2) * 2 + core
        allowed = anc_ref[head // 4] > 0
        allowed = jnp.concatenate([allowed, allowed], axis=0)
        for a in range(2):
            q = q_ref[a, own, pl.ds(gp * 2, 2)].reshape(64, 128)
            t = lax.dot_general(q, tk_ref[a, own], NT, preferred_element_type=F32) * SCALE
            t = jnp.where(allowed, t, NEG)
            peak = jnp.max(t, axis=1, keepdims=True)
            w = jnp.where(allowed, jnp.exp2(t - peak), 0.0)
            total = jnp.sum(w, axis=1, keepdims=True)
            summed = jnp.dot(w.astype(BF16), tv_ref[a, own], preferred_element_type=F32)
            acc_ref[a] = summed.reshape(2, 32, 128)
            stat_ref[0, a] = jnp.broadcast_to(peak, (64, 128)).reshape(2, 32, 128)
            stat_ref[1, a] = jnp.broadcast_to(total, (64, 128)).reshape(2, 32, 128)
        start = pl.multiple_of(y * 8, 8)
        for a in range(2):
            for g2 in range(2):
                tree_ref[a * 2 + g2] = acc_ref[a, g2, pl.ds(start, 8), :]
        peak, total = (
            four_lanes(
                lane, [stat_ref[k, a, g2, pl.ds(start, 8), :] for a in range(2) for g2 in range(2)]
            )
            for k in range(2)
        )
        tree_ref[4] = peak
        tree_ref[5] = jnp.where(first_half, total, 0.0)


    def scores(p):
        q = q_ref[:, p].reshape(512, 128)
        return lax.dot_general(q, k_ref[p], NT, preferred_element_type=F32)

    def softmax(raw, p):
        ids = ids_ref[p : p + 1, :]
        bias = []
        for b in range(8):
            hit = jnp.max(jnp.where(ids == seq * 8 + b, 1.0, 0.0), axis=1, keepdims=True)
            bias.append(jnp.broadcast_to(jnp.where(hit > 0.5, 0.0, NEG), (1, BLOCK)))
        bias = jnp.concatenate(bias, axis=1)
        peaks, weights = [], []
        for at in range(0, 512, 64):
            t = raw[at : at + 64] * SCALE
            if at < 256:
                t = t + bias
            peak = jnp.max(t, axis=1, keepdims=True).astype(BF16).astype(F32)
            peaks.append(peak)
            weights.append(jnp.exp2(t - peak).astype(BF16))
        return jnp.concatenate(peaks, axis=0), jnp.concatenate(weights, axis=0)

    def summed(w, p):
        values = jnp.concatenate([v_ref[p], jnp.ones((1024, 128), BF16)], axis=1)
        return jnp.dot(w, values, preferred_element_type=F32)

    for move in moves:
        move.wait()
    raw = [scores(0), scores(1)]
    for p in range(2):
        peaks, w = softmax(raw[p], p)
        sums = summed(w, p)
        peaks, sums = [peaks[:256], peaks[256:]], [sums[:256], sums[256:]]
        if p == 1:
            tree_part()
        for y in range(4):
            for gp in range(4):
                dest = y * 8 + p * 4 + gp
                rows = [(gp * 2 + g2) * 32 + y * 8 for g2 in range(2)]
                for a in range(2):
                    both = jnp.concatenate([sums[a][r : r + 8, :128] for r in rows], axis=0)
                    send_ref[dest, a * 16 : (a + 1) * 16, :] = both.astype(BF16)
                m = four_lanes(lane, [peaks[a][r : r + 8] for a in range(2) for r in rows])
                tot = four_lanes(lane, [sums[a][r : r + 8, 128:] for a in range(2) for r in rows])
                high = tot.astype(BF16).astype(F32)
                tot = jnp.where(first_half, high, tot - high)
                send_ref[dest, 32:48, :] = jnp.concatenate([m, tot], axis=0).astype(BF16)
            chunk = pl.ds(y * 8 + p * 4, 4)
            leave(send_ref.at[chunk], send_hbm.at[chunk])
    leave(tree_ref, tree_hbm)
    for copy in leaving:
        copy.wait()


def combine_kernel(got_ref, tree_ref, out_ref):
    def spread(tile, at):
        return jnp.broadcast_to(tile[:, at : at + 1], (8, 128))

    peak = tree_ref[4]
    for s in range(32):
        peak = jnp.maximum(peak, got_ref[s, 32:48, :].astype(F32)[:8])
    factor = jnp.exp2(tree_ref[4] - peak)
    total = factor * tree_ref[5]
    summed = [spread(factor, k * 32) * tree_ref[k] for k in range(4)]
    for s in range(32):
        stat = got_ref[s, 32:48, :].astype(F32)
        factor = jnp.exp2(stat[:8] - peak)
        total = total + factor * stat[8:]
        for a in range(2):
            part = got_ref[s, a * 16 : (a + 1) * 16, :].astype(F32)
            for g2 in range(2):
                k = a * 2 + g2
                summed[k] = summed[k] + spread(factor, k * 32) * part[g2 * 8 : (g2 + 1) * 8]
    done = [
        summed[k] / (spread(total, k * 32) + spread(total, k * 32 + 16)) for k in range(4)
    ]
    rows = jnp.concatenate([done[0], done[2], done[1], done[3]], axis=0).astype(BF16)
    for h in range(16):
        out_ref[h] = rows


def onward_kernel(one_ref, three_ref, low_ref, high_ref):
    low_ref[...] = one_ref[:128]
    high_ref[...] = three_ref[128:]


def project_kernel(x_ref, own_ref, one_ref, three_ref, low_ref, high_ref, out_ref, turn_ref):
    seq = lax.axis_index("seq")
    y = seq // 8
    total = jnp.zeros((64, 512), F32)

    def place(r, j):
        return (1 + seq % 2 * 14) * (r * 4 + j) % 16

    for k in range(4):
        j = (y + 4 - k) % 4
        left = [
            jnp.concatenate(
                [x_ref[place(r, j), g2 * 16 : (g2 + 1) * 16, :] for r in range(4)], axis=0
            )
            for g2 in range(2)
        ]
        right = (own_ref, one_ref, None, three_ref)[k]
        if right is None:
            right = jnp.concatenate([low_ref[...], high_ref[...]], axis=0)
        else:
            right = right[...]
        left = jnp.concatenate(left, axis=1)
        total = total + jnp.dot(left, right, preferred_element_type=F32)
    for r in range(4):
        for a in range(2):
            at = (r * 2 + a) * 8
            turn_ref[:, a * 4 + r, :] = total[at : at + 8]
    out_ref[...] = turn_ref[...].astype(BF16)


def add_kernel(got_ref, draft_ref, verify_ref):
    total = got_ref[0].astype(F32)
    for s in range(1, 8):
        total = total + got_ref[s].astype(F32)
    draft_ref[0] = total[:4].astype(BF16)
    verify_ref[0] = total[4:].astype(BF16)


def swap(array, axis, groups=None):
    return lax.all_to_all(array, axis, 0, 0, tiled=True, axis_index_groups=groups)


def attend(
    queries, cache_keys, cache_values, block_ids, tree_keys, tree_values, ancestors
):
    return pl.pallas_call(
        attend_kernel,
        out_shape=(
            jax.ShapeDtypeStruct((32, 48, 128), BF16),
            jax.ShapeDtypeStruct((6, 8, 128), F32),
        ),
        in_specs=[HBM] * 7,
        out_specs=(HBM, HBM),
        scratch_shapes=[
            pltpu.VMEM((2, 2, 8, 32, 128), BF16),
            pltpu.VMEM((2, 1024, 128), BF16),
            pltpu.VMEM((2, 1024, 128), BF16),
            pltpu.VMEM((2, 32), jnp.int32),
            pltpu.VMEM((2, 2, 32, 128), BF16),
            pltpu.VMEM((2, 2, 32, 128), BF16),
            pltpu.VMEM((4, 32, 32), jnp.int32),
            pltpu.VMEM((32, 48, 128), BF16),
            pltpu.VMEM((6, 8, 128), F32),
            pltpu.VMEM((2, 2, 32, 128), F32),
            pltpu.VMEM((2, 2, 2, 32, 128), F32),
            pltpu.SemaphoreType.DMA((9,)),
            pltpu.SemaphoreType.DMA((9,)),
        ],
        compiler_params=pltpu.CompilerParams(vmem_limit_bytes=55296 * 1024),
    )(queries, cache_keys, cache_values, block_ids, tree_keys, tree_values, ancestors)


def shift(array, k):
    return lax.ppermute(array, "seq", [(s, (s + 8 * k) % 32) for s in range(32)])


def local(
    queries, tree_keys, tree_values, cache_keys, cache_values, block_ids, ancestors, out_weight
):
    send, tree = attend(
        queries, cache_keys, cache_values, block_ids, tree_keys, tree_values, ancestors
    )
    got = swap(send, "seq")
    one, three = shift(out_weight, 1), shift(out_weight, 3)
    rows = pl.pallas_call(
        combine_kernel,
        out_shape=jax.ShapeDtypeStruct((16, 32, 128), BF16),
        in_specs=[VMEM, VMEM],
        out_specs=VMEM,
        compiler_params=PARAMS,
    )(got, tree)
    gathered = swap(rows, ("seq", "head"), Z_GROUPS)
    low, high = pl.pallas_call(
        onward_kernel,
        out_shape=(jax.ShapeDtypeStruct((128, 512), BF16),) * 2,
        in_specs=[VMEM] * 2,
        out_specs=(VMEM, VMEM),
        cost_estimate=pl.CostEstimate(flops=10**10, bytes_accessed=0, transcendentals=0),
        compiler_params=PARAMS,
    )(one, three)
    low, high = shift(low, 1), shift(high, 3)
    parts = pl.pallas_call(
        project_kernel,
        out_shape=jax.ShapeDtypeStruct((8, 8, 512), BF16),
        in_specs=[VMEM] * 6,
        out_specs=VMEM,
        scratch_shapes=[pltpu.VMEM((8, 8, 512), F32)],
        compiler_params=PARAMS,
    )(gathered, out_weight, one, three, low, high)
    parts = swap(parts, "seq", XC_GROUPS)
    return pl.pallas_call(
        add_kernel,
        out_shape=(jax.ShapeDtypeStruct((1, 4, 512), BF16), jax.ShapeDtypeStruct((1, 4, 512), BF16)),
        in_specs=[VMEM],
        out_specs=(VMEM, VMEM),
        compiler_params=PARAMS,
    )(parts)


def solution(mesh):
    in_specs = (
        P(None, "head", None, None, None),
        P(None, "head", None, None),
        P(None, "head", None, None),
        P("head", "seq", None),
        P("head", "seq", None),
        P("head", None),
        P(),
        P("seq", "head"),
    )
    out_specs = (P("seq", None, "head"), P("seq", None, "head"))
    return jax.shard_map(local, mesh=mesh, in_specs=in_specs, out_specs=out_specs, check_vma=False)
```

```python
import jax
import jax.numpy as jnp
from jax import lax
from jax.experimental import pallas as pl
from jax.experimental.pallas import tpu as pltpu
from jax.sharding import PartitionSpec as P

KVH = 8
BLOCK = 128
SCALE = 128 ** (-0.5) * 1.4426950408889634
NEG = -(2.0**100)
F32 = jnp.float32
BF16 = jnp.bfloat16
Z_GROUPS = [[s * 16 + (1 + s % 2 * 14) * k % 16 for k in range(16)] for s in range(32)]
XC_GROUPS = [[y * 8 + k for k in range(8)] for y in range(4)]
NT = (((1,), (1,)), ((), ()))
VMEM = pl.BlockSpec(memory_space=pltpu.VMEM)
ANY = pl.BlockSpec(memory_space=pl.ANY)
HBM = pl.BlockSpec(memory_space=pltpu.HBM)
PARAMS = pltpu.CompilerParams(vmem_limit_bytes=32 * 1024 * 1024)


def four_lanes(lane, tiles):
    low = jnp.where(lane < 32, tiles[0], tiles[1])
    high = jnp.where(lane < 96, tiles[2], tiles[3])
    return jnp.where(lane < 64, low, high)


def attend_kernel(
    q_hbm, k_hbm, v_hbm, ids_hbm, tk_hbm, tv_hbm, anc_hbm,
    send_hbm, tree_hbm,
    q_ref, k_ref, v_ref, ids_ref, tk_ref, tv_ref, anc_ref,
    send_ref, tree_ref, acc_ref, stat_ref, sems, out_sems,
):
    moves = [
        (k_hbm.at[0], k_ref.at[0]),
        (q_hbm, q_ref),
        (ids_hbm, ids_ref),
        (v_hbm.at[0], v_ref.at[0]),
        (tk_hbm, tk_ref),
        (tv_hbm, tv_ref),
        (anc_hbm, anc_ref),
        (k_hbm.at[1], k_ref.at[1]),
        (v_hbm.at[1], v_ref.at[1]),
    ]
    moves = [pltpu.make_async_copy(a, b, sems.at[i]) for i, (a, b) in enumerate(moves)]
    for move in moves:
        move.start()
    seq = lax.axis_index("seq")
    head = lax.axis_index("head")
    lane = lax.broadcasted_iota(jnp.int32, (8, 128), 1)
    first_half = (lane % 32) < 16
    leaving = []

    def leave(source, target):
        copy = pltpu.make_async_copy(source, target, out_sems.at[len(leaving)])
        copy.start()
        leaving.append(copy)

    def tree_part():
        y, x, core = seq // 8, (seq % 8) // 2, seq % 2
        own, gp = x // 2, (x % 2) * 2 + core
        allowed = anc_ref[head // 4] > 0
        allowed = jnp.concatenate([allowed, allowed], axis=0)
        for a in range(2):
            q = q_ref[a, own, pl.ds(gp * 2, 2)].reshape(64, 128)
            t = lax.dot_general(q, tk_ref[a, own], NT, preferred_element_type=F32) * SCALE
            t = jnp.where(allowed, t, NEG)
            peak = jnp.max(t, axis=1, keepdims=True)
            w = jnp.where(allowed, jnp.exp2(t - peak), 0.0)
            total = jnp.sum(w, axis=1, keepdims=True)
            summed = jnp.dot(w.astype(BF16), tv_ref[a, own], preferred_element_type=F32)
            acc_ref[a] = summed.reshape(2, 32, 128)
            stat_ref[0, a] = jnp.broadcast_to(peak, (64, 128)).reshape(2, 32, 128)
            stat_ref[1, a] = jnp.broadcast_to(total, (64, 128)).reshape(2, 32, 128)
        start = pl.multiple_of(y * 8, 8)
        for a in range(2):
            for g2 in range(2):
                tree_ref[a * 2 + g2] = acc_ref[a, g2, pl.ds(start, 8), :]
        peak, total = (
            four_lanes(
                lane, [stat_ref[k, a, g2, pl.ds(start, 8), :] for a in range(2) for g2 in range(2)]
            )
            for k in range(2)
        )
        tree_ref[4] = peak
        tree_ref[5] = jnp.where(first_half, total, 0.0)


    def scores(p):
        q = q_ref[:, p].reshape(512, 128)
        return lax.dot_general(q, k_ref[p], NT, preferred_element_type=F32)

    def softmax(raw, p):
        ids = ids_ref[p : p + 1, :]
        bias = []
        for b in range(8):
            hit = jnp.max(jnp.where(ids == seq * 8 + b, 1.0, 0.0), axis=1, keepdims=True)
            bias.append(jnp.broadcast_to(jnp.where(hit > 0.5, 0.0, NEG), (1, BLOCK)))
        bias = jnp.concatenate(bias, axis=1)
        peaks, weights = [], []
        for at in range(0, 512, 64):
            t = raw[at : at + 64] * SCALE
            if at < 256:
                t = t + bias
            peak = jnp.max(t, axis=1, keepdims=True).astype(BF16).astype(F32)
            peaks.append(peak)
            weights.append(jnp.exp2(t - peak).astype(BF16))
        return jnp.concatenate(peaks, axis=0), jnp.concatenate(weights, axis=0)

    def summed(w, p):
        values = jnp.concatenate([v_ref[p], jnp.ones((1024, 128), BF16)], axis=1)
        return jnp.dot(w, values, preferred_element_type=F32)

    for move in moves:
        move.wait()
    raw = [scores(0), scores(1)]
    for p in range(2):
        peaks, w = softmax(raw[p], p)
        sums = summed(w, p)
        peaks, sums = [peaks[:256], peaks[256:]], [sums[:256], sums[256:]]
        if p == 1:
            tree_part()
        for y in range(4):
            for gp in range(4):
                dest = y * 8 + p * 4 + gp
                rows = [(gp * 2 + g2) * 32 + y * 8 for g2 in range(2)]
                for a in range(2):
                    both = jnp.concatenate([sums[a][r : r + 8, :128] for r in rows], axis=0)
                    send_ref[dest, a * 16 : (a + 1) * 16, :] = both.astype(BF16)
                m = four_lanes(lane, [peaks[a][r : r + 8] for a in range(2) for r in rows])
                tot = four_lanes(lane, [sums[a][r : r + 8, 128:] for a in range(2) for r in rows])
                high = tot.astype(BF16).astype(F32)
                tot = jnp.where(first_half, high, tot - high)
                send_ref[dest, 32:48, :] = jnp.concatenate([m, tot], axis=0).astype(BF16)
            chunk = pl.ds(y * 8 + p * 4, 4)
            leave(send_ref.at[chunk], send_hbm.at[chunk])
    leave(tree_ref, tree_hbm)
    for copy in leaving:
        copy.wait()


def combine_kernel(got_ref, tree_ref, out_hbm, rows_ref, sems):
    def spread(tile, at):
        return jnp.broadcast_to(tile[:, at : at + 1], (8, 128))

    peak = tree_ref[4]
    for s in range(32):
        peak = jnp.maximum(peak, got_ref[s, 32:48, :].astype(F32)[:8])
    factor = jnp.exp2(tree_ref[4] - peak)
    total = factor * tree_ref[5]
    summed = [spread(factor, k * 32) * tree_ref[k] for k in range(4)]
    for s in range(32):
        stat = got_ref[s, 32:48, :].astype(F32)
        factor = jnp.exp2(stat[:8] - peak)
        total = total + factor * stat[8:]
        for a in range(2):
            part = got_ref[s, a * 16 : (a + 1) * 16, :].astype(F32)
            for g2 in range(2):
                k = a * 2 + g2
                summed[k] = summed[k] + spread(factor, k * 32) * part[g2 * 8 : (g2 + 1) * 8]
    done = [
        summed[k] / (spread(total, k * 32) + spread(total, k * 32 + 16)) for k in range(4)
    ]
    rows_ref[...] = jnp.concatenate([done[0], done[2], done[1], done[3]], axis=0).astype(BF16)
    copies = [pltpu.make_async_copy(rows_ref, out_hbm.at[h], sems.at[h]) for h in range(16)]
    for copy in copies:
        copy.start()
    for copy in copies:
        copy.wait()


def onward_kernel(one_ref, three_ref, low_ref, high_ref):
    low_ref[...] = one_ref[:128]
    high_ref[...] = three_ref[128:]


def project_kernel(x_ref, own_ref, one_ref, three_ref, low_ref, high_ref, out_ref, turn_ref):
    seq = lax.axis_index("seq")
    y = seq // 8
    total = jnp.zeros((64, 512), F32)

    def place(r, j):
        return (1 + seq % 2 * 14) * (r * 4 + j) % 16

    for k in range(4):
        j = (y + 4 - k) % 4
        left = [
            jnp.concatenate(
                [x_ref[place(r, j), g2 * 16 : (g2 + 1) * 16, :] for r in range(4)], axis=0
            )
            for g2 in range(2)
        ]
        right = (own_ref, one_ref, None, three_ref)[k]
        if right is None:
            right = jnp.concatenate([low_ref[...], high_ref[...]], axis=0)
        else:
            right = right[...]
        left = jnp.concatenate(left, axis=1)
        total = total + jnp.dot(left, right, preferred_element_type=F32)
    for r in range(4):
        for a in range(2):
            at = (r * 2 + a) * 8
            turn_ref[:, a * 4 + r, :] = total[at : at + 8]
    out_ref[...] = turn_ref[...].astype(BF16)


def add_kernel(got_ref, draft_ref, verify_ref):
    total = got_ref[0].astype(F32)
    for s in range(1, 8):
        total = total + got_ref[s].astype(F32)
    draft_ref[0] = total[:4].astype(BF16)
    verify_ref[0] = total[4:].astype(BF16)


def swap(array, axis, groups=None):
    return lax.all_to_all(array, axis, 0, 0, tiled=True, axis_index_groups=groups)


def attend(
    queries, cache_keys, cache_values, block_ids, tree_keys, tree_values, ancestors
):
    return pl.pallas_call(
        attend_kernel,
        out_shape=(
            jax.ShapeDtypeStruct((32, 48, 128), BF16),
            jax.ShapeDtypeStruct((6, 8, 128), F32),
        ),
        in_specs=[HBM] * 7,
        out_specs=(HBM, HBM),
        scratch_shapes=[
            pltpu.VMEM((2, 2, 8, 32, 128), BF16),
            pltpu.VMEM((2, 1024, 128), BF16),
            pltpu.VMEM((2, 1024, 128), BF16),
            pltpu.VMEM((2, 32), jnp.int32),
            pltpu.VMEM((2, 2, 32, 128), BF16),
            pltpu.VMEM((2, 2, 32, 128), BF16),
            pltpu.VMEM((4, 32, 32), jnp.int32),
            pltpu.VMEM((32, 48, 128), BF16),
            pltpu.VMEM((6, 8, 128), F32),
            pltpu.VMEM((2, 2, 32, 128), F32),
            pltpu.VMEM((2, 2, 2, 32, 128), F32),
            pltpu.SemaphoreType.DMA((9,)),
            pltpu.SemaphoreType.DMA((9,)),
        ],
        compiler_params=pltpu.CompilerParams(vmem_limit_bytes=55296 * 1024),
    )(queries, cache_keys, cache_values, block_ids, tree_keys, tree_values, ancestors)


def shift(array, k):
    return lax.ppermute(array, "seq", [(s, (s + 8 * k) % 32) for s in range(32)])


def local(
    queries, tree_keys, tree_values, cache_keys, cache_values, block_ids, ancestors, out_weight
):
    send, tree = attend(
        queries, cache_keys, cache_values, block_ids, tree_keys, tree_values, ancestors
    )
    got = swap(send, "seq")
    one, three = shift(out_weight, 1), shift(out_weight, 3)
    rows = pl.pallas_call(
        combine_kernel,
        out_shape=jax.ShapeDtypeStruct((16, 32, 128), BF16),
        in_specs=[VMEM, VMEM],
        out_specs=HBM,
        scratch_shapes=[pltpu.VMEM((32, 128), BF16), pltpu.SemaphoreType.DMA((16,))],
        compiler_params=PARAMS,
    )(got, tree)
    gathered = swap(rows, ("seq", "head"), Z_GROUPS)
    low, high = pl.pallas_call(
        onward_kernel,
        out_shape=(jax.ShapeDtypeStruct((128, 512), BF16),) * 2,
        in_specs=[VMEM] * 2,
        out_specs=(VMEM, VMEM),
        cost_estimate=pl.CostEstimate(flops=10**10, bytes_accessed=0, transcendentals=0),
        compiler_params=PARAMS,
    )(one, three)
    low, high = shift(low, 1), shift(high, 3)
    parts = pl.pallas_call(
        project_kernel,
        out_shape=jax.ShapeDtypeStruct((8, 8, 512), BF16),
        in_specs=[VMEM] * 6,
        out_specs=VMEM,
        scratch_shapes=[pltpu.VMEM((8, 8, 512), F32)],
        compiler_params=PARAMS,
    )(gathered, out_weight, one, three, low, high)
    parts = swap(parts, "seq", XC_GROUPS)
    return pl.pallas_call(
        add_kernel,
        out_shape=(jax.ShapeDtypeStruct((1, 4, 512), BF16), jax.ShapeDtypeStruct((1, 4, 512), BF16)),
        in_specs=[VMEM],
        out_specs=(VMEM, VMEM),
        compiler_params=PARAMS,
    )(parts)


def solution(mesh):
    in_specs = (
        P(None, "head", None, None, None),
        P(None, "head", None, None),
        P(None, "head", None, None),
        P("head", "seq", None),
        P("head", "seq", None),
        P("head", None),
        P(),
        P("seq", "head"),
    )
    out_specs = (P("seq", None, "head"), P("seq", None, "head"))
    return jax.shard_map(local, mesh=mesh, in_specs=in_specs, out_specs=out_specs, check_vma=False)
```

```python
import jax
import jax.numpy as jnp
from jax import lax
from jax.experimental import pallas as pl
from jax.experimental.pallas import tpu as pltpu
from jax.sharding import PartitionSpec as P

KVH = 8
BLOCK = 128
SCALE = 128 ** (-0.5) * 1.4426950408889634
NEG = -(2.0**100)
F32 = jnp.float32
BF16 = jnp.bfloat16
Z_GROUPS = [[s * 16 + (7 + s % 2 * 2) * k % 16 for k in range(16)] for s in range(32)]
XC_GROUPS = [[y * 8 + k for k in range(8)] for y in range(4)]
NT = (((1,), (1,)), ((), ()))
VMEM = pl.BlockSpec(memory_space=pltpu.VMEM)
ANY = pl.BlockSpec(memory_space=pl.ANY)
HBM = pl.BlockSpec(memory_space=pltpu.HBM)
PARAMS = pltpu.CompilerParams(vmem_limit_bytes=32 * 1024 * 1024)


def four_lanes(lane, tiles):
    low = jnp.where(lane < 32, tiles[0], tiles[1])
    high = jnp.where(lane < 96, tiles[2], tiles[3])
    return jnp.where(lane < 64, low, high)


def attend_kernel(
    q_hbm, k_hbm, v_hbm, ids_hbm, tk_hbm, tv_hbm, anc_hbm,
    send_hbm, tree_hbm,
    q_ref, k_ref, v_ref, ids_ref, tk_ref, tv_ref, anc_ref,
    send_ref, tree_ref, acc_ref, stat_ref, sems, out_sems,
):
    moves = [
        (k_hbm.at[0], k_ref.at[0]),
        (q_hbm, q_ref),
        (ids_hbm, ids_ref),
        (v_hbm.at[0], v_ref.at[0]),
        (tk_hbm, tk_ref),
        (tv_hbm, tv_ref),
        (anc_hbm, anc_ref),
        (k_hbm.at[1], k_ref.at[1]),
        (v_hbm.at[1], v_ref.at[1]),
    ]
    moves = [pltpu.make_async_copy(a, b, sems.at[i]) for i, (a, b) in enumerate(moves)]
    for move in moves:
        move.start()
    seq = lax.axis_index("seq")
    head = lax.axis_index("head")
    lane = lax.broadcasted_iota(jnp.int32, (8, 128), 1)
    first_half = (lane % 32) < 16
    leaving = []

    def leave(source, target):
        copy = pltpu.make_async_copy(source, target, out_sems.at[len(leaving)])
        copy.start()
        leaving.append(copy)

    def tree_part():
        y, x, core = seq // 8, (seq % 8) // 2, seq % 2
        own, gp = x // 2, (x % 2) * 2 + core
        allowed = anc_ref[head // 4] > 0
        allowed = jnp.concatenate([allowed, allowed], axis=0)
        for a in range(2):
            q = q_ref[a, own, pl.ds(gp * 2, 2)].reshape(64, 128)
            t = lax.dot_general(q, tk_ref[a, own], NT, preferred_element_type=F32) * SCALE
            t = jnp.where(allowed, t, NEG)
            peak = jnp.max(t, axis=1, keepdims=True)
            w = jnp.where(allowed, jnp.exp2(t - peak), 0.0)
            total = jnp.sum(w, axis=1, keepdims=True)
            summed = jnp.dot(w.astype(BF16), tv_ref[a, own], preferred_element_type=F32)
            acc_ref[a] = summed.reshape(2, 32, 128)
            stat_ref[0, a] = jnp.broadcast_to(peak, (64, 128)).reshape(2, 32, 128)
            stat_ref[1, a] = jnp.broadcast_to(total, (64, 128)).reshape(2, 32, 128)
        start = pl.multiple_of(y * 8, 8)
        for a in range(2):
            for g2 in range(2):
                tree_ref[a * 2 + g2] = acc_ref[a, g2, pl.ds(start, 8), :]
        peak, total = (
            four_lanes(
                lane, [stat_ref[k, a, g2, pl.ds(start, 8), :] for a in range(2) for g2 in range(2)]
            )
            for k in range(2)
        )
        tree_ref[4] = peak
        tree_ref[5] = jnp.where(first_half, total, 0.0)


    def scores(p):
        q = q_ref[:, p].reshape(512, 128)
        return lax.dot_general(q, k_ref[p], NT, preferred_element_type=F32)

    def softmax(raw, p):
        ids = ids_ref[p : p + 1, :]
        bias = []
        for b in range(8):
            hit = jnp.max(jnp.where(ids == seq * 8 + b, 1.0, 0.0), axis=1, keepdims=True)
            bias.append(jnp.broadcast_to(jnp.where(hit > 0.5, 0.0, NEG), (1, BLOCK)))
        bias = jnp.concatenate(bias, axis=1)
        peaks, weights = [], []
        for at in range(0, 512, 64):
            t = raw[at : at + 64] * SCALE
            if at < 256:
                t = t + bias
            peak = jnp.max(t, axis=1, keepdims=True).astype(BF16).astype(F32)
            peaks.append(peak)
            weights.append(jnp.exp2(t - peak).astype(BF16))
        return jnp.concatenate(peaks, axis=0), jnp.concatenate(weights, axis=0)

    def summed(w, p):
        values = jnp.concatenate([v_ref[p], jnp.ones((1024, 128), BF16)], axis=1)
        return jnp.dot(w, values, preferred_element_type=F32)

    for move in moves:
        move.wait()
    raw = [scores(0), scores(1)]
    for p in range(2):
        peaks, w = softmax(raw[p], p)
        sums = summed(w, p)
        peaks, sums = [peaks[:256], peaks[256:]], [sums[:256], sums[256:]]
        if p == 1:
            tree_part()
        for y in range(4):
            for gp in range(4):
                dest = y * 8 + p * 4 + gp
                rows = [(gp * 2 + g2) * 32 + y * 8 for g2 in range(2)]
                for a in range(2):
                    both = jnp.concatenate([sums[a][r : r + 8, :128] for r in rows], axis=0)
                    send_ref[dest, a * 16 : (a + 1) * 16, :] = both.astype(BF16)
                m = four_lanes(lane, [peaks[a][r : r + 8] for a in range(2) for r in rows])
                tot = four_lanes(lane, [sums[a][r : r + 8, 128:] for a in range(2) for r in rows])
                high = tot.astype(BF16).astype(F32)
                tot = jnp.where(first_half, high, tot - high)
                send_ref[dest, 32:48, :] = jnp.concatenate([m, tot], axis=0).astype(BF16)
            chunk = pl.ds(y * 8 + p * 4, 4)
            leave(send_ref.at[chunk], send_hbm.at[chunk])
    leave(tree_ref, tree_hbm)
    for copy in leaving:
        copy.wait()


def combine_kernel(got_ref, tree_ref, out_ref):
    def spread(tile, at):
        return jnp.broadcast_to(tile[:, at : at + 1], (8, 128))

    peak = tree_ref[4]
    for s in range(32):
        peak = jnp.maximum(peak, got_ref[s, 32:48, :].astype(F32)[:8])
    factor = jnp.exp2(tree_ref[4] - peak)
    total = factor * tree_ref[5]
    summed = [spread(factor, k * 32) * tree_ref[k] for k in range(4)]
    for s in range(32):
        stat = got_ref[s, 32:48, :].astype(F32)
        factor = jnp.exp2(stat[:8] - peak)
        total = total + factor * stat[8:]
        for a in range(2):
            part = got_ref[s, a * 16 : (a + 1) * 16, :].astype(F32)
            for g2 in range(2):
                k = a * 2 + g2
                summed[k] = summed[k] + spread(factor, k * 32) * part[g2 * 8 : (g2 + 1) * 8]
    done = [
        summed[k] / (spread(total, k * 32) + spread(total, k * 32 + 16)) for k in range(4)
    ]
    rows = jnp.concatenate([done[0], done[2], done[1], done[3]], axis=0).astype(BF16)
    for h in range(16):
        out_ref[h] = rows


def onward_kernel(one_ref, three_ref, low_ref, high_ref):
    low_ref[...] = one_ref[:128]
    high_ref[...] = three_ref[128:]


def project_kernel(x_ref, own_ref, one_ref, three_ref, low_ref, high_ref, out_ref, turn_ref):
    seq = lax.axis_index("seq")
    y = seq // 8
    total = jnp.zeros((64, 512), F32)

    def place(r, j):
        return (7 + seq % 2 * 2) * (r * 4 + j) % 16

    for k in range(4):
        j = (y + 4 - k) % 4
        left = [
            jnp.concatenate(
                [x_ref[place(r, j), g2 * 16 : (g2 + 1) * 16, :] for r in range(4)], axis=0
            )
            for g2 in range(2)
        ]
        right = (own_ref, one_ref, None, three_ref)[k]
        if right is None:
            right = jnp.concatenate([low_ref[...], high_ref[...]], axis=0)
        else:
            right = right[...]
        left = jnp.concatenate(left, axis=1)
        total = total + jnp.dot(left, right, preferred_element_type=F32)
    for r in range(4):
        for a in range(2):
            at = (r * 2 + a) * 8
            turn_ref[:, a * 4 + r, :] = total[at : at + 8]
    out_ref[...] = turn_ref[...].astype(BF16)


def add_kernel(got_ref, draft_ref, verify_ref):
    total = got_ref[0].astype(F32)
    for s in range(1, 8):
        total = total + got_ref[s].astype(F32)
    draft_ref[0] = total[:4].astype(BF16)
    verify_ref[0] = total[4:].astype(BF16)


def swap(array, axis, groups=None):
    return lax.all_to_all(array, axis, 0, 0, tiled=True, axis_index_groups=groups)


def attend(
    queries, cache_keys, cache_values, block_ids, tree_keys, tree_values, ancestors
):
    return pl.pallas_call(
        attend_kernel,
        out_shape=(
            jax.ShapeDtypeStruct((32, 48, 128), BF16),
            jax.ShapeDtypeStruct((6, 8, 128), F32),
        ),
        in_specs=[HBM] * 7,
        out_specs=(HBM, HBM),
        scratch_shapes=[
            pltpu.VMEM((2, 2, 8, 32, 128), BF16),
            pltpu.VMEM((2, 1024, 128), BF16),
            pltpu.VMEM((2, 1024, 128), BF16),
            pltpu.VMEM((2, 32), jnp.int32),
            pltpu.VMEM((2, 2, 32, 128), BF16),
            pltpu.VMEM((2, 2, 32, 128), BF16),
            pltpu.VMEM((4, 32, 32), jnp.int32),
            pltpu.VMEM((32, 48, 128), BF16),
            pltpu.VMEM((6, 8, 128), F32),
            pltpu.VMEM((2, 2, 32, 128), F32),
            pltpu.VMEM((2, 2, 2, 32, 128), F32),
            pltpu.SemaphoreType.DMA((9,)),
            pltpu.SemaphoreType.DMA((9,)),
        ],
        compiler_params=pltpu.CompilerParams(vmem_limit_bytes=55296 * 1024),
    )(queries, cache_keys, cache_values, block_ids, tree_keys, tree_values, ancestors)


def shift(array, k):
    return lax.ppermute(array, "seq", [(s, (s + 8 * k) % 32) for s in range(32)])


def local(
    queries, tree_keys, tree_values, cache_keys, cache_values, block_ids, ancestors, out_weight
):
    send, tree = attend(
        queries, cache_keys, cache_values, block_ids, tree_keys, tree_values, ancestors
    )
    got = swap(send, "seq")
    one, three = shift(out_weight, 1), shift(out_weight, 3)
    rows = pl.pallas_call(
        combine_kernel,
        out_shape=jax.ShapeDtypeStruct((16, 32, 128), BF16),
        in_specs=[VMEM, VMEM],
        out_specs=VMEM,
        compiler_params=PARAMS,
    )(got, tree)
    gathered = swap(rows, ("seq", "head"), Z_GROUPS)
    low, high = pl.pallas_call(
        onward_kernel,
        out_shape=(jax.ShapeDtypeStruct((128, 512), BF16),) * 2,
        in_specs=[VMEM] * 2,
        out_specs=(VMEM, VMEM),
        cost_estimate=pl.CostEstimate(flops=10**10, bytes_accessed=0, transcendentals=0),
        compiler_params=PARAMS,
    )(one, three)
    low, high = shift(low, 1), shift(high, 3)
    parts = pl.pallas_call(
        project_kernel,
        out_shape=jax.ShapeDtypeStruct((8, 8, 512), BF16),
        in_specs=[VMEM] * 6,
        out_specs=VMEM,
        scratch_shapes=[pltpu.VMEM((8, 8, 512), F32)],
        compiler_params=PARAMS,
    )(gathered, out_weight, one, three, low, high)
    parts = swap(parts, "seq", XC_GROUPS)
    return pl.pallas_call(
        add_kernel,
        out_shape=(jax.ShapeDtypeStruct((1, 4, 512), BF16), jax.ShapeDtypeStruct((1, 4, 512), BF16)),
        in_specs=[VMEM],
        out_specs=(VMEM, VMEM),
        compiler_params=PARAMS,
    )(parts)


def solution(mesh):
    in_specs = (
        P(None, "head", None, None, None),
        P(None, "head", None, None),
        P(None, "head", None, None),
        P("head", "seq", None),
        P("head", "seq", None),
        P("head", None),
        P(),
        P("seq", "head"),
    )
    out_specs = (P("seq", None, "head"), P("seq", None, "head"))
    return jax.shard_map(local, mesh=mesh, in_specs=in_specs, out_specs=out_specs, check_vma=False)
```
